32 devices in a mesh: wide: 8 (over y, x, core), narrow: 4 (over z).
Axes of the slice: x: 2, y: 2, z: 4, core: 2. Of those that a mesh axis runs over, the one named last changes fastest.
Arguments:
- tokens: bfloat16 [8192, 1024], P(('wide', 'narrow')), may hold values from -6 to 6
- cotangent: bfloat16 [8192, 1024], P(('wide', 'narrow')), may hold values from -6 to 6
- lengths: int32 [8], P('wide'), may hold values from 128 to 1024, as said below
- routes: int32 [8192, 1], P('wide'), may hold values from 0 to 3
- norm_params: bfloat16 [4, 1024], replicated, may hold values from -1 to 2, as said below
- qkv_weight: bfloat16 [3, 1024, 1024], P(None, None, 'narrow'), may hold values from -0.1875 to 0.1875
- out_weight: bfloat16 [1024, 1024], P('narrow'), may hold values from -1.5 to 1.5
- up_weight: bfloat16 [1024, 4096], P(None, 'narrow'), may hold values from -0.1875 to 0.1875
- down_weight: bfloat16 [4096, 1024], P('narrow'), may hold values from -0.09375 to 0.09375
- router_weight: bfloat16 [1024, 4], replicated, may hold values from -0.125 to 0.125
- mix_weight: bfloat16 [1024, 2], replicated, may hold values from -0.125 to 0.125
- norm_master: float32 [4, 1024], P(None, 'wide'), may hold values from -1 to 2, as said below
- norm_moment: float32 [4, 1024], P(None, 'wide'), may hold values from -256 to 256
- norm_average: float32 [4, 1024], P(None, 'wide'), may hold values from -1 to 2, as said below
- qkv_master: float32 [3, 1024, 1024], P(None, 'wide', 'narrow'), may hold values from -0.1875 to 0.1875
- qkv_moment: float32 [3, 1024, 1024], P(None, 'wide', 'narrow'), may hold values from -192 to 192
- qkv_average: float32 [3, 1024, 1024], P(None, 'wide', 'narrow'), may hold values from -0.1875 to 0.1875
- out_master: float32 [1024, 1024], P('narrow', 'wide'), may hold values from -1.5 to 1.5
- out_moment: float32 [1024, 1024], P('narrow', 'wide'), may hold values from -24 to 24
- out_average: float32 [1024, 1024], P('narrow', 'wide'), may hold values from -1.5 to 1.5
- up_master: float32 [1024, 4096], P('wide', 'narrow'), may hold values from -0.1875 to 0.1875
- up_moment: float32 [1024, 4096], P('wide', 'narrow'), may hold values from -4 to 4
- up_average: float32 [1024, 4096], P('wide', 'narrow'), may hold values from -0.1875 to 0.1875
- down_master: float32 [4096, 1024], P('narrow', 'wide'), may hold values from -0.09375 to 0.09375
- down_moment: float32 [4096, 1024], P('narrow', 'wide'), may hold values from -12 to 12
- down_average: float32 [4096, 1024], P('narrow', 'wide'), may hold values from -0.09375 to 0.09375
- router_master: float32 [1024, 4], P('wide'), may hold values from -0.125 to 0.125
- router_moment: float32 [1024, 4], P('wide'), may hold values from -2048 to 2048
- router_average: float32 [1024, 4], P('wide'), may hold values from -0.125 to 0.125
- mix_master: float32 [1024, 2], P('wide'), may hold values from -0.125 to 0.125
- mix_moment: float32 [1024, 2], P('wide'), may hold values from -128 to 128
- mix_average: float32 [1024, 2], P('wide'), may hold values from -0.125 to 0.125
- expert_up_master: float32 [8, 1024, 2048], P('wide', None, 'narrow'), may hold values from -0.1875 to 0.1875
- expert_up_moment: float32 [8, 1024, 2048], P('wide', None, 'narrow'), may hold values from -14 to 14
- expert_up_average: float32 [8, 1024, 2048], P('wide', None, 'narrow'), may hold values from -0.1875 to 0.1875
- expert_down_master: float32 [8, 2048, 1024], P('wide', 'narrow'), may hold values from -1.5 to 1.5
- expert_down_moment: float32 [8, 2048, 1024], P('wide', 'narrow'), may hold values from -4 to 4
- expert_down_average: float32 [8, 2048, 1024], P('wide', 'narrow'), may hold values from -1.5 to 1.5
Outputs:
- block_output: bfloat16 [8192, 1024], P(('wide', 'narrow'))
- input_grad: float32 [8192, 1024], P(('wide', 'narrow'))
- expert_counts: int32 [4], replicated
- norm_grad: float32 [4, 1024], P(None, 'wide')
- norm_new: float32 [4, 1024], P(None, 'wide')
- norm_moment_new: float32 [4, 1024], P(None, 'wide')
- norm_average_new: float32 [4, 1024], P(None, 'wide')
- qkv_grad: float32 [3, 1024, 1024], P(None, 'wide', 'narrow')
- qkv_new: float32 [3, 1024, 1024], P(None, 'wide', 'narrow')
- qkv_moment_new: float32 [3, 1024, 1024], P(None, 'wide', 'narrow')
- qkv_average_new: float32 [3, 1024, 1024], P(None, 'wide', 'narrow')
- out_grad: float32 [1024, 1024], P('narrow', 'wide')
- out_new: float32 [1024, 1024], P('narrow', 'wide')
- out_moment_new: float32 [1024, 1024], P('narrow', 'wide')
- out_average_new: float32 [1024, 1024], P('narrow', 'wide')
- up_grad: float32 [1024, 4096], P('wide', 'narrow')
- up_new: float32 [1024, 4096], P('wide', 'narrow')
- up_moment_new: float32 [1024, 4096], P('wide', 'narrow')
- up_average_new: float32 [1024, 4096], P('wide', 'narrow')
- down_grad: float32 [4096, 1024], P('narrow', 'wide')
- down_new: float32 [4096, 1024], P('narrow', 'wide')
- down_moment_new: float32 [4096, 1024], P('narrow', 'wide')
- down_average_new: float32 [4096, 1024], P('narrow', 'wide')
- router_grad: float32 [1024, 4], P('wide')
- router_new: float32 [1024, 4], P('wide')
- router_moment_new: float32 [1024, 4], P('wide')
- router_average_new: float32 [1024, 4], P('wide')
- mix_grad: float32 [1024, 2], P('wide')
- mix_new: float32 [1024, 2], P('wide')
- mix_moment_new: float32 [1024, 2], P('wide')
- mix_average_new: float32 [1024, 2], P('wide')
- expert_up_grad: float32 [8, 1024, 2048], P('wide', None, 'narrow')
- expert_up_new: float32 [8, 1024, 2048], P('wide', None, 'narrow')
- expert_up_moment_new: float32 [8, 1024, 2048], P('wide', None, 'narrow')
- expert_up_average_new: float32 [8, 1024, 2048], P('wide', None, 'narrow')
- expert_down_grad: float32 [8, 2048, 1024], P('wide', 'narrow')
- expert_down_new: float32 [8, 2048, 1024], P('wide', 'narrow')
- expert_down_moment_new: float32 [8, 2048, 1024], P('wide', 'narrow')
- expert_down_average_new: float32 [8, 2048, 1024], P('wide', 'narrow')
The draws below stay inside these ranges and needn't reach their ends.
Inputs may be any that keep to these rules, and one draw needn't show every extreme that they name: `lengths`: live tokens of each sequence; in every draw some sequence is full. `norm_params`: gains near one in rows 0 and 2, shifts in rows 1 and 3. `norm_master`: gains near one in rows 0 and 2, shifts in rows 1 and 3. `norm_average`: gains near one in rows 0 and 2, shifts in rows 1 and 3.
All inputs are finite; a program needn't handle non-finite values.
Results may differ from the reference program's by a relative error of at most 0.03.
Values may be sent and summed in bfloat16 or wider, within the bound.
No kernel may reach another device: no remote copies, remote signals or barrier semaphores. Data moves between devices by JAX's collectives and lax.ppermute only.
A program may use at most 192 MiB of HBM per device.

```python
import math
import jax
import jax.numpy as jnp
from jax import lax

D = 1024
HEADS = 16
HEAD_DIM = 64
FF = 4096
SEQ = 1024
NSEQ = 8
TOKENS = 8192
EXPERTS = 4
CAP = 256
N_NARROW = 4


def draw_lengths(key, part):
    drawn_len = jax.random.randint(key, (NSEQ,), SEQ // 8, SEQ + 1, dtype=jnp.int32)
    full_at = jax.random.randint(jax.random.fold_in(key, 7), (), 0, NSEQ, dtype=jnp.int32)
    return jnp.where(jnp.arange(NSEQ, dtype=jnp.int32) == full_at, SEQ, drawn_len).astype(jnp.int32)


def norm_table(key):
    gain_rows = 1.0 + jax.random.uniform(jax.random.fold_in(key, 1), (2, D), jnp.float32, -0.3, 0.3)
    shifts = 0.2 * jax.random.truncated_normal(jax.random.fold_in(key, 2), -4.0, 4.0, (2, D), jnp.float32)
    return jnp.stack([gain_rows[0], shifts[0], gain_rows[1], shifts[1]], 0)


def draw_norm_params(key, part):
    return norm_table(jax.random.fold_in(key, 11)).astype(jnp.bfloat16)


def draw_norm_master(key, part):
    return norm_table(jax.random.fold_in(key, 12))


def draw_norm_average(key, part):
    return norm_table(jax.random.fold_in(key, 13))


def shard_levels(rng, shape, split, low, top_value):
    factor_of = 1.0
    for axis_at, parts in split:
        heights = jax.random.uniform(jax.random.fold_in(jax.random.fold_in(rng, 6), axis_at), (parts,), jnp.float32, low / len(split), top_value / len(split))
        factor_of = factor_of * jnp.repeat(jnp.exp(heights), shape[axis_at] // parts).reshape((-1,) + (1,) * (len(shape) - 1 - axis_at))
    return factor_of


def choose_distinct(key, rows, number_of, top, lift):
    ranking = jax.random.permutation(jax.random.fold_in(key, 1), number_of)
    favour = ranking
    for power in range(3):
        favour = favour * favour // number_of
    favour = favour * lift // number_of
    tickets = jax.random.randint(jax.random.fold_in(key, 2), (rows, number_of), 0, 4096) + favour
    sure = jax.random.permutation(jax.random.fold_in(key, 3), rows)[jnp.arange(number_of) % rows]
    tickets = jnp.where(jnp.arange(rows)[:, None] == sure[None, :], 1 << 14, tickets)
    merit = tickets * number_of + jnp.arange(number_of)
    return lax.top_k(merit.astype(jnp.int32), top)[1].astype(jnp.int32)


def bell_draw(own_key, extent, deviation, limit, cuts=(), held_as=jnp.bfloat16):
    entries = deviation * jax.random.normal(own_key, extent, jnp.float32)
    if cuts:
        entries = entries * shard_levels(own_key, extent, cuts, -0.22, 0.18)
    return jnp.clip(entries, -limit, limit).astype(held_as)


def setup_inputs(seed: int = 0) -> dict:
    key_list = jax.random.split(jax.random.key(seed), 39)
    tokens = bell_draw(key_list[0], (TOKENS, D), 1.0, 6.0, ((0, 32),))
    cotangent = bell_draw(key_list[1], (TOKENS, D), 1.0, 6.0, ((0, 32),))
    lengths = draw_lengths(jax.random.fold_in(key_list[38], 71), 0)
    routes = choose_distinct(key_list[3], TOKENS, EXPERTS, 1, 2048)
    norm_params = draw_norm_params(jax.random.fold_in(key_list[38], 71), 0)
    qkv_weight = bell_draw(key_list[5], (3, D, D), D ** -0.5, 0.1875, ((2, 4),))
    out_weight = bell_draw(key_list[6], (D, D), (D // 64) ** -0.5, 1.5, ((0, 4),))
    up_weight = bell_draw(key_list[7], (D, FF), D ** -0.5, 0.1875, ((1, 4),))
    down_weight = bell_draw(key_list[8], (FF, D), FF ** -0.5, 0.09375, ((0, 4),))
    router_weight = bell_draw(key_list[9], (D, EXPERTS), (2 * D) ** -0.5, 0.125)
    mix_weight = bell_draw(key_list[10], (D, 2), (2 * D) ** -0.5, 0.125)
    norm_master = draw_norm_master(jax.random.fold_in(key_list[38], 71), 0)
    norm_moment = bell_draw(key_list[12], (4, D), (TOKENS ** 0.5 / 2.25), 256.0, ((1, 8),), jnp.float32)
    norm_average = draw_norm_average(jax.random.fold_in(key_list[38], 71), 0)
    qkv_master = bell_draw(key_list[14], (3, D, D), D ** -0.5, 0.1875, ((1, 8), (2, 4)), jnp.float32)
    qkv_moment = bell_draw(key_list[15], (3, D, D), (TOKENS ** 0.5 / 3), 192.0, ((1, 8), (2, 4)), jnp.float32)
    qkv_average = bell_draw(key_list[16], (3, D, D), D ** -0.5, 0.1875, ((1, 8), (2, 4)), jnp.float32)
    out_master = bell_draw(key_list[17], (D, D), (D // 64) ** -0.5, 1.5, ((0, 4), (1, 8)), jnp.float32)
    out_moment = bell_draw(key_list[18], (D, D), (TOKENS ** 0.5 / 22.5), 24.0, ((0, 4), (1, 8)), jnp.float32)
    out_average = bell_draw(key_list[19], (D, D), (D // 64) ** -0.5, 1.5, ((0, 4), (1, 8)), jnp.float32)
    up_master = bell_draw(key_list[20], (D, FF), D ** -0.5, 0.1875, ((0, 8), (1, 4)), jnp.float32)
    up_moment = bell_draw(key_list[21], (D, FF), (TOKENS ** 0.5 / 60), 4.0, ((0, 8), (1, 4)), jnp.float32)
    up_average = bell_draw(key_list[22], (D, FF), D ** -0.5, 0.1875, ((0, 8), (1, 4)), jnp.float32)
    down_master = bell_draw(key_list[23], (FF, D), FF ** -0.5, 0.09375, ((0, 4), (1, 8)), jnp.float32)
    down_moment = bell_draw(key_list[24], (FF, D), (TOKENS ** 0.5 / 45), 12.0, ((0, 4), (1, 8)), jnp.float32)
    down_average = bell_draw(key_list[25], (FF, D), FF ** -0.5, 0.09375, ((0, 4), (1, 8)), jnp.float32)
    router_master = bell_draw(key_list[26], (D, EXPERTS), (2 * D) ** -0.5, 0.125, ((0, 8),), jnp.float32)
    router_moment = bell_draw(key_list[27], (D, EXPERTS), (TOKENS ** 0.5 * D ** 0.5 / (2 * EXPERTS)), 2048.0, ((0, 8),), jnp.float32)
    router_average = bell_draw(key_list[28], (D, EXPERTS), (2 * D) ** -0.5, 0.125, ((0, 8),), jnp.float32)
    mix_master = bell_draw(key_list[29], (D, 2), (2 * D) ** -0.5, 0.125, ((0, 8),), jnp.float32)
    mix_moment = bell_draw(key_list[30], (D, 2), (TOKENS ** 0.5 / 4), 128.0, ((0, 8),), jnp.float32)
    mix_average = bell_draw(key_list[31], (D, 2), (2 * D) ** -0.5, 0.125, ((0, 8),), jnp.float32)
    expert_up_master = bell_draw(key_list[32], (2 * EXPERTS, D, FF // 2), D ** -0.5, 0.1875, ((0, 8), (2, 4)), jnp.float32)
    expert_up_moment = bell_draw(key_list[33], (2 * EXPERTS, D, FF // 2), ((TOKENS // EXPERTS) ** 0.5 / (5 * EXPERTS)), 14.0, ((0, 8), (2, 4)), jnp.float32)
    expert_up_average = bell_draw(key_list[34], (2 * EXPERTS, D, FF // 2), D ** -0.5, 0.1875, ((0, 8), (2, 4)), jnp.float32)
    expert_down_master = bell_draw(key_list[35], (2 * EXPERTS, FF // 2, D), (max(FF // 256, 1)) ** -0.5, 1.5, ((0, 8), (1, 4)), jnp.float32)
    expert_down_moment = bell_draw(key_list[36], (2 * EXPERTS, FF // 2, D), ((TOKENS // EXPERTS) ** 0.5 / (20 * EXPERTS)), 4.0, ((0, 8), (1, 4)), jnp.float32)
    expert_down_average = bell_draw(key_list[37], (2 * EXPERTS, FF // 2, D), (max(FF // 256, 1)) ** -0.5, 1.5, ((0, 8), (1, 4)), jnp.float32)
    return {"tokens": tokens, "cotangent": cotangent, "lengths": lengths, "routes": routes, "norm_params": norm_params, "qkv_weight": qkv_weight, "out_weight": out_weight, "up_weight": up_weight, "down_weight": down_weight, "router_weight": router_weight, "mix_weight": mix_weight, "norm_master": norm_master, "norm_moment": norm_moment, "norm_average": norm_average, "qkv_master": qkv_master, "qkv_moment": qkv_moment, "qkv_average": qkv_average, "out_master": out_master, "out_moment": out_moment, "out_average": out_average, "up_master": up_master, "up_moment": up_moment, "up_average": up_average, "down_master": down_master, "down_moment": down_moment, "down_average": down_average, "router_master": router_master, "router_moment": router_moment, "router_average": router_average, "mix_master": mix_master, "mix_moment": mix_moment, "mix_average": mix_average, "expert_up_master": expert_up_master, "expert_up_moment": expert_up_moment, "expert_up_average": expert_up_average, "expert_down_master": expert_down_master, "expert_down_moment": expert_down_moment, "expert_down_average": expert_down_average}


precise = lax.Precision.HIGHEST
eps_norm = 1e-05
momentum_decay = 0.9
average_decay = 0.75
rate_base = 0.05
expert_down_boost = 12.0
neg_large = -1e+30

@jax.custom_vjp
def low(v):
    return lax.optimization_barrier(v.astype(jnp.bfloat16)).astype(jnp.float32)

@jax.custom_vjp
def low_back(v):
    return v

def low_keep(v):
    return (low(v), None)

def low_pass(kept, grad):
    return (grad,)

def back_keep(v):
    return (v, None)

def back_low(kept, grad):
    return (low(grad),)
low.defvjp(low_keep, low_pass)
low_back.defvjp(back_keep, back_low)

def layer_norm(values, gain, shift):
    mean_val = lax.optimization_barrier(jnp.mean(values, -1, keepdims=True))
    centered = values - mean_val
    variance = lax.optimization_barrier(jnp.mean(centered * centered, -1, keepdims=True))
    return centered * lax.rsqrt(variance + eps_norm) * gain + shift

def routing(route, length):
    positions = jnp.arange(SEQ, dtype=jnp.int32)
    live_rows = positions < length
    route_hot = ((route[:, None] == jnp.arange(EXPERTS, dtype=jnp.int32)[None, :]) & live_rows[:, None]).astype(jnp.int32)
    earlier = jnp.cumsum(route_hot, 0) - route_hot
    slot_pos = lax.optimization_barrier(jnp.sum(earlier * route_hot, -1))
    kept_rows = live_rows & (slot_pos < CAP)
    slot_ids = jnp.where(kept_rows, route * CAP + slot_pos, EXPERTS * CAP).astype(jnp.int32)
    token_of_slot = jnp.zeros((EXPERTS * CAP,), jnp.int32).at[slot_ids].set(positions, mode='drop')
    slot_live = jnp.zeros((EXPERTS * CAP,), jnp.float32).at[slot_ids].set(1.0, mode='drop')
    gather_ids = jnp.where(kept_rows, slot_ids, 0).astype(jnp.int32)
    return (kept_rows.astype(jnp.float32), gather_ids, token_of_slot, slot_live)

def head_attend(query, keys_in, values_in, length):
    positions = jnp.arange(SEQ, dtype=jnp.int32)
    allowed = (positions[None, :] <= positions[:, None]) & (positions[None, :] < length)
    scores = low_back(jnp.dot(query, keys_in.T, precision=precise) * HEAD_DIM ** (-0.5))
    scores = jnp.where(allowed, scores, neg_large)
    soft_max = jax.nn.softmax(scores, -1)
    return jnp.dot(low(soft_max), values_in, precision=precise)

def one_sequence(inputs, length, route, params):
    norms, qkv, proj, up_w, down_w, router_w, mix_w, expert_up, expert_down = params
    kept_rows, gather_ids, token_of_slot, slot_live = routing(route, length)
    act_one = low(layer_norm(inputs, norms[0], norms[1]))
    head_local = HEADS // N_NARROW
    head_cols = head_local * HEAD_DIM
    attend_head = jax.checkpoint(head_attend)
    attn_total = jnp.zeros_like(inputs)
    for narrow_pos in range(N_NARROW):
        col_range = slice(narrow_pos * head_cols, (narrow_pos + 1) * head_cols)
        act_copy = low_back(act_one)
        triple = [low_back(low(jnp.dot(act_copy, qkv[member][:, col_range], precision=precise))) for member in range(3)]
        split_heads = tuple((matrix.reshape(SEQ, head_local, HEAD_DIM).transpose(1, 0, 2) for matrix in triple))
        head_out = lax.map(lambda bundle: attend_head(bundle[0], bundle[1], bundle[2], length), split_heads)
        joined = low_back(low(head_out.transpose(1, 0, 2).reshape(SEQ, head_cols)))
        attn_total = attn_total + low(jnp.dot(joined, proj[col_range], precision=precise))
    attn_total = low_back(attn_total)
    hidden_skip_state = inputs + attn_total
    act_two = low(layer_norm(hidden_skip_state, norms[2], norms[3]))
    router_probs = jax.nn.softmax(jnp.dot(act_two, router_w, precision=precise), -1)
    route_float = (route[:, None] == jnp.arange(EXPERTS, dtype=jnp.int32)[None, :]).astype(act_two.dtype)
    gate_value = lax.optimization_barrier(jnp.sum(router_probs * route_float, -1))
    mix_coef = jax.nn.softmax(jnp.dot(act_two, mix_w, precision=precise), -1)
    dense_cols = FF // N_NARROW
    expert_cols = FF // (2 * N_NARROW)
    up_split = expert_up.reshape(EXPERTS, 2, D, FF // 2)
    down_split = expert_down.reshape(EXPERTS, 2, FF // 2, D)
    dense_sum = jnp.zeros_like(inputs)
    expert_sum = jnp.zeros((EXPERTS, CAP, D), inputs.dtype)
    slot_rows = (act_two[token_of_slot] * slot_live[:, None]).reshape(EXPERTS, CAP, D)
    for narrow_pos in range(N_NARROW):
        dense_range = slice(narrow_pos * dense_cols, (narrow_pos + 1) * dense_cols)
        dense_pre = low_back(jnp.dot(act_two, up_w[:, dense_range], precision=precise))
        dense_hid = low(jax.nn.gelu(dense_pre, approximate=True))
        dense_sum = dense_sum + jnp.dot(dense_hid, down_w[dense_range], precision=precise)
        unit_range = slice(narrow_pos * expert_cols, (narrow_pos + 1) * expert_cols)
        for half_pos in range(2):
            expert_pre = low_back(jnp.einsum('ecd,edh->ech', slot_rows, up_split[:, half_pos, :, unit_range], precision=precise))
            expert_hid = low(jax.nn.gelu(expert_pre, approximate=True))
            expert_sum = expert_sum + jnp.einsum('ech,ehd->ecd', expert_hid, down_split[:, half_pos, unit_range, :], precision=precise)
    dense_out = low_back(dense_sum)
    expert_out = low_back(expert_sum).reshape(EXPERTS * CAP, D)
    token_moe = expert_out[gather_ids] * kept_rows[:, None]
    mix_out = mix_coef[:, 0:1] * dense_out + (mix_coef[:, 1] * gate_value)[:, None] * token_moe
    return hidden_skip_state + mix_out

def apply_update(gradient, master, moment, average, step_rate):
    new_moment = momentum_decay * moment + gradient
    new_master = master - step_rate * (gradient + momentum_decay * new_moment)
    new_average = average_decay * average + (1.0 - average_decay) * new_master
    return (gradient, new_master, new_moment, new_average)

def reference(tokens, cotangent, lengths, routes, norm_params, qkv_weight, out_weight, up_weight, down_weight, router_weight, mix_weight, norm_master, norm_moment, norm_average, qkv_master, qkv_moment, qkv_average, out_master, out_moment, out_average, up_master, up_moment, up_average, down_master, down_moment, down_average, router_master, router_moment, router_average, mix_master, mix_moment, mix_average, expert_up_master, expert_up_moment, expert_up_average, expert_down_master, expert_down_moment, expert_down_average):
    working = (norm_params, qkv_weight, out_weight, up_weight, down_weight, router_weight, mix_weight)
    params_in = tuple((weight.astype(jnp.float32) for weight in working)) + (expert_up_master, expert_down_master)
    route_rows = routes.reshape(NSEQ, SEQ)

    def forward(inputs, params):
        rounded = tuple(params[:7]) + (low(params[7]), low(params[8]))

        def scan_step(scan_carry, scan_item):
            return (scan_carry, jax.checkpoint(one_sequence)(scan_item[0], scan_item[1], scan_item[2], rounded))
        _, outputs = lax.scan(scan_step, jnp.zeros((), inputs.dtype), (inputs.reshape(NSEQ, SEQ, D), lengths, route_rows))
        return outputs.reshape(TOKENS, D)
    block_out, pull_back = jax.vjp(forward, tokens.astype(jnp.float32), params_in)
    input_grad, param_grads = pull_back(cotangent.astype(jnp.float32))
    live_mask = jnp.arange(SEQ, dtype=jnp.int32)[None, :] < lengths[:, None]
    route_hot = (route_rows[:, :, None] == jnp.arange(EXPERTS, dtype=jnp.int32)[None, None, :]) & live_mask[:, :, None]
    expert_counts = lax.optimization_barrier(jnp.sum(route_hot.astype(jnp.int32), (0, 1))).astype(jnp.int32)
    step_rate = rate_base / math.sqrt(TOKENS)
    expert_rate = step_rate * (EXPERTS / 4.0) ** 1.5
    rate_list = (step_rate,) * 7 + (expert_rate, expert_down_boost * expert_rate)
    states = ((norm_master, norm_moment, norm_average), (qkv_master, qkv_moment, qkv_average), (out_master, out_moment, out_average), (up_master, up_moment, up_average), (down_master, down_moment, down_average), (router_master, router_moment, router_average), (mix_master, mix_moment, mix_average), (expert_up_master, expert_up_moment, expert_up_average), (expert_down_master, expert_down_moment, expert_down_average))
    results = [block_out.astype(jnp.bfloat16), input_grad, expert_counts]
    for gradient, state, rate_now in zip(param_grads, states, rate_list):
        results.extend(apply_update(gradient, state[0], state[1], state[2], rate_now))
    return tuple(results)
```

```python
import functools
import math

import jax
import jax.numpy as jnp
from jax import lax
from jax.experimental import pallas as pl
from jax.experimental.pallas import tpu as pltpu
from jax.sharding import PartitionSpec as P

HEAD_DIM = 64
F32 = jnp.float32
BF16 = jnp.bfloat16

precise = lax.Precision.HIGHEST
eps_norm = 1e-05
momentum_decay = 0.9
average_decay = 0.75
rate_base = 0.05
expert_down_boost = 12.0
neg_large = -1e30
lane_pad = 128


def dot_nn(a, b):
    return jnp.dot(a, b, preferred_element_type=F32)


def dot_nt(a, b):
    return lax.dot_general(a, b, (((1,), (1,)), ((), ())), preferred_element_type=F32)


def dot_tn(a, b):
    return lax.dot_general(a, b, (((0,), (0,)), ((), ())), preferred_element_type=F32)


def normalize(values):
    mean_val = jnp.mean(values, -1, keepdims=True)
    centered = values - mean_val
    inverse = lax.rsqrt(jnp.mean(centered * centered, -1, keepdims=True) + eps_norm)
    return (centered * inverse, inverse)


def layer_norm_reverse(upstream, normed, inverse, gain):
    scaled = upstream * gain
    return inverse * (
        scaled
        - jnp.mean(scaled, -1, keepdims=True)
        - normed * jnp.mean(scaled * normed, -1, keepdims=True)
    )


def gelu_pair(pre):
    root = math.sqrt(2.0 / math.pi)
    square = pre * pre
    tanh_val = jnp.tanh(root * pre * (1.0 + 0.044715 * square))
    half = 0.5 * (1.0 + tanh_val)
    slope = half + 0.5 * pre * (1.0 - tanh_val * tanh_val) * root * (1.0 + 0.134145 * square)
    return (pre * half, slope)


def attend_masks(length, keys, chunk):
    key_at = lax.broadcasted_iota(jnp.int32, (keys, 1), 0)
    bias = jnp.where(key_at < length, 0.0, neg_large).astype(F32)
    below = lax.broadcasted_iota(jnp.int32, (chunk, chunk), 0)
    across = lax.broadcasted_iota(jnp.int32, (chunk, chunk), 1)
    return (bias, below <= across)


def masked_scores(key, query, bias, causal, chunk):
    scores = dot_nt(key, query) + bias
    edge = jnp.where(causal, scores[-chunk:], neg_large)
    if scores.shape[0] == chunk:
        return edge
    return jnp.concatenate([scores[:-chunk], edge], 0)


def attend_forward_kernel(length_ref, qkv_ref, heads_ref, sums_ref, *, chunk):
    rows = qkv_ref.shape[0]
    width = qkv_ref.shape[1] // 3
    scale = jnp.asarray(HEAD_DIM**-0.5, BF16)
    for block in range(rows // chunk):
        at, keys = block * chunk, (block + 1) * chunk
        bias, causal = attend_masks(length_ref[0], keys, chunk)
        outs = []
        for head in range(width // HEAD_DIM):
            col = head * HEAD_DIM
            query = qkv_ref[at:keys, col : col + HEAD_DIM] * scale
            key = qkv_ref[0:keys, width + col : width + col + HEAD_DIM]
            value = qkv_ref[0:keys, 2 * width + col : 2 * width + col + HEAD_DIM]
            scores = masked_scores(key, query, bias, causal, chunk)
            top = jnp.max(scores, 0, keepdims=True)
            expo = jnp.exp(scores - top)
            total = jnp.sum(expo, 0, keepdims=True)
            soft = (expo * (1.0 / total)).astype(BF16)
            outs.append(dot_tn(value, soft))
            sums_ref[head : head + 1, at:keys] = top + jnp.log(total)
        heads_ref[at:keys, :] = jnp.concatenate(outs, 0).T.astype(BF16)


def attend_forward(qkv, length):
    rows, wide3 = qkv.shape
    width = wide3 // 3
    heads = width // HEAD_DIM
    return pl.pallas_call(
        functools.partial(attend_forward_kernel, chunk=min(256, rows)),
        out_shape=(
            jax.ShapeDtypeStruct((rows, width), BF16),
            jax.ShapeDtypeStruct((heads, rows), F32),
        ),
        in_specs=[
            pl.BlockSpec(memory_space=pltpu.SMEM),
            pl.BlockSpec(memory_space=pltpu.VMEM),
        ],
        out_specs=(
            pl.BlockSpec(memory_space=pltpu.VMEM),
            pl.BlockSpec(memory_space=pltpu.VMEM),
        ),
        compiler_params=pltpu.CompilerParams(vmem_limit_bytes=32 * 2**20),
        cost_estimate=pl.CostEstimate(
            flops=4 * rows * rows * width,
            bytes_accessed=rows * width * 8,
            transcendentals=rows * rows * heads,
        ),
        name="attend_forward",
    )(length, qkv)


def attend_backward_kernel(length_ref, qkv_ref, cot_ref, sums_ref, out_ref, dk_ref, dv_ref, *, chunk):
    rows = qkv_ref.shape[0]
    width = qkv_ref.shape[1] // 3
    scale = jnp.asarray(HEAD_DIM**-0.5, BF16)
    blocks = rows // chunk
    for block in range(blocks):
        at, keys = block * chunk, (block + 1) * chunk
        bias, causal = attend_masks(length_ref[0], keys, chunk)
        outs = []
        for head in range(width // HEAD_DIM):
            col = head * HEAD_DIM
            query = qkv_ref[at:keys, col : col + HEAD_DIM] * scale
            key = qkv_ref[0:keys, width + col : width + col + HEAD_DIM]
            value = qkv_ref[0:keys, 2 * width + col : 2 * width + col + HEAD_DIM]
            cot = cot_ref[at:keys, col : col + HEAD_DIM]
            scores = masked_scores(key, query, bias, causal, chunk)
            prob = jnp.exp(scores - sums_ref[head : head + 1, at:keys])
            dprob = dot_nt(value, cot)
            delta = jnp.sum(prob * dprob, 0, keepdims=True)
            dscore = (prob * (dprob - delta)).astype(BF16)
            dvalue = dot_nn(prob.astype(BF16), cot)
            dkey = dot_nn(dscore, query)
            outs.append(dot_tn(key * scale, dscore))
            here = slice(col, col + HEAD_DIM)
            if block > 0:
                dv_ref[0:at, here] += dvalue[:at]
                dk_ref[0:at, here] += dkey[:at]
            dv_ref[at:keys, here] = dvalue[at:]
            dk_ref[at:keys, here] = dkey[at:]
        out_ref[at:keys, 0:width] = jnp.concatenate(outs, 0).T.astype(BF16)
    out_ref[:, width : 2 * width] = dk_ref[...].astype(BF16)
    out_ref[:, 2 * width : 3 * width] = dv_ref[...].astype(BF16)


def attend_backward(qkv, cot, sums, length):
    rows, wide3 = qkv.shape
    width = wide3 // 3
    heads = width // HEAD_DIM
    vmem = pl.BlockSpec(memory_space=pltpu.VMEM)
    return pl.pallas_call(
        functools.partial(attend_backward_kernel, chunk=min(256, rows)),
        out_shape=jax.ShapeDtypeStruct((rows, wide3), BF16),
        in_specs=[pl.BlockSpec(memory_space=pltpu.SMEM), vmem, vmem, vmem],
        out_specs=vmem,
        scratch_shapes=[pltpu.VMEM((rows, width), F32), pltpu.VMEM((rows, width), F32)],
        compiler_params=pltpu.CompilerParams(vmem_limit_bytes=32 * 2**20),
        cost_estimate=pl.CostEstimate(
            flops=10 * rows * rows * width,
            bytes_accessed=rows * width * 14,
            transcendentals=rows * rows * heads,
        ),
        name="attend_backward",
    )(length, qkv, cot, sums)


def swap(values, axis, bit):
    count = lax.axis_size(axis)
    return lax.ppermute(values, axis, [(i, i ^ bit) for i in range(count)])


def bits_of(axis):
    count = lax.axis_size(axis)
    return [1 << b for b in range(count.bit_length() - 1)]


def gather_pieces(own, axis):
    pieces = {0: own}
    for bit in reversed(bits_of(axis)):
        for m in list(pieces):
            pieces[m | bit] = swap(pieces[m], axis, bit)
    return [pieces[m] for m in range(lax.axis_size(axis))]


def assemble(pieces, axis):
    me = lax.axis_index(axis)
    rows = pieces[0].shape[0]
    full = jnp.zeros((rows * len(pieces),) + pieces[0].shape[1:], pieces[0].dtype)
    for m, piece in enumerate(pieces):
        full = lax.dynamic_update_slice_in_dim(full, piece, (me ^ m) * rows, 0)
    return full


def reduce_pieces(blocks, axis):
    held = dict(enumerate(blocks))
    for bit in bits_of(axis):
        for m in sorted((m for m in held if m & bit), reverse=True):
            got = swap(held.pop(m).astype(BF16), axis, bit)
            held[m ^ bit] = held[m ^ bit].astype(F32) + got.astype(F32)
    return held[0]


def split_rows(values, axis):
    me = lax.axis_index(axis)
    count = lax.axis_size(axis)
    rows = values.shape[0] // count
    return [lax.dynamic_slice_in_dim(values, (me ^ m) * rows, rows, 0) for m in range(count)]


def exchange_pieces(pieces, axis):
    return [pieces[0]] + [swap(pieces[m], axis, m) for m in range(1, len(pieces))]


def apply_update(gradient, master, moment, average, step_rate):
    new_moment = momentum_decay * moment + gradient
    new_master = master - step_rate * (gradient + momentum_decay * new_moment)
    new_average = average_decay * average + (1.0 - average_decay) * new_master
    return (gradient, new_master, new_moment, new_average)


def token_slots(route_ids, length, expert_count, capacity):
    rows = route_ids.shape[0]
    at = jnp.arange(rows, dtype=jnp.int32)
    live = at < length
    hot = (route_ids[:, None] == jnp.arange(expert_count, dtype=jnp.int32)[None, :]) & live[:, None]
    hot_f = hot.astype(F32)
    before = (at[None, :] < at[:, None]).astype(BF16)
    earlier = dot_nn(before, hot.astype(BF16))
    pos = jnp.sum(earlier * hot_f, -1)
    totals = jnp.sum(hot_f, 0)
    kept = live & (pos < capacity)
    counts = jnp.minimum(totals, capacity)
    spare = capacity - counts
    order = jnp.arange(expert_count)
    spare_before = jnp.sum(jnp.where(order[None, :] < order[:, None], spare[None, :], 0.0), 1)
    rank = at.astype(F32) - jnp.sum(jnp.minimum(earlier, capacity), -1)
    inside = (rank[:, None] >= spare_before[None, :]) & (rank[:, None] < (spare_before + spare)[None, :])
    base = order.astype(F32) * capacity + counts - spare_before
    loose = jnp.sum(jnp.where(inside, base[None, :] + rank[:, None], 0.0), -1)
    slot = jnp.where(kept, route_ids * capacity + pos.astype(jnp.int32), loose.astype(jnp.int32))
    slot_live = (jnp.arange(capacity, dtype=F32)[None, :] < counts[:, None]).reshape(-1)
    return (slot.astype(jnp.int32), slot_live.astype(F32), totals)


def on_device(
    tokens,
    cotangent,
    lengths,
    routes,
    norm_params,
    qkv_weight,
    out_weight,
    up_weight,
    down_weight,
    router_weight,
    mix_weight,
    norm_master,
    norm_moment,
    norm_average,
    qkv_master,
    qkv_moment,
    qkv_average,
    out_master,
    out_moment,
    out_average,
    up_master,
    up_moment,
    up_average,
    down_master,
    down_moment,
    down_average,
    router_master,
    router_moment,
    router_average,
    mix_master,
    mix_moment,
    mix_average,
    expert_up_master,
    expert_up_moment,
    expert_up_average,
    expert_down_master,
    expert_down_moment,
    expert_down_average,
):
    narrow_count = lax.axis_size("narrow")
    wide_count = lax.axis_size("wide")
    narrow_index = lax.axis_index("narrow")
    wide_index = lax.axis_index("wide")
    local_rows, width = tokens.shape
    group_rows = local_rows * narrow_count
    expert_count = router_weight.shape[1]
    capacity = group_rows // expert_count
    head_width = qkv_weight.shape[2]
    own_at = narrow_index * local_rows
    norms = norm_params.astype(F32)

    up_local = expert_up_master[0].astype(BF16)
    down_local = expert_down_master[0].astype(BF16)
    units = up_local.shape[1]
    expert_pack = lax.all_gather(
        jnp.concatenate([up_local.T, down_local], 0), "wide", axis=0, tiled=False
    ).reshape(expert_count, 2, 2, units, width)
    expert_up = expert_pack[:, :, 0]
    expert_down = expert_pack[:, :, 1]

    tok_full = assemble(gather_pieces(tokens, "narrow"), "narrow")
    cot_full = assemble(gather_pieces(cotangent, "narrow"), "narrow")

    out_rows = out_weight.shape[0] // wide_count
    out_slice = lax.dynamic_slice_in_dim(out_weight, wide_index * out_rows, out_rows, 0)
    out_stack = jnp.stack(gather_pieces(out_slice, "narrow"), 0)
    out_all = lax.all_gather(out_stack, "wide", axis=1, tiled=True)

    slot, slot_live, totals = token_slots(routes[:, 0], lengths[0], expert_count, capacity)
    expert_counts = lax.psum(totals.astype(jnp.int32), "wide")
    into_slot = (
        jnp.arange(group_rows, dtype=jnp.int32)[:, None] == slot[None, :]
    ).astype(BF16)

    qkv_cat = jnp.concatenate([qkv_weight[c] for c in range(3)], 1)
    residual_input = tok_full.astype(F32)
    hat_one, inverse_one = normalize(residual_input)
    act_one = (hat_one * norms[0] + norms[1]).astype(BF16)
    qkv = dot_nn(act_one, qkv_cat).astype(BF16)
    heads, log_sums = attend_forward(qkv, lengths)
    head_pieces = gather_pieces(heads, "narrow")
    attn = sum(dot_nn(piece, out_all[m]) for m, piece in enumerate(head_pieces))
    resid = residual_input + attn
    hat_two, inverse_two = normalize(resid)
    act_two = (hat_two * norms[2] + norms[3]).astype(BF16)

    sorted_act = dot_nn(into_slot, act_two).astype(BF16)
    sorted_cot = dot_nn(into_slot, cot_full).astype(BF16)
    side_weight = jnp.concatenate([router_weight, mix_weight], 1)

    def coefficients(act):
        logits = dot_nn(act, side_weight)
        return (
            jax.nn.softmax(logits[:, :expert_count], -1),
            jax.nn.softmax(logits[:, expert_count:], -1),
        )

    probs, coef = coefficients(sorted_act)
    slot_expert = jnp.arange(group_rows, dtype=jnp.int32) // capacity
    expert_ids = jnp.arange(expert_count, dtype=jnp.int32)
    gate = jnp.sum(jnp.where(slot_expert[:, None] == expert_ids[None, :], probs, 0.0), -1)
    slot_scale = (slot_live * gate * coef[:, 1])[:, None]
    dense_scale = coef[:, 0:1]

    act_blocks = sorted_act.reshape(expert_count, capacity, width)
    cot_blocks = sorted_cot.reshape(expert_count, capacity, width)
    dense_pre = dot_nn(sorted_act, up_weight)
    dense_hid, dense_slope = gelu_pair(dense_pre)
    dense_back = dot_nt(sorted_cot, down_weight)
    dense_dot = jnp.sum(dense_hid * dense_back, -1)
    dense_dpre = (dense_slope * (dense_scale * dense_back)).astype(BF16)
    dense_hid = dense_hid.astype(BF16)

    expert_pre = jnp.einsum("ecd,epfd->ecpf", act_blocks, expert_up, preferred_element_type=F32)
    expert_hid, expert_slope = gelu_pair(expert_pre)
    expert_back = jnp.einsum("ecd,epfd->ecpf", cot_blocks, expert_down, preferred_element_type=F32)
    expert_dot = slot_live * jnp.sum(expert_hid * expert_back, (2, 3)).reshape(-1)
    scale4 = slot_scale.reshape(expert_count, capacity, 1, 1)
    expert_dpre = (expert_slope * (scale4 * expert_back)).astype(BF16)
    expert_hid = expert_hid.astype(BF16)

    sorted_dact = dot_nt(dense_dpre, up_weight) + jnp.einsum(
        "ecpf,epfd->ecd", expert_dpre, expert_up, preferred_element_type=F32
    ).reshape(group_rows, width)
    dact_part = dot_tn(into_slot, sorted_dact.astype(BF16))
    dact_own = reduce_pieces(split_rows(dact_part, "narrow"), "narrow")
    dots = jnp.stack(
        [
            jnp.sum(into_slot.astype(F32) * dense_dot[:, None], 0),
            jnp.sum(into_slot.astype(F32) * expert_dot[:, None], 0),
        ],
        0,
    )
    dot_parts = [
        lax.dynamic_slice_in_dim(dots, (narrow_index ^ m) * local_rows, local_rows, 1)
        for m in range(narrow_count)
    ]
    dots_own = sum(exchange_pieces(dot_parts, "narrow"))

    def own(values):
        return lax.dynamic_slice_in_dim(values, own_at, local_rows, 0)

    act_own = own(act_two)
    probs_own, coef_own = coefficients(act_own)
    route_own = own(routes[:, 0])
    hot_own = (route_own[:, None] == expert_ids[None, :]).astype(F32)
    gate_own = jnp.sum(probs_own * hot_own, -1)
    coef_grad = jnp.stack([dots_own[0], gate_own * dots_own[1]], -1)
    gate_grad = coef_own[:, 1] * dots_own[1]
    dmix = coef_own * (coef_grad - jnp.sum(coef_own * coef_grad, -1, keepdims=True))
    prob_grad = hot_own * gate_grad[:, None]
    dlogit = probs_own * (prob_grad - jnp.sum(probs_own * prob_grad, -1, keepdims=True))
    dside = jnp.concatenate([dlogit, dmix], 1)
    side_grad = jnp.dot(dside, side_weight.astype(F32).T, precision=precise)
    side_weight_grad = lax.dot_general(
        act_own.astype(F32), dside, (((0,), (0,)), ((), ())), precision=precise
    )

    dact_own = dact_own + side_grad
    hat_own = own(hat_two)
    dresid = cotangent.astype(F32) + layer_norm_reverse(
        dact_own, hat_own, own(inverse_two), norms[2]
    )
    resid_low = dresid.astype(BF16)
    dheads = exchange_pieces(
        [dot_nt(resid_low, out_all[m]).astype(BF16) for m in range(narrow_count)], "narrow"
    )
    attn_cot = assemble(dheads, "narrow")
    dqkv = attend_backward(qkv, attn_cot, log_sums, lengths)
    done_part = dot_nt(dqkv, qkv_cat)
    done_own = reduce_pieces(split_rows(done_part, "narrow"), "narrow")
    input_grad = dresid + layer_norm_reverse(done_own, own(hat_one), own(inverse_one), norms[0])

    dense_out = dot_nn(dense_hid, down_weight)
    expert_out = jnp.einsum(
        "ecpf,epfd->ecd", expert_hid, expert_down, preferred_element_type=F32
    ).reshape(group_rows, width)
    sorted_mlp = (dense_scale * dense_out + slot_scale * expert_out).astype(BF16)
    mlp_own = reduce_pieces(split_rows(dot_tn(into_slot, sorted_mlp), "narrow"), "narrow")
    block_out = (own(resid) + mlp_own).astype(BF16)

    dense_cot = (dense_scale * sorted_cot.astype(F32)).astype(BF16)
    up_down = jnp.concatenate(
        [
            dot_tn(sorted_act, dense_dpre).astype(BF16),
            dot_tn(dense_cot, dense_hid).astype(BF16),
        ],
        1,
    )
    up_down = lax.psum_scatter(up_down, "wide", scatter_dimension=0, tiled=True).astype(F32)
    hidden = up_weight.shape[1]
    up_gradient = up_down[:, :hidden]
    down_gradient = up_down[:, hidden:].T

    def padded(columns):
        return jnp.pad(columns, ((0, 0), (0, lane_pad - columns.shape[1]))).astype(BF16)

    small_two = padded(
        jnp.concatenate(
            [
                jnp.stack([jnp.sum(dact_own * hat_own, 0), jnp.sum(dact_own, 0)], 1),
                side_weight_grad,
            ],
            1,
        )
    )
    out_part = [dot_tn(resid_low, own(piece)).astype(BF16) for piece in head_pieces]
    second = lax.psum_scatter(
        jnp.concatenate(out_part + [small_two], 1), "wide", scatter_dimension=0, tiled=True
    )
    small_at = narrow_count * head_width
    second_parts = exchange_pieces(
        [
            jnp.concatenate(
                [second[:, m * head_width : (m + 1) * head_width], second[:, small_at:]], 1
            )
            for m in range(narrow_count)
        ],
        "narrow",
    )
    second_sum = sum(part.astype(F32) for part in second_parts)
    out_gradient = second_sum[:, :head_width].T
    small_second = second_sum[:, head_width:]

    small_one = padded(
        jnp.stack([jnp.sum(done_part * hat_one, 0), jnp.sum(done_part, 0)], 1)
    )
    third = lax.psum_scatter(
        jnp.concatenate([dot_tn(act_one, dqkv).astype(BF16), small_one], 1),
        "wide",
        scatter_dimension=0,
        tiled=True,
    )
    qkv_gradient = jnp.stack(
        [third[:, c * head_width : (c + 1) * head_width] for c in range(3)], 0
    ).astype(F32)
    small_first = sum(
        part.astype(F32)
        for part in exchange_pieces([third[:, 3 * head_width :]] * narrow_count, "narrow")
    )
    norm_gradient = jnp.concatenate([small_first[:, :2], small_second[:, :2]], 1).T
    router_gradient = small_second[:, 2 : 2 + expert_count]
    mix_gradient = small_second[:, 2 + expert_count : 4 + expert_count]

    scaled_cot = (slot_scale * sorted_cot.astype(F32)).astype(BF16)

    def to_owners(blocks):
        got = []
        for m in range(0, wide_count, 2):
            at = ((wide_index ^ m) // 2) * capacity
            block = lax.dynamic_slice_in_dim(blocks, at, capacity, 0)
            got.append(block if m == 0 else swap(block, "wide", m))
        mine = jnp.concatenate(got, 0)
        return jnp.concatenate([mine, swap(mine, "wide", 1)], 0)

    owner_act = to_owners(sorted_act)
    owner_cot = to_owners(scaled_cot)
    owner_hid, owner_slope = gelu_pair(dot_nn(owner_act, up_local))
    owner_dpre = (owner_slope * dot_nt(owner_cot, down_local)).astype(BF16)
    expert_down_gradient = dot_tn(owner_hid.astype(BF16), owner_cot)
    expert_up_gradient = dot_tn(owner_act, owner_dpre)

    step_rate = rate_base / math.sqrt(group_rows * wide_count)
    expert_rate = step_rate * (expert_count / 4.0) ** 1.5
    rate_list = (step_rate,) * 7 + (expert_rate, expert_down_boost * expert_rate)
    states = (
        (norm_master, norm_moment, norm_average),
        (qkv_master, qkv_moment, qkv_average),
        (out_master, out_moment, out_average),
        (up_master, up_moment, up_average),
        (down_master, down_moment, down_average),
        (router_master, router_moment, router_average),
        (mix_master, mix_moment, mix_average),
        (expert_up_master, expert_up_moment, expert_up_average),
        (expert_down_master, expert_down_moment, expert_down_average),
    )
    gradient_list = (
        norm_gradient,
        qkv_gradient,
        out_gradient,
        up_gradient,
        down_gradient,
        router_gradient,
        mix_gradient,
        expert_up_gradient[None],
        expert_down_gradient[None],
    )
    results = [block_out, input_grad, expert_counts]
    for gradient, state, rate_now in zip(gradient_list, states, rate_list):
        results.extend(apply_update(gradient, state[0], state[1], state[2], rate_now))
    return tuple(results)


def solution(mesh):
    in_specs = (
        P(("wide", "narrow"), None),
        P(("wide", "narrow"), None),
        P("wide"),
        P("wide", None),
        P(),
        P(None, None, "narrow"),
        P("narrow", None),
        P(None, "narrow"),
        P("narrow", None),
        P(),
        P(),
        P(None, "wide"),
        P(None, "wide"),
        P(None, "wide"),
        P(None, "wide", "narrow"),
        P(None, "wide", "narrow"),
        P(None, "wide", "narrow"),
        P("narrow", "wide"),
        P("narrow", "wide"),
        P("narrow", "wide"),
        P("wide", "narrow"),
        P("wide", "narrow"),
        P("wide", "narrow"),
        P("narrow", "wide"),
        P("narrow", "wide"),
        P("narrow", "wide"),
        P("wide", None),
        P("wide", None),
        P("wide", None),
        P("wide", None),
        P("wide", None),
        P("wide", None),
        P("wide", None, "narrow"),
        P("wide", None, "narrow"),
        P("wide", None, "narrow"),
        P("wide", "narrow", None),
        P("wide", "narrow", None),
        P("wide", "narrow", None),
    )
    out_specs = (
        P(("wide", "narrow"), None),
        P(("wide", "narrow"), None),
        P(),
        P(None, "wide"),
        P(None, "wide"),
        P(None, "wide"),
        P(None, "wide"),
        P(None, "wide", "narrow"),
        P(None, "wide", "narrow"),
        P(None, "wide", "narrow"),
        P(None, "wide", "narrow"),
        P("narrow", "wide"),
        P("narrow", "wide"),
        P("narrow", "wide"),
        P("narrow", "wide"),
        P("wide", "narrow"),
        P("wide", "narrow"),
        P("wide", "narrow"),
        P("wide", "narrow"),
        P("narrow", "wide"),
        P("narrow", "wide"),
        P("narrow", "wide"),
        P("narrow", "wide"),
        P("wide", None),
        P("wide", None),
        P("wide", None),
        P("wide", None),
        P("wide", None),
        P("wide", None),
        P("wide", None),
        P("wide", None),
        P("wide", None, "narrow"),
        P("wide", None, "narrow"),
        P("wide", None, "narrow"),
        P("wide", None, "narrow"),
        P("wide", "narrow", None),
        P("wide", "narrow", None),
        P("wide", "narrow", None),
        P("wide", "narrow", None),
    )
    return jax.shard_map(
        on_device, mesh=mesh, in_specs=in_specs, out_specs=out_specs, check_vma=False
    )
```

```python
import functools
import math

import jax
import jax.numpy as jnp
from jax import lax
from jax.experimental import pallas as pl
from jax.experimental.pallas import tpu as pltpu
from jax.sharding import PartitionSpec as P

HEAD_DIM = 64
F32 = jnp.float32
BF16 = jnp.bfloat16

precise = lax.Precision.HIGHEST
eps_norm = 1e-05
momentum_decay = 0.9
average_decay = 0.75
rate_base = 0.05
expert_down_boost = 12.0
neg_large = -1e30
lane_pad = 128


def dot_nn(a, b):
    return jnp.dot(a, b, preferred_element_type=F32)


def dot_nt(a, b):
    return lax.dot_general(a, b, (((1,), (1,)), ((), ())), preferred_element_type=F32)


def dot_tn(a, b):
    return lax.dot_general(a, b, (((0,), (0,)), ((), ())), preferred_element_type=F32)


def normalize(values):
    mean_val = jnp.mean(values, -1, keepdims=True)
    centered = values - mean_val
    inverse = lax.rsqrt(jnp.mean(centered * centered, -1, keepdims=True) + eps_norm)
    return (centered * inverse, inverse)


def layer_norm_reverse(upstream, normed, inverse, gain):
    scaled = upstream * gain
    return inverse * (
        scaled
        - jnp.mean(scaled, -1, keepdims=True)
        - normed * jnp.mean(scaled * normed, -1, keepdims=True)
    )


def gelu_pair(pre):
    root = math.sqrt(2.0 / math.pi)
    square = pre * pre
    half = 0.5 + 0.5 * jnp.tanh(pre * (root + (root * 0.044715) * square))
    hid = pre * half
    slope = half + hid * (1.0 - half) * (2.0 * root + (root * 0.26829) * square)
    return (hid, slope)


def attend_masks(length, keys, chunk):
    key_at = lax.broadcasted_iota(jnp.int32, (keys, 1), 0)
    bias = jnp.where(key_at < length, 0.0, neg_large).astype(F32)
    below = lax.broadcasted_iota(jnp.int32, (chunk, chunk), 0)
    across = lax.broadcasted_iota(jnp.int32, (chunk, chunk), 1)
    return (bias, below <= across)


def masked_scores(key, query, bias, causal, chunk):
    scores = dot_nt(key, query) + bias
    edge = jnp.where(causal, scores[-chunk:], neg_large)
    if scores.shape[0] == chunk:
        return edge
    return jnp.concatenate([scores[:-chunk], edge], 0)


VMEM = pl.BlockSpec(memory_space=pltpu.VMEM)
SMEM = pl.BlockSpec(memory_space=pltpu.SMEM)
MIB = 2**20
LIMITS = {"project": 12, "attend_forward": 16, "join": 20, "pack_expert": 12, "second_norm_reverse": 12, "attend_backward": 60, "qkv_grad": 60, "first_norm_reverse": 10, "owner_grad": 44, "hidden_update": 12, "out_update": 8, "qkv_update": 8}


def shape_of(shape, dtype=BF16):
    return jax.ShapeDtypeStruct(shape, dtype)


def cost(micros):
    return pl.CostEstimate(flops=int(micros * 1e5), bytes_accessed=1024, transcendentals=0)


def local_call(kernel, name, outs, in_specs, micros, scratch=()):
    return pl.pallas_call(
        kernel,
        out_shape=outs,
        in_specs=in_specs,
        out_specs=jax.tree.map(lambda _: VMEM, outs),
        scratch_shapes=list(scratch),
        compiler_params=pltpu.CompilerParams(vmem_limit_bytes=LIMITS[name] * MIB),
        cost_estimate=cost(micros),
        name=name,
    )


def project_kernel(tok_ref, norms_ref, weight_ref, act_ref, qkv_ref):
    hat, _ = normalize(tok_ref[...].astype(F32))
    act = (hat * norms_ref[0:1, :] + norms_ref[1:2, :]).astype(BF16)
    act_ref[...] = act
    width = weight_ref.shape[2]
    for c in range(3):
        qkv_ref[:, c * width : (c + 1) * width] = dot_nn(act, weight_ref[c]).astype(BF16)


def project(tok, norms, weight):
    rows, width = tok.shape
    columns = 3 * weight.shape[2]
    return local_call(
        project_kernel,
        "project",
        (shape_of((rows, width)), shape_of((rows, columns))),
        [VMEM] * 3,
        2,
    )(tok, norms, weight)


def place_rows(place_ref, pieces, full_ref):
    rows = pieces[0].shape[0]
    for m, piece in enumerate(pieces):
        at = pl.multiple_of(place_ref[m] * rows, rows)
        full_ref[pl.ds(at, rows), :] = piece[...]


def attend_forward_kernel(place_ref, length_ref, *refs, count, chunk):
    pieces, (heads_ref, sums_ref, qkv_ref) = refs[:count], refs[count:]
    place_rows(place_ref, pieces, qkv_ref)
    rows = qkv_ref.shape[0]
    width = qkv_ref.shape[1] // 3
    scale = jnp.asarray(HEAD_DIM**-0.5, BF16)
    for block in range(rows // chunk):
        at, keys = block * chunk, (block + 1) * chunk
        bias, causal = attend_masks(length_ref[0], keys, chunk)
        outs = []
        for head in range(width // HEAD_DIM):
            col = head * HEAD_DIM
            query = qkv_ref[at:keys, col : col + HEAD_DIM] * scale
            key = qkv_ref[0:keys, width + col : width + col + HEAD_DIM]
            value = qkv_ref[0:keys, 2 * width + col : 2 * width + col + HEAD_DIM]
            scores = masked_scores(key, query, bias, causal, chunk)
            top = jnp.max(scores, 0, keepdims=True)
            expo = jnp.exp(scores - top)
            total = jnp.sum(expo, 0, keepdims=True)
            soft = (expo * (1.0 / total)).astype(BF16)
            outs.append(dot_tn(value, soft))
            sums_ref[head : head + 1, at:keys] = top + jnp.log(total)
        heads_ref[at:keys, :] = jnp.concatenate(outs, 0).T.astype(BF16)


def attend_forward(place, length, pieces):
    count = len(pieces)
    rows = pieces[0].shape[0] * count
    width = pieces[0].shape[1] // 3
    heads = width // HEAD_DIM
    return local_call(
        functools.partial(attend_forward_kernel, count=count, chunk=min(256, rows)),
        "attend_forward",
        (shape_of((rows, width)), shape_of((heads, rows), F32), shape_of((rows, 3 * width))),
        [SMEM, SMEM] + [VMEM] * count,
        11,
    )(place, length, *pieces)


def join_kernel(place_ref, *refs, count):
    heads, toks = refs[:count], refs[count : 2 * count]
    out_ref, norms_ref, act_ref, resid_ref = refs[2 * count :]
    rows = toks[0].shape[0]
    for m in range(count):
        at = pl.multiple_of(place_ref[m] * rows, rows)
        total = toks[m][...].astype(F32)
        for j in range(count):
            total = total + dot_nn(heads[j][pl.ds(at, rows), :], out_ref[j])
        if m == 0:
            resid_ref[...] = total
        hat, _ = normalize(total)
        act = hat * norms_ref[2:3, :] + norms_ref[3:4, :]
        act_ref[m * rows : (m + 1) * rows, :] = act.astype(BF16)


def join(place, heads, toks, out_all, norms):
    count = len(heads)
    rows, width = toks[0].shape
    return local_call(
        functools.partial(join_kernel, count=count),
        "join",
        (shape_of((rows * count, width)), shape_of((rows, width), F32)),
        [SMEM] + [VMEM] * (2 * count + 2),
        6,
    )(place, *heads, *toks, out_all, norms)


def fixed(shape):
    return pl.BlockSpec(shape, lambda e: (0,) * len(shape), pipeline_mode=pl.Buffered(1))


def one_hot_block(slot_ref, at, rows):
    index = lax.broadcasted_iota(jnp.int32, (rows, slot_ref.shape[1]), 0) + at
    return jnp.where(index == slot_ref[...], 1.0, 0.0).astype(BF16)


def unsort(hot_ref, sorted_ref, outs):
    rows = outs[0].shape[0]
    for m, out in enumerate(outs):
        out[...] = dot_tn(hot_ref[:, m * rows : (m + 1) * rows], sorted_ref[...]).astype(BF16)


def pack_kernel(up_ref, down_ref, *refs):
    rest, out_ref = refs[:-1], refs[-1]
    units = down_ref.shape[0]
    out_ref[0:units, :] = up_ref[...].T.astype(BF16)
    out_ref[units : 2 * units, :] = down_ref[...].astype(BF16)
    out_ref[2 * units :, :] = jnp.concatenate([piece[...] for piece in rest], 0)


def pack_expert(up, down, rest):
    units, width = down.shape
    rows = 2 * units + sum(piece.shape[0] for piece in rest)
    return local_call(
        pack_kernel, "pack_expert", shape_of((rows, width)), [VMEM] * (2 + len(rest)), 3
    )(up, down, *rest)


def sorted_cot_kernel(slot_ref, *refs, count):
    cots, (down_ref, cot_ref, back_ref) = refs[:count], refs[count:]
    rows = cots[0].shape[0]
    capacity = cot_ref.shape[0]
    hot = one_hot_block(slot_ref, pl.program_id(0) * capacity, capacity)
    cot = sum(dot_nn(hot[:, m * rows : (m + 1) * rows], cots[m][...]) for m in range(count))
    cot = cot.astype(BF16)
    cot_ref[...] = cot
    back_ref[...] = dot_nt(cot, down_ref[...]).astype(BF16)


def sorted_cot(slot_row, cots, down):
    count = len(cots)
    rows, width = cots[0].shape
    total = rows * count
    hidden = down.shape[0]
    block_rows = min(256, rows)
    return pl.pallas_call(
        functools.partial(sorted_cot_kernel, count=count),
        grid=(total // block_rows,),
        in_specs=[fixed(slot_row.shape)] + [fixed((rows, width))] * count + [fixed(down.shape)],
        out_specs=[
            pl.BlockSpec((block_rows, width), lambda e: (e, 0)),
            pl.BlockSpec((block_rows, hidden), lambda e: (e, 0)),
        ],
        out_shape=[shape_of((total, width)), shape_of((total, hidden))],
        compiler_params=pltpu.CompilerParams(vmem_limit_bytes=16 * MIB),
        cost_estimate=cost(8),
        name="sorted_cot",
    )(slot_row, *cots, down)


def expert_back_kernel(cot_ref, pack_ref, back_ref):
    units = pack_ref.shape[1]
    for p in range(2):
        back_ref[:, p * units : (p + 1) * units] = dot_nt(cot_ref[...], pack_ref[p]).astype(BF16)


def expert_back(cot, pack, units):
    total, width = cot.shape
    experts = pack.shape[0] // 2
    capacity = total // experts
    return pl.pallas_call(
        expert_back_kernel,
        grid=(experts,),
        in_specs=[
            pl.BlockSpec((capacity, width), lambda e: (e, 0)),
            pl.BlockSpec((2, units, width), lambda e: (e, 1, 0)),
        ],
        out_specs=pl.BlockSpec((capacity, 2 * units), lambda e: (e, 0)),
        out_shape=shape_of((total, 2 * units)),
        compiler_params=pltpu.CompilerParams(vmem_limit_bytes=47 * MIB),
        cost_estimate=cost(4),
        name="expert_back",
    )(cot, pack)


def route_kernel(counts_ref, slot_ref, act_ref, side_ref, sorted_ref, table_ref, *, experts):
    expert = pl.program_id(0)
    capacity, lanes = table_ref.shape
    width = act_ref.shape[1]
    hot = one_hot_block(slot_ref, expert * capacity, capacity)
    act = dot_nn(hot, act_ref[...]).astype(BF16)
    lane = lax.broadcasted_iota(jnp.int32, (capacity, lanes), 1)

    def pick(values, index):
        return jnp.sum(jnp.where(lane == index, values, 0.0), -1, keepdims=True)

    def soft(values, inside):
        values = jnp.where(inside, values, neg_large)
        expo = jnp.exp(values - jnp.max(values, -1, keepdims=True))
        return expo / jnp.sum(expo, -1, keepdims=True)

    logits = dot_nn(act, side_ref[...])
    probs = soft(logits, lane < experts)
    coef = soft(logits, (lane >= experts) & (lane < experts + 2))
    gate = pick(probs, expert)
    coef0, coef1 = pick(coef, experts), pick(coef, experts + 1)
    live = jnp.where(
        lax.broadcasted_iota(jnp.int32, (capacity, 1), 0) < counts_ref[expert], 1.0, 0.0
    )
    scale = live * gate * coef1
    table = jnp.where(lane < experts, probs, 0.0)
    for at, column in enumerate((coef0, coef1, gate, live, scale)):
        table = jnp.where(lane == experts + at, column, table)
    table_ref[...] = table
    high = scale.astype(BF16).astype(F32)
    sorted_ref[:, :width] = act
    sorted_ref[:, width:] = jnp.where(
        lane == 0, high, jnp.where(lane == 1, scale - high, 0.0)
    ).astype(BF16)


def route(counts, slot_row, act, side, experts):
    total, width = act.shape
    capacity = total // experts
    lanes = side.shape[1]
    return pl.pallas_call(
        functools.partial(route_kernel, experts=experts),
        grid=(experts,),
        in_specs=[SMEM, fixed(slot_row.shape), fixed(act.shape), fixed(side.shape)],
        out_specs=[
            pl.BlockSpec((capacity, width + lanes), lambda e: (e, 0)),
            pl.BlockSpec((capacity, lanes), lambda e: (e, 0)),
        ],
        out_shape=[shape_of((total, width + lanes)), shape_of((total, lanes), F32)],
        compiler_params=pltpu.CompilerParams(vmem_limit_bytes=12 * MIB),
        cost_estimate=cost(4),
        name="route",
    )(counts, slot_row, act, side)


def mixture_kernel(
    slot_ref, act_ref, table_ref, back_ref, eback_ref, up_ref, pack_ref, side_ref, *refs,
    count, experts
):
    parts, refs = refs[:count], refs[count:]
    dpre_ref, hid_ref, ehid_ref, dside_ref, hot_ref, dact_ref = refs
    expert = pl.program_id(0)
    capacity, width = dpre_ref.shape[0], dact_ref.shape[1]
    at = pl.multiple_of(expert * capacity, capacity)
    hot_ref[pl.ds(at, capacity), :] = one_hot_block(slot_ref, at, capacity)
    act = act_ref[:, :width]
    table = table_ref[...]
    coef0, coef1, gate, live, scale = (
        table[:, experts + j : experts + j + 1] for j in range(5)
    )
    pre = dot_nn(act, up_ref[...])
    back = back_ref[...].astype(F32)
    hid, slope = gelu_pair(pre)
    dense_dot = jnp.sum(hid * back, -1, keepdims=True)
    dpre = (slope * (coef0 * back)).astype(BF16)
    hid_ref[...] = (coef0 * hid).astype(BF16)
    dpre_ref[...] = dpre
    dact = dot_nt(dpre, up_ref[...])
    expert_dot = jnp.zeros_like(dense_dot)
    units = pack_ref.shape[1]
    for p in range(2):
        here = slice(p * units, (p + 1) * units)
        pre = dot_nt(act, pack_ref[p])
        back = eback_ref[:, here].astype(F32)
        hid, slope = gelu_pair(pre)
        expert_dot = expert_dot + jnp.sum(hid * back, -1, keepdims=True)
        ehid_ref[:, here] = (scale * hid).astype(BF16)
        dact = dact + dot_nn((slope * (scale * back)).astype(BF16), pack_ref[p])
    expert_dot = live * expert_dot
    mean = coef0 * dense_dot + coef1 * gate * expert_dot
    dgate = coef1 * expert_dot
    lane = lax.broadcasted_iota(jnp.int32, table.shape, 1)
    dside = jnp.where(
        lane < experts, table * (jnp.where(lane == expert, dgate, 0.0) - gate * dgate), 0.0
    )
    dside = jnp.where(lane == experts, coef0 * (dense_dot - mean), dside)
    dside = jnp.where(lane == experts + 1, coef1 * (gate * expert_dot - mean), dside)
    high = dside.astype(BF16)
    rest = (dside - high.astype(F32)).astype(BF16)
    dside_ref[...] = high
    dact = dact + dot_nt(high, side_ref[...]) + dot_nt(rest, side_ref[...])
    dact_ref[pl.ds(at, capacity), :] = dact.astype(BF16)

    @pl.when(expert == pl.num_programs(0) - 1)
    def _():
        unsort(hot_ref, dact_ref, parts)


def mixture(slot_row, act, table, back, eback, up, pack, side, count):
    total, hidden = back.shape
    width = up.shape[0]
    rows = total // count
    experts, units = pack.shape[0] // 2, eback.shape[1] // 2
    capacity = total // experts
    lanes = side.shape[1]

    def block(columns):
        return pl.BlockSpec((capacity, columns), lambda e: (e, 0))

    return pl.pallas_call(
        functools.partial(mixture_kernel, count=count, experts=experts),
        grid=(experts,),
        in_specs=[
            fixed(slot_row.shape),
            block(width + lanes),
            block(lanes),
            block(hidden),
            block(2 * units),
            fixed(up.shape),
            pl.BlockSpec((2, units, width), lambda e: (e, 0, 0)),
            fixed(side.shape),
        ],
        out_specs=[fixed((rows, width))] * count
        + [block(hidden), block(hidden), block(2 * units), block(lanes)],
        out_shape=[shape_of((rows, width))] * count
        + [
            shape_of((total, hidden)),
            shape_of((total, hidden)),
            shape_of((total, 2 * units)),
            shape_of((total, lanes)),
        ],
        scratch_shapes=[pltpu.VMEM((total, total), BF16), pltpu.VMEM((total, width), BF16)],
        compiler_params=pltpu.CompilerParams(vmem_limit_bytes=52 * MIB),
        cost_estimate=cost(18),
        name="mixture",
    )(slot_row, act, table, back, eback, up, pack, side)


def output_kernel(slot_ref, hid_ref, ehid_ref, down_ref, pack_ref, *refs):
    parts, (hot_ref, sorted_ref) = refs[:-2], refs[-2:]
    expert = pl.program_id(0)
    capacity = hid_ref.shape[0]
    units = pack_ref.shape[1]
    at = pl.multiple_of(expert * capacity, capacity)
    hot_ref[pl.ds(at, capacity), :] = one_hot_block(slot_ref, at, capacity)
    dense = dot_nn(hid_ref[...], down_ref[...])
    routed = dot_nn(ehid_ref[:, :units], pack_ref[0]) + dot_nn(ehid_ref[:, units:], pack_ref[1])
    mixed = dense + routed
    sorted_ref[pl.ds(at, capacity), :] = mixed.astype(BF16)

    @pl.when(expert == pl.num_programs(0) - 1)
    def _():
        unsort(hot_ref, sorted_ref, parts)


def mixture_output(slot_row, hid, ehid, down, pack, count):
    total, hidden = hid.shape
    width = down.shape[1]
    experts, units = pack.shape[0] // 2, ehid.shape[1] // 2
    capacity = total // experts
    rows = total // count

    def block(columns):
        return pl.BlockSpec((capacity, columns), lambda e: (e, 0))

    return pl.pallas_call(
        output_kernel,
        grid=(experts,),
        in_specs=[
            fixed(slot_row.shape),
            block(hidden),
            block(2 * units),
            fixed(down.shape),
            pl.BlockSpec((2, units, width), lambda e: (e, 1, 0)),
        ],
        out_specs=[fixed((rows, width))] * count,
        out_shape=[shape_of((rows, width))] * count,
        scratch_shapes=[pltpu.VMEM((total, total), BF16), pltpu.VMEM((total, width), BF16)],
        compiler_params=pltpu.CompilerParams(vmem_limit_bytes=52 * MIB),
        cost_estimate=cost(10),
        name="mixture_output",
    )(slot_row, hid, ehid, down, pack)


def second_norm_kernel(*refs, got, count):
    parts, refs = refs[:got], refs[got:]
    resid_ref, cot_ref, norms_ref, out_ref = refs[:4]
    dresid_ref, low_ref, sums_ref = refs[4:7]
    dheads = refs[7:]
    upstream = sum(part[...].astype(F32) for part in parts)
    hat, inverse = normalize(resid_ref[...])
    sums_ref[...] = jnp.zeros_like(sums_ref)
    sums_ref[0:1, :] = jnp.sum(upstream * hat, 0, keepdims=True)
    sums_ref[1:2, :] = jnp.sum(upstream, 0, keepdims=True)
    dresid = cot_ref[...].astype(F32) + layer_norm_reverse(
        upstream, hat, inverse, norms_ref[2:3, :]
    )
    dresid_ref[...] = dresid
    low = dresid.astype(BF16)
    low_ref[...] = low
    for j in range(count):
        dheads[j][...] = dot_nt(low, out_ref[j]).astype(BF16)


def second_norm_reverse(parts, resid, cot, norms, out_all):
    rows, width = resid.shape
    count, head_width, _ = out_all.shape
    return local_call(
        functools.partial(second_norm_kernel, got=len(parts), count=count),
        "second_norm_reverse",
        [
            shape_of((rows, width), F32),
            shape_of((rows, width)),
            shape_of((8, width), F32),
        ]
        + [shape_of((rows, head_width))] * count,
        [VMEM] * (len(parts) + 4),
        3,
    )(*parts, resid, cot, norms, out_all)


def attend_backward_kernel(place_ref, length_ref, *refs, count, chunk):
    cots, refs = refs[:count], refs[count:]
    qkv_ref, lse_ref, weight_ref, out_ref = refs[:4]
    parts, (cot_ref, dk_ref, dv_ref, dqkv_ref) = refs[4 : 4 + count], refs[4 + count :]
    place_rows(place_ref, cots, cot_ref)
    rows = qkv_ref.shape[0]
    width = qkv_ref.shape[1] // 3
    scale = jnp.asarray(HEAD_DIM**-0.5, BF16)
    blocks = rows // chunk
    for block in range(blocks):
        at, keys = block * chunk, (block + 1) * chunk
        bias, causal = attend_masks(length_ref[0], keys, chunk)
        outs = []
        for head in range(width // HEAD_DIM):
            col = head * HEAD_DIM
            query = qkv_ref[at:keys, col : col + HEAD_DIM] * scale
            key = qkv_ref[0:keys, width + col : width + col + HEAD_DIM]
            value = qkv_ref[0:keys, 2 * width + col : 2 * width + col + HEAD_DIM]
            cot = cot_ref[at:keys, col : col + HEAD_DIM]
            scores = masked_scores(key, query, bias, causal, chunk)
            prob = jnp.exp(scores - lse_ref[head : head + 1, at:keys])
            dprob = dot_nt(value, cot)
            delta = jnp.sum(prob * dprob, 0, keepdims=True)
            dscore = (prob * (dprob - delta)).astype(BF16)
            dvalue = dot_nn(prob.astype(BF16), cot)
            dkey = dot_nn(dscore, query)
            outs.append(dot_tn(key * scale, dscore))
            here = slice(col, col + HEAD_DIM)
            if block > 0:
                dv_ref[0:at, here] += dvalue[:at]
                dk_ref[0:at, here] += dkey[:at]
            dv_ref[at:keys, here] = dvalue[at:]
            dk_ref[at:keys, here] = dkey[at:]
        dqkv_ref[at:keys, 0:width] = jnp.concatenate(outs, 0).T.astype(BF16)
    dqkv_ref[:, width : 2 * width] = dk_ref[...].astype(BF16)
    dqkv_ref[:, 2 * width : 3 * width] = dv_ref[...].astype(BF16)
    part_rows = parts[0].shape[0]
    for m in reversed(range(count)):
        at = pl.multiple_of(place_ref[m] * part_rows, part_rows)
        mine = dqkv_ref[pl.ds(at, part_rows), :]
        out_ref[m * part_rows : (m + 1) * part_rows, :] = mine
        total = sum(
            dot_nt(mine[:, c * width : (c + 1) * width], weight_ref[c]) for c in range(3)
        )
        parts[m][...] = total.astype(BF16)


def attend_backward(place, length, qkv, cots, lse, weight):
    count = len(cots)
    rows, wide3 = qkv.shape
    part_rows, width = rows // count, wide3 // 3
    heads = width // HEAD_DIM
    model = weight.shape[1]
    return local_call(
        functools.partial(attend_backward_kernel, count=count, chunk=min(256, rows)),
        "attend_backward",
        [shape_of((rows, wide3))] + [shape_of((part_rows, model))] * count,
        [SMEM, SMEM] + [VMEM] * (count + 3),
        12,
        [
            pltpu.VMEM((rows, width), BF16),
            pltpu.VMEM((rows, width), F32),
            pltpu.VMEM((rows, width), F32),
            pltpu.VMEM((rows, wide3), BF16),
        ],
    )(place, length, *cots, qkv, lse, weight)


def qkv_grad_kernel(owner_ref, *refs, count):
    acts, dones, toks = refs[:count], refs[count : 2 * count], refs[2 * count : 3 * count]
    dqkv_ref, even_ref, odd_ref, total_ref = refs[3 * count :]
    columns = dqkv_ref.shape[1]
    rows, width = acts[0].shape
    tile = min(256, width)
    for at in range(0, width, tile):
        total = sum(
            dot_tn(acts[m][:, at : at + tile], dqkv_ref[m * rows : (m + 1) * rows, :])
            for m in range(count)
        )
        total_ref[at : at + tile, :columns] = total.astype(BF16)
    first, second = 0.0, 0.0
    for m in range(count):
        hat, _ = normalize(toks[m][...].astype(F32))
        upstream = dones[m][...].astype(F32)
        first = first + jnp.sum(upstream * hat, 0, keepdims=True)
        second = second + jnp.sum(upstream, 0, keepdims=True)
    sums = jnp.concatenate([jnp.zeros((lane_pad - 2, width), F32), first, second], 0)
    total_ref[:, columns:] = sums.T.astype(BF16)
    owned = even_ref.shape[1]
    for m in range(2 * even_ref.shape[0]):
        at = pl.multiple_of(owner_ref[m] * owned, owned)
        (odd_ref if m % 2 else even_ref)[m // 2] = total_ref[pl.ds(at, owned), :]


def qkv_grad(owner, acts, dones, toks, dqkv):
    count = len(acts)
    width = acts[0].shape[1]
    columns = dqkv.shape[1] + lane_pad
    owners = owner.shape[0]
    half = shape_of((owners // 2, width // owners, columns))
    return local_call(
        functools.partial(qkv_grad_kernel, count=count),
        "qkv_grad",
        [half, half],
        [SMEM] + [VMEM] * (3 * count + 1),
        6,
        [pltpu.VMEM((width, columns), BF16)],
    )(owner, *acts, *dones, *toks, dqkv)


def first_norm_kernel(*refs, got):
    parts, (dresid_ref, tok_ref, norms_ref, out_ref) = refs[:got], refs[got:]
    upstream = sum(part[...].astype(F32) for part in parts)
    hat, inverse = normalize(tok_ref[...].astype(F32))
    out_ref[...] = dresid_ref[...] + layer_norm_reverse(
        upstream, hat, inverse, norms_ref[0:1, :]
    )


def first_norm_reverse(parts, dresid, tok, norms):
    rows, width = tok.shape
    return local_call(
        functools.partial(first_norm_kernel, got=len(parts)),
        "first_norm_reverse",
        shape_of((rows, width), F32),
        [VMEM] * (len(parts) + 3),
        2,
    )(*parts, dresid, tok, norms)


def shared_grad_kernel(place_ref, totals_ref, *refs, count, side):
    heads, refs = refs[:count], refs[count:]
    act_ref, cot_ref, dpre_ref, hid_ref, low_ref, sums_ref, dside_ref, out_ref = refs
    rows = low_ref.shape[0]
    hidden = hid_ref.shape[1]
    head_width = heads[0].shape[1]
    out_ref[:, :hidden] = dot_tn(act_ref[...], dpre_ref[...]).astype(BF16)
    out_ref[:, hidden : 2 * hidden] = dot_tn(cot_ref[...], hid_ref[...]).astype(BF16)
    at = pl.multiple_of(place_ref[0] * rows, rows)
    low = low_ref[...]
    for j in range(count):
        part = dot_tn(low, heads[j][pl.ds(at, rows), :])
        to = 2 * hidden + j * head_width
        out_ref[:, to : to + head_width] = part.astype(BF16)
    small = dot_tn(act_ref[...], dside_ref[...])
    tile = small.shape[0]
    lane = lax.broadcasted_iota(jnp.int32, small.shape, 1)
    sums = jnp.concatenate([sums_ref[...], jnp.zeros((lane_pad - 8, tile), F32)], 0).T
    small = jnp.where(lane == side, sums[:, 0:1], small)
    small = jnp.where(lane == side + 1, sums[:, 1:2], small)
    digit = lax.broadcasted_iota(jnp.int32, (8, lane_pad), 1) - (side + 2)
    row = jnp.zeros((8, lane_pad), F32)
    for e in range(side - 2):
        for d in range(4):
            value = lax.shift_right_logical(totals_ref[e], 3 * d) & 7
            row = jnp.where(digit == 4 * e + d, value.astype(F32), row)
    out_ref[:, 2 * hidden + count * head_width :] = (small + row[0:1, :]).astype(BF16)


def shared_grad(place, totals, heads, act, cot, dpre, hid, low, sums, dside, side):
    count = len(heads)
    total, width = cot.shape
    hidden = hid.shape[1]
    columns = 2 * hidden + count * heads[0].shape[1] + lane_pad
    tile = min(256, width)

    def columns_of(rows):
        return pl.BlockSpec((rows, tile), lambda i: (0, i))

    return pl.pallas_call(
        functools.partial(shared_grad_kernel, count=count, side=side),
        grid=(width // tile,),
        in_specs=[SMEM, SMEM]
        + [fixed(h.shape) for h in heads]
        + [columns_of(total), columns_of(total), fixed(dpre.shape), fixed(hid.shape)]
        + [columns_of(low.shape[0]), columns_of(8), fixed(dside.shape)],
        out_specs=pl.BlockSpec((tile, columns), lambda i: (i, 0)),
        out_shape=pltpu.HBM((width, columns), BF16),
        compiler_params=pltpu.CompilerParams(vmem_limit_bytes=24 * MIB),
        cost_estimate=cost(9),
        name="shared_grad",
    )(place, totals, *heads, act, cot, dpre, hid, low, sums, dside)


def owner_kernel(at_ref, *refs):
    count = (len(refs) - 5) // 2
    acts, cots = refs[:count], refs[count : 2 * count]
    pack_ref, dup_other, ddown_other, dup_mine, ddown_mine = refs[2 * count :]
    units, width = pack_ref.shape[1] // 2, pack_ref.shape[2]
    act = jnp.concatenate([block[:, :width] for block in acts], 0)
    scale = jnp.concatenate([block[:, width:] for block in acts], 0)
    scale = scale[:, 0:1].astype(F32) + scale[:, 1:2].astype(F32)
    cot = jnp.concatenate([block[...] for block in cots], 0)
    cot = (scale * cot.astype(F32)).astype(BF16)
    hid, slope = gelu_pair(dot_nt(act, pack_ref[0, 0:units, :]))
    dpre = (slope * dot_nt(cot, pack_ref[0, units : 2 * units, :])).astype(BF16)
    dup = dot_tn(act, dpre)
    ddown = dot_tn(hid.astype(BF16), cot)

    @pl.when(pl.program_id(0) == 0)
    def _():
        dup_other[...] = dup.astype(BF16)
        ddown_other[...] = ddown.astype(BF16)

    @pl.when(pl.program_id(0) == 1)
    def _():
        dup_mine[...] = dup
        ddown_mine[...] = ddown


def owner_grad(at, acts, cots, pack, units):
    width = pack.shape[2]
    up, down = (width, units), (units, width)

    def same(shape):
        return pl.BlockSpec(
            shape, lambda q, at: (0,) * len(shape), pipeline_mode=pl.Buffered(1)
        )

    return pl.pallas_call(
        owner_kernel,
        grid_spec=pltpu.PrefetchScalarGridSpec(
            num_scalar_prefetch=1,
            grid=(2,),
            in_specs=[same(block.shape) for block in (*acts, *cots)]
            + [pl.BlockSpec((1, 2 * units, width), lambda q, at: (at[q], 0, 0))],
            out_specs=[same(up), same(down), same(up), same(down)],
        ),
        out_shape=[shape_of(up), shape_of(down), shape_of(up, F32), shape_of(down, F32)],
        compiler_params=pltpu.CompilerParams(vmem_limit_bytes=40 * MIB),
        cost_estimate=cost(16),
        name="owner_grad",
    )(at, *acts, *cots, pack)


def update_into(outs, gradient, state, rate):
    master, moment, average = (ref[...] for ref in state)
    new_moment = momentum_decay * moment + gradient
    new_master = master - rate * (gradient + momentum_decay * new_moment)
    outs[0][...] = gradient
    outs[1][...] = new_master
    outs[2][...] = new_moment
    outs[3][...] = average_decay * average + (1.0 - average_decay) * new_master


def four(states):
    return [shape_of(state.shape, F32) for group in states for state in (group[0],) * 4]


def hidden_update_kernel(grad_ref, *refs, rate):
    hidden = refs[0].shape[1]
    grad = grad_ref[...].astype(F32)
    update_into(refs[6:10], grad[:, :hidden], refs[0:3], rate)
    update_into(refs[10:14], grad[:, hidden : 2 * hidden].T, refs[3:6], rate)


def hidden_update(grad, states, rate):
    return local_call(
        functools.partial(hidden_update_kernel, rate=rate),
        "hidden_update",
        four(states),
        [VMEM] * 7,
        4,
    )(grad, *states[0], *states[1])


def out_update_kernel(*refs, got, side, rate):
    parts, refs = refs[:got], refs[got:]
    total = sum(part[...].astype(F32) for part in parts)
    width = refs[0].shape[0]
    outs = refs[12:]
    update_into(outs[0:4], total[:, :width].T, refs[0:3], rate)
    small = total[:, width:].T
    update_into(outs[4:8], small[: side - 2], refs[3:6], rate)
    update_into(outs[8:12], small[side - 2 : side], refs[6:9], rate)
    norm = jnp.concatenate([small[lane_pad - 2 :], small[side : side + 2]], 0)
    update_into(outs[12:16], norm, refs[9:12], rate)
    outs[16][...] = small


def out_update(parts, states, side, rate):
    turned = [tuple(v.T for v in group) for group in states[1:3]]
    states = (states[0], *turned, states[3])
    made = local_call(
        functools.partial(out_update_kernel, got=len(parts), side=side, rate=rate),
        "out_update",
        four(states) + [shape_of((lane_pad, parts[0].shape[0]), F32)],
        [VMEM] * (len(parts) + 12),
        2,
    )(*parts, *states[0], *states[1], *states[2], *states[3])
    return list(made[:4]) + [v.T for v in made[4:12]] + list(made[12:])


def qkv_update_kernel(*refs, got, rate):
    parts, refs = refs[:got], refs[got:]
    qkv, outs = refs[0:3], refs[3:]
    total = sum(part[0].astype(F32) for part in parts)
    width = qkv[0].shape[2]
    gradient = jnp.stack([total[:, c * width : (c + 1) * width] for c in range(3)], 0)
    update_into(outs[0:4], gradient, qkv, rate)


def qkv_update(parts, state, rate):
    return local_call(
        functools.partial(qkv_update_kernel, got=len(parts), rate=rate),
        "qkv_update",
        four((state,)),
        [VMEM] * (len(parts) + 3),
        2,
    )(*parts, *state)


def swap(values, axis, bit):
    count = lax.axis_size(axis)
    return lax.ppermute(values, axis, [(i, i ^ bit) for i in range(count)])


def bits_of(axis):
    count = lax.axis_size(axis)
    return [1 << b for b in range(count.bit_length() - 1)]


def gather_pieces(own, axis, *earlier):
    pieces = {0: own}
    for bit in reversed(bits_of(axis)):
        for m in list(pieces):
            known = [*earlier] if m else []
            if bit == 1 and m:
                known.append(pieces[1])
            sent = after(pieces[m], *known) if known else pieces[m]
            pieces[m | bit] = swap(sent, axis, bit)
    return [pieces[m] for m in range(lax.axis_size(axis))]


def first_step(blocks, axis, *earlier):
    held = {m: [block] for m, block in enumerate(blocks)}
    for m in sorted((m for m in held if m & 1 and m > 1), reverse=True):
        got = swap(after(held.pop(m)[0], *earlier), axis, 1)
        held[m ^ 1] = [(held[m ^ 1][0].astype(F32) + got.astype(F32)).astype(BF16)]
    return held


def last_steps(held, axis, *earlier):
    held = {m: [after(parts[0], *earlier)] if m else list(parts) for m, parts in held.items()}
    if len(held) > 2:
        held[1] = [after(held[1][0], held[2][0])]
    for bit in bits_of(axis):
        for m in sorted((m for m in held if m & bit), reverse=True):
            parts = held.pop(m)
            sent = parts[0]
            if len(parts) > 1:
                sent = sum(part.astype(F32) for part in parts).astype(BF16)
            held[m ^ bit].append(swap(sent, axis, bit))
    return held[0]


def after(values, *earlier):
    return lax.optimization_barrier((values, earlier))[0]


def reduce_halves(even, odd, axis):
    bit = 1
    while True:
        got = swap(odd, axis, bit)
        if even.shape[0] == 1:
            return [even, got]
        held = (even.astype(F32) + got.astype(F32)).astype(BF16)
        even, odd, bit = held[0::2], held[1::2], bit * 2


def exchange_pieces(pieces, axis):
    return [pieces[0]] + [swap(pieces[m], axis, m) for m in range(1, len(pieces))]


def apply_update(gradient, master, moment, average, step_rate):
    new_moment = momentum_decay * moment + gradient
    new_master = master - step_rate * (gradient + momentum_decay * new_moment)
    new_average = average_decay * average + (1.0 - average_decay) * new_master
    return (gradient, new_master, new_moment, new_average)


def token_slots(route_ids, length, expert_count, capacity):
    rows = route_ids.shape[0]
    at = jnp.arange(rows, dtype=jnp.int32)
    live = at < length
    hot = (route_ids[:, None] == jnp.arange(expert_count, dtype=jnp.int32)[None, :]) & live[:, None]
    hot_f = hot.astype(F32)
    before = (at[None, :] < at[:, None]).astype(BF16)
    earlier = dot_nn(before, hot.astype(BF16))
    pos = jnp.sum(earlier * hot_f, -1)
    totals = jnp.sum(hot_f, 0)
    kept = live & (pos < capacity)
    counts = jnp.minimum(totals, capacity)
    spare = capacity - counts
    order = jnp.arange(expert_count)
    spare_before = jnp.sum(jnp.where(order[None, :] < order[:, None], spare[None, :], 0.0), 1)
    rank = at.astype(F32) - jnp.sum(jnp.minimum(earlier, capacity), -1)
    inside = (rank[:, None] >= spare_before[None, :]) & (rank[:, None] < (spare_before + spare)[None, :])
    base = order.astype(F32) * capacity + counts - spare_before
    loose = jnp.sum(jnp.where(inside, base[None, :] + rank[:, None], 0.0), -1)
    slot = jnp.where(kept, route_ids * capacity + pos.astype(jnp.int32), loose.astype(jnp.int32))
    return (slot.astype(jnp.int32), totals.astype(jnp.int32))


def on_device(
    tokens,
    cotangent,
    lengths,
    routes,
    norm_params,
    qkv_weight,
    out_weight,
    up_weight,
    down_weight,
    router_weight,
    mix_weight,
    norm_master,
    norm_moment,
    norm_average,
    qkv_master,
    qkv_moment,
    qkv_average,
    out_master,
    out_moment,
    out_average,
    up_master,
    up_moment,
    up_average,
    down_master,
    down_moment,
    down_average,
    router_master,
    router_moment,
    router_average,
    mix_master,
    mix_moment,
    mix_average,
    expert_up_master,
    expert_up_moment,
    expert_up_average,
    expert_down_master,
    expert_down_moment,
    expert_down_average,
):
    narrow_count = lax.axis_size("narrow")
    wide_count = lax.axis_size("wide")
    narrow_index = lax.axis_index("narrow")
    wide_index = lax.axis_index("wide")
    local_rows, width = tokens.shape
    group_rows = local_rows * narrow_count
    expert_count = router_weight.shape[1]
    capacity = group_rows // expert_count
    head_width = qkv_weight.shape[2]
    norms = norm_params.astype(F32)
    place = (narrow_index ^ jnp.arange(narrow_count, dtype=jnp.int32)).astype(jnp.int32)

    units = expert_up_master.shape[2]
    out_rows = out_weight.shape[0] // wide_count
    out_slice = lax.dynamic_slice_in_dim(out_weight, wide_index * out_rows, out_rows, 0)
    out_slices = exchange_pieces([out_slice] * narrow_count, "narrow")
    packed = pack_expert(expert_up_master[0], expert_down_master[0], out_slices)
    pack = lax.all_gather(packed, "wide", axis=0, tiled=False)
    out_all = pack[:, 2 * units :].reshape(wide_count, narrow_count, out_rows, width)
    out_all = out_all.transpose(1, 0, 2, 3).reshape(narrow_count, head_width, width)

    slot, totals = token_slots(routes[:, 0], lengths[0], expert_count, capacity)
    tok_pieces = gather_pieces(after(tokens, out_slices[1]), "narrow", packed)
    slot_row = jnp.concatenate(
        [
            lax.dynamic_slice_in_dim(slot, place[m] * local_rows, local_rows, 0)
            for m in range(narrow_count)
        ],
        0,
    )[None, :]
    side = jnp.concatenate(
        [
            router_weight,
            mix_weight,
            jnp.zeros((width, lane_pad - expert_count - 2), BF16),
        ],
        1,
    )

    projected = [project(piece, norms, qkv_weight) for piece in tok_pieces]
    act_pieces = [pair[0] for pair in projected]
    qkv_pieces = [pair[1] for pair in projected]
    heads, log_sums, qkv = attend_forward(after(place, slot_row), lengths, qkv_pieces)
    cot_pieces = gather_pieces(after(cotangent, tok_pieces[-1]), "narrow", heads)
    cot_sorted, dense_back = sorted_cot(slot_row, cot_pieces, down_weight)
    head_pieces = gather_pieces(after(heads, cot_pieces), "narrow", cot_sorted)

    def to_owners(rows):
        got = []
        for m in range(0, wide_count, 2):
            at = ((wide_index ^ m) // 2) * capacity
            block = lax.dynamic_slice_in_dim(rows, at, capacity, 0)
            got.append(block if m == 0 else swap(block, "wide", m))
        return got

    routed_back = expert_back(cot_sorted, pack, units)
    cot_blocks = to_owners(cot_sorted)
    act_two, resid = join(
        after(place, routed_back), head_pieces, tok_pieces, out_all, norms
    )
    act_sorted, table = route(
        jnp.minimum(totals, capacity), slot_row, act_two, side, expert_count
    )
    act_blocks = to_owners(act_sorted)
    made = mixture(
        slot_row,
        act_sorted,
        table,
        dense_back,
        routed_back,
        up_weight,
        pack,
        side,
        narrow_count,
    )
    dact_parts = made[:narrow_count]
    dense_dpre, dense_hid, expert_hid, dside = made[narrow_count:]
    dact_parts = [*dact_parts[:-1], after(dact_parts[-1], act_blocks[1:3])]
    mlp_parts = mixture_output(
        slot_row, dense_hid, expert_hid, down_weight, pack, narrow_count
    )
    dact_held = first_step(dact_parts, "narrow")
    dact_sum = last_steps(dact_held, "narrow", mlp_parts)
    second = second_norm_reverse(
        [after(dact_sum[0], act_blocks[3:], cot_blocks[1:3])] + dact_sum[1:], resid, cotangent, norms, out_all
    )
    dresid, resid_low, sums_two = second[:3]
    dheads = exchange_pieces(second[3:], "narrow")
    side_columns = expert_count + 2
    shared_part = shared_grad(
        place,
        totals,
        head_pieces,
        act_sorted,
        cot_sorted,
        dense_dpre,
        dense_hid,
        resid_low,
        sums_two,
        dside,
        side_columns,
    )
    shared_rows = lax.psum_scatter(
        after(shared_part, dheads), "wide", scatter_dimension=0, tiled=True)
    back = attend_backward(
        after(place, shared_part, cot_blocks), lengths, qkv, dheads, log_sums, qkv_weight
    )
    dqkv, done_parts = back[0], back[1:]
    mlp_held = first_step(mlp_parts, "narrow", dheads)
    done_held = first_step(done_parts, "narrow", mlp_held[narrow_count // 2])
    halves = jnp.stack([wide_index ^ 1, wide_index]).astype(jnp.int32)
    owned = owner_grad(after(halves, back, mlp_held[narrow_count // 2]), act_blocks, cot_blocks, pack, units)
    owned_got = [swap(part, "wide", 1) for part in owned[:2]]

    owner = (wide_index ^ jnp.arange(wide_count, dtype=jnp.int32)).astype(jnp.int32)
    even, odd = qkv_grad(after(owner, done_held[narrow_count // 2]), act_pieces, done_parts, tok_pieces, dqkv)
    step_rate = rate_base / math.sqrt(group_rows * wide_count)
    expert_rate = step_rate * (expert_count / 4.0) ** 1.5
    done_sum = last_steps(done_held, "narrow", owned)
    expert_new = []
    for gradient, got, state, rate in (
        (owned[2], owned_got[0], (expert_up_master, expert_up_moment, expert_up_average), expert_rate),
        (
            owned[3],
            owned_got[1],
            (expert_down_master, expert_down_moment, expert_down_average),
            expert_down_boost * expert_rate,
        ),
    ):
        gradient = after(gradient, done_sum) + got.astype(F32)
        expert_new.extend(apply_update(gradient[None], *state, rate))
    mlp_sum = last_steps(mlp_held, "narrow", done_sum)
    qkv_sum = reduce_halves(even, after(odd, done_sum), "wide")

    hidden_new = hidden_update(
        shared_rows,
        ((up_master, up_moment, up_average), (down_master, down_moment, down_average)),
        step_rate,
    )

    shared_out = after(shared_rows, mlp_sum, expert_new)
    qkv_columns = 3 * head_width
    small_one = sum(part[0, :, qkv_columns:].astype(F32) for part in qkv_sum)
    out_at = 2 * up_weight.shape[1]
    small_at = out_at + narrow_count * head_width
    small = (shared_out[:, small_at:].astype(F32) + small_one).astype(BF16)
    out_parts = exchange_pieces(
        [
            jnp.concatenate(
                [
                    shared_out[:, out_at + m * head_width : out_at + (m + 1) * head_width],
                    small,
                ],
                1,
            )
            for m in range(narrow_count)
        ],
        "narrow",
    )
    out_new = out_update(
        out_parts,
        (
            (out_master, out_moment, out_average),
            (router_master, router_moment, router_average),
            (mix_master, mix_moment, mix_average),
            (norm_master, norm_moment, norm_average),
        ),
        side_columns,
        step_rate,
    )

    qkv_new = qkv_update(qkv_sum, (qkv_master, qkv_moment, qkv_average), step_rate)
    input_grad = first_norm_reverse(
        done_sum,
        dresid,
        tokens,
        norms,
    )
    digits = out_new[16][side_columns + 2 : side_columns + 2 + 4 * expert_count, 0]
    digits = jnp.sum(digits.reshape(expert_count, 4) * jnp.asarray([1.0, 8.0, 64.0, 512.0]), 1)
    expert_counts = (digits / narrow_count + 0.5).astype(jnp.int32)
    block_out = (resid + sum(part.astype(F32) for part in mlp_sum)).astype(BF16)
    results = [block_out, input_grad, expert_counts]
    for group in (out_new[12:16], qkv_new, out_new[0:4], hidden_new, out_new[4:12]):
        results.extend(group)
    results.extend(expert_new)
    return tuple(results)


def solution(mesh):
    in_specs = (
        P(("wide", "narrow"), None),
        P(("wide", "narrow"), None),
        P("wide"),
        P("wide", None),
        P(),
        P(None, None, "narrow"),
        P("narrow", None),
        P(None, "narrow"),
        P("narrow", None),
        P(),
        P(),
        P(None, "wide"),
        P(None, "wide"),
        P(None, "wide"),
        P(None, "wide", "narrow"),
        P(None, "wide", "narrow"),
        P(None, "wide", "narrow"),
        P("narrow", "wide"),
        P("narrow", "wide"),
        P("narrow", "wide"),
        P("wide", "narrow"),
        P("wide", "narrow"),
        P("wide", "narrow"),
        P("narrow", "wide"),
        P("narrow", "wide"),
        P("narrow", "wide"),
        P("wide", None),
        P("wide", None),
        P("wide", None),
        P("wide", None),
        P("wide", None),
        P("wide", None),
        P("wide", None, "narrow"),
        P("wide", None, "narrow"),
        P("wide", None, "narrow"),
        P("wide", "narrow", None),
        P("wide", "narrow", None),
        P("wide", "narrow", None),
    )
    out_specs = (
        P(("wide", "narrow"), None),
        P(("wide", "narrow"), None),
        P(),
        P(None, "wide"),
        P(None, "wide"),
        P(None, "wide"),
        P(None, "wide"),
        P(None, "wide", "narrow"),
        P(None, "wide", "narrow"),
        P(None, "wide", "narrow"),
        P(None, "wide", "narrow"),
        P("narrow", "wide"),
        P("narrow", "wide"),
        P("narrow", "wide"),
        P("narrow", "wide"),
        P("wide", "narrow"),
        P("wide", "narrow"),
        P("wide", "narrow"),
        P("wide", "narrow"),
        P("narrow", "wide"),
        P("narrow", "wide"),
        P("narrow", "wide"),
        P("narrow", "wide"),
        P("wide", None),
        P("wide", None),
        P("wide", None),
        P("wide", None),
        P("wide", None),
        P("wide", None),
        P("wide", None),
        P("wide", None),
        P("wide", None, "narrow"),
        P("wide", None, "narrow"),
        P("wide", None, "narrow"),
        P("wide", None, "narrow"),
        P("wide", "narrow", None),
        P("wide", "narrow", None),
        P("wide", "narrow", None),
        P("wide", "narrow", None),
    )
    return jax.shard_map(
        on_device, mesh=mesh, in_specs=in_specs, out_specs=out_specs, check_vma=False
    )
```

```python
import functools
import math

import jax
import jax.numpy as jnp
from jax import lax
from jax.experimental import pallas as pl
from jax.experimental.pallas import tpu as pltpu
from jax.sharding import PartitionSpec as P

HEAD_DIM = 64
F32 = jnp.float32
BF16 = jnp.bfloat16

precise = lax.Precision.HIGHEST
eps_norm = 1e-05
momentum_decay = 0.9
average_decay = 0.75
rate_base = 0.05
expert_down_boost = 12.0
neg_large = -1e30
lane_pad = 128


def dot_nn(a, b):
    return jnp.dot(a, b, preferred_element_type=F32)


def dot_nt(a, b):
    return lax.dot_general(a, b, (((1,), (1,)), ((), ())), preferred_element_type=F32)


def dot_tn(a, b):
    return lax.dot_general(a, b, (((0,), (0,)), ((), ())), preferred_element_type=F32)


def normalize(values):
    mean_val = jnp.mean(values, -1, keepdims=True)
    centered = values - mean_val
    inverse = lax.rsqrt(jnp.mean(centered * centered, -1, keepdims=True) + eps_norm)
    return (centered * inverse, inverse)


def layer_norm_reverse(upstream, normed, inverse, gain):
    scaled = upstream * gain
    return inverse * (
        scaled
        - jnp.mean(scaled, -1, keepdims=True)
        - normed * jnp.mean(scaled * normed, -1, keepdims=True)
    )


def gelu_pair(pre):
    root = math.sqrt(2.0 / math.pi)
    square = pre * pre
    half = 0.5 + 0.5 * jnp.tanh(pre * (root + (root * 0.044715) * square))
    hid = pre * half
    slope = half + hid * (1.0 - half) * (2.0 * root + (root * 0.26829) * square)
    return (hid, slope)


def attend_masks(length, keys, chunk):
    key_at = lax.broadcasted_iota(jnp.int32, (keys, 1), 0)
    bias = jnp.where(key_at < length, 0.0, neg_large).astype(F32)
    below = lax.broadcasted_iota(jnp.int32, (chunk, chunk), 0)
    across = lax.broadcasted_iota(jnp.int32, (chunk, chunk), 1)
    return (bias, below <= across)


def masked_scores(key, query, bias, causal, chunk):
    scores = dot_nt(key, query) + bias
    edge = jnp.where(causal, scores[-chunk:], neg_large)
    if scores.shape[0] == chunk:
        return edge
    return jnp.concatenate([scores[:-chunk], edge], 0)


VMEM = pl.BlockSpec(memory_space=pltpu.VMEM)
SMEM = pl.BlockSpec(memory_space=pltpu.SMEM)
MIB = 2**20
LIMITS = {"project": 12, "attend_forward": 16, "join": 20, "pack_expert": 12, "second_norm_reverse": 12, "attend_backward": 60, "qkv_grad": 60, "first_norm_reverse": 10, "owner_grad": 44, "hidden_update": 12, "out_update": 8, "qkv_update": 8}


def shape_of(shape, dtype=BF16):
    return jax.ShapeDtypeStruct(shape, dtype)


def cost(micros):
    return pl.CostEstimate(flops=int(micros * 1e5), bytes_accessed=1024, transcendentals=0)


def local_call(kernel, name, outs, in_specs, micros, scratch=()):
    return pl.pallas_call(
        kernel,
        out_shape=outs,
        in_specs=in_specs,
        out_specs=jax.tree.map(lambda _: VMEM, outs),
        scratch_shapes=list(scratch),
        compiler_params=pltpu.CompilerParams(vmem_limit_bytes=LIMITS[name] * MIB),
        cost_estimate=cost(micros),
        name=name,
    )


def project_kernel(tok_ref, norms_ref, weight_ref, act_ref, qkv_ref):
    hat, _ = normalize(tok_ref[...].astype(F32))
    act = (hat * norms_ref[0:1, :] + norms_ref[1:2, :]).astype(BF16)
    act_ref[...] = act
    width = weight_ref.shape[2]
    for c in range(3):
        qkv_ref[:, c * width : (c + 1) * width] = dot_nn(act, weight_ref[c]).astype(BF16)


def project(tok, norms, weight):
    rows, width = tok.shape
    columns = 3 * weight.shape[2]
    return local_call(
        project_kernel,
        "project",
        (shape_of((rows, width)), shape_of((rows, columns))),
        [VMEM] * 3,
        2,
    )(tok, norms, weight)


def place_rows(place_ref, pieces, full_ref):
    rows = pieces[0].shape[0]
    for m, piece in enumerate(pieces):
        at = pl.multiple_of(place_ref[m] * rows, rows)
        full_ref[pl.ds(at, rows), :] = piece[...]


def attend_forward_kernel(place_ref, length_ref, *refs, count, chunk):
    pieces, (heads_ref, sums_ref, qkv_ref) = refs[:count], refs[count:]
    place_rows(place_ref, pieces, qkv_ref)
    rows = qkv_ref.shape[0]
    width = qkv_ref.shape[1] // 3
    scale = jnp.asarray(HEAD_DIM**-0.5, BF16)
    for block in range(rows // chunk):
        at, keys = block * chunk, (block + 1) * chunk
        bias, causal = attend_masks(length_ref[0], keys, chunk)
        outs = []
        for head in range(width // HEAD_DIM):
            col = head * HEAD_DIM
            query = qkv_ref[at:keys, col : col + HEAD_DIM] * scale
            key = qkv_ref[0:keys, width + col : width + col + HEAD_DIM]
            value = qkv_ref[0:keys, 2 * width + col : 2 * width + col + HEAD_DIM]
            scores = masked_scores(key, query, bias, causal, chunk)
            top = jnp.max(scores, 0, keepdims=True)
            expo = jnp.exp(scores - top)
            total = jnp.sum(expo, 0, keepdims=True)
            soft = (expo * (1.0 / total)).astype(BF16)
            outs.append(dot_tn(value, soft))
            sums_ref[head : head + 1, at:keys] = top + jnp.log(total)
        heads_ref[at:keys, :] = jnp.concatenate(outs, 0).T.astype(BF16)


def attend_forward(place, length, pieces):
    count = len(pieces)
    rows = pieces[0].shape[0] * count
    width = pieces[0].shape[1] // 3
    heads = width // HEAD_DIM
    return local_call(
        functools.partial(attend_forward_kernel, count=count, chunk=min(256, rows)),
        "attend_forward",
        (shape_of((rows, width)), shape_of((heads, rows), F32), shape_of((rows, 3 * width))),
        [SMEM, SMEM] + [VMEM] * count,
        11,
    )(place, length, *pieces)


def join_kernel(place_ref, *refs, count):
    heads, toks = refs[:count], refs[count : 2 * count]
    out_ref, norms_ref, act_ref, resid_ref = refs[2 * count :]
    rows = toks[0].shape[0]
    for m in range(count):
        at = pl.multiple_of(place_ref[m] * rows, rows)
        total = toks[m][...].astype(F32)
        for j in range(count):
            total = total + dot_nn(heads[j][pl.ds(at, rows), :], out_ref[j])
        if m == 0:
            resid_ref[...] = total
        hat, _ = normalize(total)
        act = hat * norms_ref[2:3, :] + norms_ref[3:4, :]
        act_ref[m * rows : (m + 1) * rows, :] = act.astype(BF16)


def join(place, heads, toks, out_all, norms):
    count = len(heads)
    rows, width = toks[0].shape
    return local_call(
        functools.partial(join_kernel, count=count),
        "join",
        (shape_of((rows * count, width)), shape_of((rows, width), F32)),
        [SMEM] + [VMEM] * (2 * count + 2),
        6,
    )(place, *heads, *toks, out_all, norms)


def fixed(shape):
    return pl.BlockSpec(shape, lambda e: (0,) * len(shape), pipeline_mode=pl.Buffered(1))


def one_hot_block(slot_ref, at, rows):
    index = lax.broadcasted_iota(jnp.int32, (rows, slot_ref.shape[1]), 0) + at
    return jnp.where(index == slot_ref[...], 1.0, 0.0).astype(BF16)


def unsort(hot_ref, sorted_ref, outs):
    rows = outs[0].shape[0]
    for m, out in enumerate(outs):
        out[...] = dot_tn(hot_ref[:, m * rows : (m + 1) * rows], sorted_ref[...]).astype(BF16)


def pack_kernel(up_ref, down_ref, *refs):
    rest, out_ref = refs[:-1], refs[-1]
    units = down_ref.shape[0]
    out_ref[0:units, :] = up_ref[...].T.astype(BF16)
    out_ref[units : 2 * units, :] = down_ref[...].astype(BF16)
    out_ref[2 * units :, :] = jnp.concatenate([piece[...] for piece in rest], 0)


def pack_expert(up, down, rest):
    units, width = down.shape
    rows = 2 * units + sum(piece.shape[0] for piece in rest)
    return local_call(
        pack_kernel, "pack_expert", shape_of((rows, width)), [VMEM] * (2 + len(rest)), 3
    )(up, down, *rest)


def sorted_cot_kernel(slot_ref, *refs, count):
    cots, (down_ref, cot_ref, back_ref) = refs[:count], refs[count:]
    rows = cots[0].shape[0]
    capacity = cot_ref.shape[0]
    hot = one_hot_block(slot_ref, pl.program_id(0) * capacity, capacity)
    cot = sum(dot_nn(hot[:, m * rows : (m + 1) * rows], cots[m][...]) for m in range(count))
    cot = cot.astype(BF16)
    cot_ref[...] = cot
    back_ref[...] = dot_nt(cot, down_ref[...]).astype(BF16)


def sorted_cot(slot_row, cots, down):
    count = len(cots)
    rows, width = cots[0].shape
    total = rows * count
    hidden = down.shape[0]
    block_rows = min(256, rows)
    return pl.pallas_call(
        functools.partial(sorted_cot_kernel, count=count),
        grid=(total // block_rows,),
        in_specs=[fixed(slot_row.shape)] + [fixed((rows, width))] * count + [fixed(down.shape)],
        out_specs=[
            pl.BlockSpec((block_rows, width), lambda e: (e, 0)),
            pl.BlockSpec((block_rows, hidden), lambda e: (e, 0)),
        ],
        out_shape=[shape_of((total, width)), shape_of((total, hidden))],
        compiler_params=pltpu.CompilerParams(vmem_limit_bytes=16 * MIB),
        cost_estimate=cost(8),
        name="sorted_cot",
    )(slot_row, *cots, down)


def expert_back_kernel(cot_ref, pack_ref, back_ref):
    units = pack_ref.shape[1]
    for p in range(2):
        back_ref[:, p * units : (p + 1) * units] = dot_nt(cot_ref[...], pack_ref[p]).astype(BF16)


def expert_back(cot, pack, units):
    total, width = cot.shape
    experts = pack.shape[0] // 2
    capacity = total // experts
    return pl.pallas_call(
        expert_back_kernel,
        grid=(experts,),
        in_specs=[
            pl.BlockSpec((capacity, width), lambda e: (e, 0)),
            pl.BlockSpec((2, units, width), lambda e: (e, 1, 0)),
        ],
        out_specs=pl.BlockSpec((capacity, 2 * units), lambda e: (e, 0)),
        out_shape=shape_of((total, 2 * units)),
        compiler_params=pltpu.CompilerParams(vmem_limit_bytes=47 * MIB),
        cost_estimate=cost(4),
        name="expert_back",
    )(cot, pack)


def route_kernel(counts_ref, slot_ref, act_ref, side_ref, sorted_ref, table_ref, *, experts):
    expert = pl.program_id(0)
    capacity, lanes = table_ref.shape
    width = act_ref.shape[1]
    hot = one_hot_block(slot_ref, expert * capacity, capacity)
    act = dot_nn(hot, act_ref[...]).astype(BF16)
    lane = lax.broadcasted_iota(jnp.int32, (capacity, lanes), 1)

    def pick(values, index):
        return jnp.sum(jnp.where(lane == index, values, 0.0), -1, keepdims=True)

    def soft(values, inside):
        values = jnp.where(inside, values, neg_large)
        expo = jnp.exp(values - jnp.max(values, -1, keepdims=True))
        return expo / jnp.sum(expo, -1, keepdims=True)

    logits = dot_nn(act, side_ref[...])
    probs = soft(logits, lane < experts)
    coef = soft(logits, (lane >= experts) & (lane < experts + 2))
    gate = pick(probs, expert)
    coef0, coef1 = pick(coef, experts), pick(coef, experts + 1)
    live = jnp.where(
        lax.broadcasted_iota(jnp.int32, (capacity, 1), 0) < counts_ref[expert], 1.0, 0.0
    )
    scale = live * gate * coef1
    table = jnp.where(lane < experts, probs, 0.0)
    for at, column in enumerate((coef0, coef1, gate, live, scale)):
        table = jnp.where(lane == experts + at, column, table)
    table_ref[...] = table
    high = scale.astype(BF16).astype(F32)
    sorted_ref[:, :width] = act
    sorted_ref[:, width:] = jnp.where(
        lane == 0, high, jnp.where(lane == 1, scale - high, 0.0)
    ).astype(BF16)


def route(counts, slot_row, act, side, experts):
    total, width = act.shape
    capacity = total // experts
    lanes = side.shape[1]
    return pl.pallas_call(
        functools.partial(route_kernel, experts=experts),
        grid=(experts,),
        in_specs=[SMEM, fixed(slot_row.shape), fixed(act.shape), fixed(side.shape)],
        out_specs=[
            pl.BlockSpec((capacity, width + lanes), lambda e: (e, 0)),
            pl.BlockSpec((capacity, lanes), lambda e: (e, 0)),
        ],
        out_shape=[shape_of((total, width + lanes)), shape_of((total, lanes), F32)],
        compiler_params=pltpu.CompilerParams(vmem_limit_bytes=12 * MIB),
        cost_estimate=cost(4),
        name="route",
    )(counts, slot_row, act, side)


def mixture_kernel(
    slot_ref, act_ref, table_ref, back_ref, eback_ref, up_ref, pack_ref, side_ref, *refs,
    count, experts
):
    parts, refs = refs[:count], refs[count:]
    dpre_ref, hid_ref, ehid_ref, dside_ref, hot_ref, dact_ref = refs
    expert = pl.program_id(0)
    capacity, width = dpre_ref.shape[0], dact_ref.shape[1]
    at = pl.multiple_of(expert * capacity, capacity)
    hot_ref[pl.ds(at, capacity), :] = one_hot_block(slot_ref, at, capacity)
    act = act_ref[:, :width]
    table = table_ref[...]
    coef0, coef1, gate, live, scale = (
        table[:, experts + j : experts + j + 1] for j in range(5)
    )
    pre = dot_nn(act, up_ref[...])
    back = back_ref[...].astype(F32)
    hid, slope = gelu_pair(pre)
    dense_dot = jnp.sum(hid * back, -1, keepdims=True)
    dpre = (slope * (coef0 * back)).astype(BF16)
    hid_ref[...] = (coef0 * hid).astype(BF16)
    dpre_ref[...] = dpre
    dact = dot_nt(dpre, up_ref[...])
    expert_dot = jnp.zeros_like(dense_dot)
    units = pack_ref.shape[1]
    for p in range(2):
        here = slice(p * units, (p + 1) * units)
        pre = dot_nt(act, pack_ref[p])
        back = eback_ref[:, here].astype(F32)
        hid, slope = gelu_pair(pre)
        expert_dot = expert_dot + jnp.sum(hid * back, -1, keepdims=True)
        ehid_ref[:, here] = (scale * hid).astype(BF16)
        dact = dact + dot_nn((slope * (scale * back)).astype(BF16), pack_ref[p])
    expert_dot = live * expert_dot
    mean = coef0 * dense_dot + coef1 * gate * expert_dot
    dgate = coef1 * expert_dot
    lane = lax.broadcasted_iota(jnp.int32, table.shape, 1)
    dside = jnp.where(
        lane < experts, table * (jnp.where(lane == expert, dgate, 0.0) - gate * dgate), 0.0
    )
    dside = jnp.where(lane == experts, coef0 * (dense_dot - mean), dside)
    dside = jnp.where(lane == experts + 1, coef1 * (gate * expert_dot - mean), dside)
    high = dside.astype(BF16)
    rest = (dside - high.astype(F32)).astype(BF16)
    dside_ref[...] = high
    dact = dact + dot_nt(high, side_ref[...]) + dot_nt(rest, side_ref[...])
    dact_ref[pl.ds(at, capacity), :] = dact.astype(BF16)

    @pl.when(expert == pl.num_programs(0) - 1)
    def _():
        unsort(hot_ref, dact_ref, parts)


def mixture(slot_row, act, table, back, eback, up, pack, side, count):
    total, hidden = back.shape
    width = up.shape[0]
    rows = total // count
    experts, units = pack.shape[0] // 2, eback.shape[1] // 2
    capacity = total // experts
    lanes = side.shape[1]

    def block(columns):
        return pl.BlockSpec((capacity, columns), lambda e: (e, 0))

    return pl.pallas_call(
        functools.partial(mixture_kernel, count=count, experts=experts),
        grid=(experts,),
        in_specs=[
            fixed(slot_row.shape),
            block(width + lanes),
            block(lanes),
            block(hidden),
            block(2 * units),
            fixed(up.shape),
            pl.BlockSpec((2, units, width), lambda e: (e, 0, 0)),
            fixed(side.shape),
        ],
        out_specs=[fixed((rows, width))] * count
        + [block(hidden), block(hidden), block(2 * units), block(lanes)],
        out_shape=[shape_of((rows, width))] * count
        + [
            shape_of((total, hidden)),
            shape_of((total, hidden)),
            shape_of((total, 2 * units)),
            shape_of((total, lanes)),
        ],
        scratch_shapes=[pltpu.VMEM((total, total), BF16), pltpu.VMEM((total, width), BF16)],
        compiler_params=pltpu.CompilerParams(vmem_limit_bytes=52 * MIB),
        cost_estimate=cost(18),
        name="mixture",
    )(slot_row, act, table, back, eback, up, pack, side)


def output_kernel(slot_ref, hid_ref, ehid_ref, down_ref, pack_ref, *refs):
    parts, (hot_ref, sorted_ref) = refs[:-2], refs[-2:]
    expert = pl.program_id(0)
    capacity = hid_ref.shape[0]
    units = pack_ref.shape[1]
    at = pl.multiple_of(expert * capacity, capacity)
    hot_ref[pl.ds(at, capacity), :] = one_hot_block(slot_ref, at, capacity)
    dense = dot_nn(hid_ref[...], down_ref[...])
    routed = dot_nn(ehid_ref[:, :units], pack_ref[0]) + dot_nn(ehid_ref[:, units:], pack_ref[1])
    mixed = dense + routed
    sorted_ref[pl.ds(at, capacity), :] = mixed.astype(BF16)

    @pl.when(expert == pl.num_programs(0) - 1)
    def _():
        unsort(hot_ref, sorted_ref, parts)


def mixture_output(slot_row, hid, ehid, down, pack, count):
    total, hidden = hid.shape
    width = down.shape[1]
    experts, units = pack.shape[0] // 2, ehid.shape[1] // 2
    capacity = total // experts
    rows = total // count

    def block(columns):
        return pl.BlockSpec((capacity, columns), lambda e: (e, 0))

    return pl.pallas_call(
        output_kernel,
        grid=(experts,),
        in_specs=[
            fixed(slot_row.shape),
            block(hidden),
            block(2 * units),
            fixed(down.shape),
            pl.BlockSpec((2, units, width), lambda e: (e, 1, 0)),
        ],
        out_specs=[fixed((rows, width))] * count,
        out_shape=[shape_of((rows, width))] * count,
        scratch_shapes=[pltpu.VMEM((total, total), BF16), pltpu.VMEM((total, width), BF16)],
        compiler_params=pltpu.CompilerParams(vmem_limit_bytes=52 * MIB),
        cost_estimate=cost(10),
        name="mixture_output",
    )(slot_row, hid, ehid, down, pack)


def second_norm_kernel(*refs, got, count):
    parts, refs = refs[:got], refs[got:]
    resid_ref, cot_ref, norms_ref, out_ref = refs[:4]
    dresid_ref, low_ref, sums_ref = refs[4:7]
    dheads = refs[7:]
    upstream = sum(part[...].astype(F32) for part in parts)
    hat, inverse = normalize(resid_ref[...])
    sums_ref[...] = jnp.zeros_like(sums_ref)
    sums_ref[0:1, :] = jnp.sum(upstream * hat, 0, keepdims=True)
    sums_ref[1:2, :] = jnp.sum(upstream, 0, keepdims=True)
    dresid = cot_ref[...].astype(F32) + layer_norm_reverse(
        upstream, hat, inverse, norms_ref[2:3, :]
    )
    dresid_ref[...] = dresid
    low = dresid.astype(BF16)
    low_ref[...] = low
    for j in range(count):
        dheads[j][...] = dot_nt(low, out_ref[j]).astype(BF16)


def second_norm_reverse(parts, resid, cot, norms, out_all):
    rows, width = resid.shape
    count, head_width, _ = out_all.shape
    return local_call(
        functools.partial(second_norm_kernel, got=len(parts), count=count),
        "second_norm_reverse",
        [
            shape_of((rows, width), F32),
            shape_of((rows, width)),
            shape_of((8, width), F32),
        ]
        + [shape_of((rows, head_width))] * count,
        [VMEM] * (len(parts) + 4),
        3,
    )(*parts, resid, cot, norms, out_all)


def attend_backward_kernel(place_ref, length_ref, *refs, count, chunk):
    cots, refs = refs[:count], refs[count:]
    qkv_ref, lse_ref, weight_ref, out_ref = refs[:4]
    parts, (cot_ref, dk_ref, dv_ref, dqkv_ref) = refs[4 : 4 + count], refs[4 + count :]
    place_rows(place_ref, cots, cot_ref)
    rows = qkv_ref.shape[0]
    width = qkv_ref.shape[1] // 3
    scale = jnp.asarray(HEAD_DIM**-0.5, BF16)
    blocks = rows // chunk
    for block in range(blocks):
        at, keys = block * chunk, (block + 1) * chunk
        bias, causal = attend_masks(length_ref[0], keys, chunk)
        outs = []
        for head in range(width // HEAD_DIM):
            col = head * HEAD_DIM
            query = qkv_ref[at:keys, col : col + HEAD_DIM] * scale
            key = qkv_ref[0:keys, width + col : width + col + HEAD_DIM]
            value = qkv_ref[0:keys, 2 * width + col : 2 * width + col + HEAD_DIM]
            cot = cot_ref[at:keys, col : col + HEAD_DIM]
            scores = masked_scores(key, query, bias, causal, chunk)
            prob = jnp.exp(scores - lse_ref[head : head + 1, at:keys])
            dprob = dot_nt(value, cot)
            delta = jnp.sum(prob * dprob, 0, keepdims=True)
            dscore = (prob * (dprob - delta)).astype(BF16)
            dvalue = dot_nn(prob.astype(BF16), cot)
            dkey = dot_nn(dscore, query)
            outs.append(dot_tn(key * scale, dscore))
            here = slice(col, col + HEAD_DIM)
            if block > 0:
                dv_ref[0:at, here] += dvalue[:at]
                dk_ref[0:at, here] += dkey[:at]
            dv_ref[at:keys, here] = dvalue[at:]
            dk_ref[at:keys, here] = dkey[at:]
        dqkv_ref[at:keys, 0:width] = jnp.concatenate(outs, 0).T.astype(BF16)
    dqkv_ref[:, width : 2 * width] = dk_ref[...].astype(BF16)
    dqkv_ref[:, 2 * width : 3 * width] = dv_ref[...].astype(BF16)
    part_rows = parts[0].shape[0]
    for m in reversed(range(count)):
        at = pl.multiple_of(place_ref[m] * part_rows, part_rows)
        mine = dqkv_ref[pl.ds(at, part_rows), :]
        out_ref[m * part_rows : (m + 1) * part_rows, :] = mine
        total = sum(
            dot_nt(mine[:, c * width : (c + 1) * width], weight_ref[c]) for c in range(3)
        )
        parts[m][...] = total.astype(BF16)


def attend_backward(place, length, qkv, cots, lse, weight):
    count = len(cots)
    rows, wide3 = qkv.shape
    part_rows, width = rows // count, wide3 // 3
    heads = width // HEAD_DIM
    model = weight.shape[1]
    return local_call(
        functools.partial(attend_backward_kernel, count=count, chunk=min(256, rows)),
        "attend_backward",
        [shape_of((rows, wide3))] + [shape_of((part_rows, model))] * count,
        [SMEM, SMEM] + [VMEM] * (count + 3),
        12,
        [
            pltpu.VMEM((rows, width), BF16),
            pltpu.VMEM((rows, width), F32),
            pltpu.VMEM((rows, width), F32),
            pltpu.VMEM((rows, wide3), BF16),
        ],
    )(place, length, *cots, qkv, lse, weight)


def qkv_grad_kernel(owner_ref, *refs, count):
    acts, dones, toks = refs[:count], refs[count : 2 * count], refs[2 * count : 3 * count]
    dqkv_ref, even_ref, odd_ref, total_ref = refs[3 * count :]
    columns = dqkv_ref.shape[1]
    rows, width = acts[0].shape
    tile = min(256, width)
    for at in range(0, width, tile):
        total = sum(
            dot_tn(acts[m][:, at : at + tile], dqkv_ref[m * rows : (m + 1) * rows, :])
            for m in range(count)
        )
        total_ref[at : at + tile, :columns] = total.astype(BF16)
    first, second = 0.0, 0.0
    for m in range(count):
        hat, _ = normalize(toks[m][...].astype(F32))
        upstream = dones[m][...].astype(F32)
        first = first + jnp.sum(upstream * hat, 0, keepdims=True)
        second = second + jnp.sum(upstream, 0, keepdims=True)
    sums = jnp.concatenate([jnp.zeros((lane_pad - 2, width), F32), first, second], 0)
    total_ref[:, columns:] = sums.T.astype(BF16)
    owned = even_ref.shape[1]
    for m in range(2 * even_ref.shape[0]):
        at = pl.multiple_of(owner_ref[m] * owned, owned)
        (odd_ref if m % 2 else even_ref)[m // 2] = total_ref[pl.ds(at, owned), :]


def qkv_grad(owner, acts, dones, toks, dqkv):
    count = len(acts)
    width = acts[0].shape[1]
    columns = dqkv.shape[1] + lane_pad
    owners = owner.shape[0]
    half = shape_of((owners // 2, width // owners, columns))
    return local_call(
        functools.partial(qkv_grad_kernel, count=count),
        "qkv_grad",
        [half, half],
        [SMEM] + [VMEM] * (3 * count + 1),
        6,
        [pltpu.VMEM((width, columns), BF16)],
    )(owner, *acts, *dones, *toks, dqkv)


def first_norm_kernel(*refs, got):
    parts, (dresid_ref, tok_ref, norms_ref, out_ref) = refs[:got], refs[got:]
    upstream = sum(part[...].astype(F32) for part in parts)
    hat, inverse = normalize(tok_ref[...].astype(F32))
    out_ref[...] = dresid_ref[...] + layer_norm_reverse(
        upstream, hat, inverse, norms_ref[0:1, :]
    )


def first_norm_reverse(parts, dresid, tok, norms):
    rows, width = tok.shape
    return local_call(
        functools.partial(first_norm_kernel, got=len(parts)),
        "first_norm_reverse",
        shape_of((rows, width), F32),
        [VMEM] * (len(parts) + 3),
        2,
    )(*parts, dresid, tok, norms)


def dense_grad_kernel(act_ref, cot_ref, dpre_ref, hid_ref, out_ref):
    hidden = hid_ref.shape[1]
    out_ref[:, :hidden] = dot_tn(act_ref[...], dpre_ref[...]).astype(BF16)
    out_ref[:, hidden:] = dot_tn(cot_ref[...], hid_ref[...]).astype(BF16)


def columns_of(rows, tile):
    return pl.BlockSpec((rows, tile), lambda i: (0, i))


def dense_grad(act, cot, dpre, hid, columns):
    total, width = cot.shape
    tile = min(256, width)
    return pl.pallas_call(
        dense_grad_kernel,
        grid=(width // tile,),
        in_specs=[
            columns_of(total, tile),
            columns_of(total, tile),
            fixed(dpre.shape),
            fixed(hid.shape),
        ],
        out_specs=pl.BlockSpec((tile, 2 * hid.shape[1]), lambda i: (i, 0)),
        out_shape=pltpu.HBM((width, columns), BF16),
        compiler_params=pltpu.CompilerParams(vmem_limit_bytes=24 * MIB),
        cost_estimate=cost(7),
        name="dense_grad",
    )(act, cot, dpre, hid)


def out_grad_kernel(place_ref, *refs, count):
    heads, (low_ref, _, out_ref) = refs[:count], refs[count:]
    rows = low_ref.shape[0]
    head_width = heads[0].shape[1]
    at = pl.multiple_of(place_ref[0] * rows, rows)
    low = low_ref[...]
    for j in range(count):
        part = dot_tn(low, heads[j][pl.ds(at, rows), :])
        out_ref[:, j * head_width : (j + 1) * head_width] = part.astype(BF16)


def out_grad(place, heads, low, shared, at):
    count = len(heads)
    rows, width = low.shape
    columns = count * heads[0].shape[1]
    tile = min(256, width)
    return pl.pallas_call(
        functools.partial(out_grad_kernel, count=count),
        grid=(width // tile,),
        in_specs=[SMEM]
        + [fixed(h.shape) for h in heads]
        + [columns_of(rows, tile), pl.BlockSpec(memory_space=pl.ANY)],
        out_specs=pl.BlockSpec((tile, columns), lambda i: (i, at // columns)),
        out_shape=pltpu.HBM(shared.shape, BF16),
        input_output_aliases={count + 2: 0},
        compiler_params=pltpu.CompilerParams(vmem_limit_bytes=16 * MIB),
        cost_estimate=cost(3),
        name="out_grad",
    )(place, *heads, low, shared)


def side_grad_kernel(totals_ref, act_ref, sums_ref, dside_ref, _, out_ref, *, side):
    small = dot_tn(act_ref[...], dside_ref[...])
    tile = small.shape[0]
    lane = lax.broadcasted_iota(jnp.int32, small.shape, 1)
    sums = jnp.concatenate([sums_ref[...], jnp.zeros((lane_pad - 8, tile), F32)], 0).T
    small = jnp.where(lane == side, sums[:, 0:1], small)
    small = jnp.where(lane == side + 1, sums[:, 1:2], small)
    digit = lax.broadcasted_iota(jnp.int32, (8, lane_pad), 1) - (side + 2)
    row = jnp.zeros((8, lane_pad), F32)
    for e in range(side - 2):
        for d in range(4):
            value = lax.shift_right_logical(totals_ref[e], 3 * d) & 7
            row = jnp.where(digit == 4 * e + d, value.astype(F32), row)
    out_ref[...] = (small + row[0:1, :]).astype(BF16)


def side_grad(totals, act, sums, dside, shared, at, side):
    width = sums.shape[1]
    tile = min(256, width)
    return pl.pallas_call(
        functools.partial(side_grad_kernel, side=side),
        grid=(width // tile,),
        in_specs=[SMEM, columns_of(act.shape[0], tile), columns_of(8, tile), fixed(dside.shape)]
        + [pl.BlockSpec(memory_space=pl.ANY)],
        out_specs=pl.BlockSpec((tile, lane_pad), lambda i: (i, at // lane_pad)),
        out_shape=pltpu.HBM(shared.shape, BF16),
        input_output_aliases={4: 0},
        compiler_params=pltpu.CompilerParams(vmem_limit_bytes=16 * MIB),
        cost_estimate=cost(2),
        name="side_grad",
    )(totals, act, sums, dside, shared)


def owner_kernel(at_ref, *refs):
    count = (len(refs) - 5) // 2
    acts, cots = refs[:count], refs[count : 2 * count]
    pack_ref, dup_other, ddown_other, dup_mine, ddown_mine = refs[2 * count :]
    units, width = pack_ref.shape[1] // 2, pack_ref.shape[2]
    act = jnp.concatenate([block[:, :width] for block in acts], 0)
    scale = jnp.concatenate([block[:, width:] for block in acts], 0)
    scale = scale[:, 0:1].astype(F32) + scale[:, 1:2].astype(F32)
    cot = jnp.concatenate([block[...] for block in cots], 0)
    cot = (scale * cot.astype(F32)).astype(BF16)
    hid, slope = gelu_pair(dot_nt(act, pack_ref[0, 0:units, :]))
    dpre = (slope * dot_nt(cot, pack_ref[0, units : 2 * units, :])).astype(BF16)
    dup = dot_tn(act, dpre)
    ddown = dot_tn(hid.astype(BF16), cot)

    @pl.when(pl.program_id(0) == 0)
    def _():
        dup_other[...] = dup.astype(BF16)
        ddown_other[...] = ddown.astype(BF16)

    @pl.when(pl.program_id(0) == 1)
    def _():
        dup_mine[...] = dup
        ddown_mine[...] = ddown


def owner_grad(at, acts, cots, pack, units):
    width = pack.shape[2]
    up, down = (width, units), (units, width)

    def same(shape):
        return pl.BlockSpec(
            shape, lambda q, at: (0,) * len(shape), pipeline_mode=pl.Buffered(1)
        )

    return pl.pallas_call(
        owner_kernel,
        grid_spec=pltpu.PrefetchScalarGridSpec(
            num_scalar_prefetch=1,
            grid=(2,),
            in_specs=[same(block.shape) for block in (*acts, *cots)]
            + [pl.BlockSpec((1, 2 * units, width), lambda q, at: (at[q], 0, 0))],
            out_specs=[same(up), same(down), same(up), same(down)],
        ),
        out_shape=[shape_of(up), shape_of(down), shape_of(up, F32), shape_of(down, F32)],
        compiler_params=pltpu.CompilerParams(vmem_limit_bytes=40 * MIB),
        cost_estimate=cost(16),
        name="owner_grad",
    )(at, *acts, *cots, pack)


def update_into(outs, gradient, state, rate):
    master, moment, average = (ref[...] for ref in state)
    new_moment = momentum_decay * moment + gradient
    new_master = master - rate * (gradient + momentum_decay * new_moment)
    outs[0][...] = gradient
    outs[1][...] = new_master
    outs[2][...] = new_moment
    outs[3][...] = average_decay * average + (1.0 - average_decay) * new_master


def four(states):
    return [shape_of(state.shape, F32) for group in states for state in (group[0],) * 4]


def hidden_update_kernel(grad_ref, *refs, rate):
    hidden = refs[0].shape[1]
    grad = grad_ref[...].astype(F32)
    update_into(refs[6:10], grad[:, :hidden], refs[0:3], rate)
    update_into(refs[10:14], grad[:, hidden : 2 * hidden].T, refs[3:6], rate)


def hidden_update(grad, states, rate):
    return local_call(
        functools.partial(hidden_update_kernel, rate=rate),
        "hidden_update",
        four(states),
        [VMEM] * 7,
        4,
    )(grad, *states[0], *states[1])


def out_update_kernel(*refs, got, side, rate):
    parts, refs = refs[:got], refs[got:]
    total = sum(part[...].astype(F32) for part in parts)
    width = refs[0].shape[0]
    outs = refs[12:]
    update_into(outs[0:4], total[:, :width].T, refs[0:3], rate)
    small = total[:, width:].T
    update_into(outs[4:8], small[: side - 2], refs[3:6], rate)
    update_into(outs[8:12], small[side - 2 : side], refs[6:9], rate)
    norm = jnp.concatenate([small[lane_pad - 2 :], small[side : side + 2]], 0)
    update_into(outs[12:16], norm, refs[9:12], rate)
    outs[16][...] = small


def out_update(parts, states, side, rate):
    turned = [tuple(v.T for v in group) for group in states[1:3]]
    states = (states[0], *turned, states[3])
    made = local_call(
        functools.partial(out_update_kernel, got=len(parts), side=side, rate=rate),
        "out_update",
        four(states) + [shape_of((lane_pad, parts[0].shape[0]), F32)],
        [VMEM] * (len(parts) + 12),
        2,
    )(*parts, *states[0], *states[1], *states[2], *states[3])
    return list(made[:4]) + [v.T for v in made[4:12]] + list(made[12:])


def qkv_update_kernel(*refs, got, rate):
    parts, refs = refs[:got], refs[got:]
    qkv, outs = refs[0:3], refs[3:]
    total = sum(part[0].astype(F32) for part in parts)
    width = qkv[0].shape[2]
    gradient = jnp.stack([total[:, c * width : (c + 1) * width] for c in range(3)], 0)
    update_into(outs[0:4], gradient, qkv, rate)


def qkv_update(parts, state, rate):
    return local_call(
        functools.partial(qkv_update_kernel, got=len(parts), rate=rate),
        "qkv_update",
        four((state,)),
        [VMEM] * (len(parts) + 3),
        2,
    )(*parts, *state)


def swap(values, axis, bit):
    count = lax.axis_size(axis)
    return lax.ppermute(values, axis, [(i, i ^ bit) for i in range(count)])


def bits_of(axis):
    count = lax.axis_size(axis)
    return [1 << b for b in range(count.bit_length() - 1)]


def gather_pieces(own, axis, *earlier):
    pieces = {0: own}
    for bit in reversed(bits_of(axis)):
        for m in list(pieces):
            known = [*earlier] if m else []
            if bit == 1 and m:
                known.append(pieces[1])
            sent = after(pieces[m], *known) if known else pieces[m]
            pieces[m | bit] = swap(sent, axis, bit)
    return [pieces[m] for m in range(lax.axis_size(axis))]


def first_step(blocks, axis, *earlier):
    held = {m: [block] for m, block in enumerate(blocks)}
    for m in sorted((m for m in held if m & 1 and m > 1), reverse=True):
        got = swap(after(held.pop(m)[0], *earlier), axis, 1)
        held[m ^ 1] = [(held[m ^ 1][0].astype(F32) + got.astype(F32)).astype(BF16)]
    return held


def last_steps(held, axis, *earlier):
    held = {m: [after(parts[0], *earlier)] if m else list(parts) for m, parts in held.items()}
    if len(held) > 2:
        held[1] = [after(held[1][0], held[2][0])]
    for bit in bits_of(axis):
        for m in sorted((m for m in held if m & bit), reverse=True):
            parts = held.pop(m)
            sent = parts[0]
            if len(parts) > 1:
                sent = sum(part.astype(F32) for part in parts).astype(BF16)
            held[m ^ bit].append(swap(sent, axis, bit))
    return held[0]


def after(values, *earlier):
    return lax.optimization_barrier((values, earlier))[0]


def reduce_halves(even, odd, axis, bit):
    while True:
        got = swap(odd, axis, bit)
        if even.shape[0] == 1:
            return [even, got]
        held = (even.astype(F32) + got.astype(F32)).astype(BF16)
        even, odd, bit = held[0::2], held[1::2], bit * 2


def exchange_pieces(pieces, axis):
    return [pieces[0]] + [swap(pieces[m], axis, m) for m in range(1, len(pieces))]


def apply_update(gradient, master, moment, average, step_rate):
    new_moment = momentum_decay * moment + gradient
    new_master = master - step_rate * (gradient + momentum_decay * new_moment)
    new_average = average_decay * average + (1.0 - average_decay) * new_master
    return (gradient, new_master, new_moment, new_average)


def token_slots(route_ids, length, expert_count, capacity):
    rows = route_ids.shape[0]
    at = jnp.arange(rows, dtype=jnp.int32)
    live = at < length
    hot = (route_ids[:, None] == jnp.arange(expert_count, dtype=jnp.int32)[None, :]) & live[:, None]
    hot_f = hot.astype(F32)
    before = (at[None, :] < at[:, None]).astype(BF16)
    earlier = dot_nn(before, hot.astype(BF16))
    pos = jnp.sum(earlier * hot_f, -1)
    totals = jnp.sum(hot_f, 0)
    kept = live & (pos < capacity)
    counts = jnp.minimum(totals, capacity)
    spare = capacity - counts
    order = jnp.arange(expert_count)
    spare_before = jnp.sum(jnp.where(order[None, :] < order[:, None], spare[None, :], 0.0), 1)
    rank = at.astype(F32) - jnp.sum(jnp.minimum(earlier, capacity), -1)
    inside = (rank[:, None] >= spare_before[None, :]) & (rank[:, None] < (spare_before + spare)[None, :])
    base = order.astype(F32) * capacity + counts - spare_before
    loose = jnp.sum(jnp.where(inside, base[None, :] + rank[:, None], 0.0), -1)
    slot = jnp.where(kept, route_ids * capacity + pos.astype(jnp.int32), loose.astype(jnp.int32))
    return (slot.astype(jnp.int32), totals.astype(jnp.int32))


def on_device(
    tokens,
    cotangent,
    lengths,
    routes,
    norm_params,
    qkv_weight,
    out_weight,
    up_weight,
    down_weight,
    router_weight,
    mix_weight,
    norm_master,
    norm_moment,
    norm_average,
    qkv_master,
    qkv_moment,
    qkv_average,
    out_master,
    out_moment,
    out_average,
    up_master,
    up_moment,
    up_average,
    down_master,
    down_moment,
    down_average,
    router_master,
    router_moment,
    router_average,
    mix_master,
    mix_moment,
    mix_average,
    expert_up_master,
    expert_up_moment,
    expert_up_average,
    expert_down_master,
    expert_down_moment,
    expert_down_average,
):
    narrow_count = lax.axis_size("narrow")
    wide_count = lax.axis_size("wide")
    narrow_index = lax.axis_index("narrow")
    wide_index = lax.axis_index("wide")
    local_rows, width = tokens.shape
    group_rows = local_rows * narrow_count
    expert_count = router_weight.shape[1]
    capacity = group_rows // expert_count
    head_width = qkv_weight.shape[2]
    norms = norm_params.astype(F32)
    place = (narrow_index ^ jnp.arange(narrow_count, dtype=jnp.int32)).astype(jnp.int32)

    units = expert_up_master.shape[2]
    out_rows = out_weight.shape[0] // wide_count
    out_slice = lax.dynamic_slice_in_dim(out_weight, wide_index * out_rows, out_rows, 0)
    out_slices = exchange_pieces([out_slice] * narrow_count, "narrow")
    packed = pack_expert(expert_up_master[0], expert_down_master[0], out_slices)
    pack = lax.all_gather(packed, "wide", axis=0, tiled=False)
    out_all = pack[:, 2 * units :].reshape(wide_count, narrow_count, out_rows, width)
    out_all = out_all.transpose(1, 0, 2, 3).reshape(narrow_count, head_width, width)

    slot, totals = token_slots(routes[:, 0], lengths[0], expert_count, capacity)
    tok_pieces = gather_pieces(after(tokens, out_slices[1]), "narrow", packed)
    slot_row = jnp.concatenate(
        [
            lax.dynamic_slice_in_dim(slot, place[m] * local_rows, local_rows, 0)
            for m in range(narrow_count)
        ],
        0,
    )[None, :]
    side = jnp.concatenate(
        [
            router_weight,
            mix_weight,
            jnp.zeros((width, lane_pad - expert_count - 2), BF16),
        ],
        1,
    )

    projected = [project(piece, norms, qkv_weight) for piece in tok_pieces]
    act_pieces = [pair[0] for pair in projected]
    qkv_pieces = [pair[1] for pair in projected]
    heads, log_sums, qkv = attend_forward(after(place, slot_row), lengths, qkv_pieces)
    cot_pieces = gather_pieces(after(cotangent, tok_pieces[-1]), "narrow", heads)
    cot_sorted, dense_back = sorted_cot(slot_row, cot_pieces, down_weight)
    head_pieces = gather_pieces(after(heads, cot_pieces), "narrow", cot_sorted)

    def to_owners(rows):
        got = []
        for m in range(0, wide_count, 2):
            at = ((wide_index ^ m) // 2) * capacity
            block = lax.dynamic_slice_in_dim(rows, at, capacity, 0)
            got.append(block if m == 0 else swap(block, "wide", m))
        return got

    routed_back = expert_back(cot_sorted, pack, units)
    cot_blocks = to_owners(cot_sorted)
    act_two, resid = join(
        after(place, routed_back), head_pieces, tok_pieces, out_all, norms
    )
    act_sorted, table = route(
        jnp.minimum(totals, capacity), slot_row, act_two, side, expert_count
    )
    act_blocks = to_owners(act_sorted)
    made = mixture(
        slot_row,
        act_sorted,
        table,
        dense_back,
        routed_back,
        up_weight,
        pack,
        side,
        narrow_count,
    )
    dact_parts = made[:narrow_count]
    dense_dpre, dense_hid, expert_hid, dside = made[narrow_count:]
    dact_parts = [*dact_parts[:-1], after(dact_parts[-1], act_blocks[1:3])]
    mlp_parts = mixture_output(
        slot_row, dense_hid, expert_hid, down_weight, pack, narrow_count
    )
    dact_held = first_step(dact_parts, "narrow")
    dact_sum = last_steps(dact_held, "narrow", mlp_parts)
    out_at = 2 * up_weight.shape[1]
    small_at = out_at + narrow_count * head_width
    shared_part = dense_grad(
        after(act_sorted, mlp_parts), cot_sorted, dense_dpre, dense_hid, small_at + lane_pad
    )
    second = second_norm_reverse(
        [after(dact_sum[0], act_blocks[3:], cot_blocks[1:3], shared_part)] + dact_sum[1:], resid, cotangent, norms, out_all
    )
    dresid, resid_low, sums_two = second[:3]
    dheads = exchange_pieces(second[3:], "narrow")
    side_columns = expert_count + 2
    shared_part = out_grad(place, head_pieces, resid_low, shared_part, out_at)
    shared_part = side_grad(
        totals, act_sorted, sums_two, dside, shared_part, small_at, side_columns
    )
    shared_rows = lax.psum_scatter(
        after(shared_part, dheads), "wide", scatter_dimension=0, tiled=True)
    back = attend_backward(
        after(place, shared_part), lengths, qkv, dheads, log_sums, qkv_weight
    )
    dqkv, done_parts = back[0], back[1:]
    mlp_held = first_step(mlp_parts, "narrow", dheads)
    done_held = first_step(done_parts, "narrow", mlp_held[narrow_count // 2])

    owner = (wide_index ^ jnp.arange(wide_count, dtype=jnp.int32)).astype(jnp.int32)
    even, odd = qkv_grad(owner, act_pieces, done_parts, tok_pieces, dqkv)
    halves = jnp.stack([wide_index ^ 1, wide_index]).astype(jnp.int32)
    owned = owner_grad(after(halves, even), act_blocks, cot_blocks, pack, units)
    owned_got = [swap(part, "wide", 1) for part in owned[:2]]
    step_rate = rate_base / math.sqrt(group_rows * wide_count)
    expert_rate = step_rate * (expert_count / 4.0) ** 1.5
    done_sum = last_steps(done_held, "narrow", even)
    qkv_got = swap(after(odd, done_sum, owned), "wide", 1)
    qkv_held = (even.astype(F32) + qkv_got.astype(F32)).astype(BF16)
    hidden_new = hidden_update(
        shared_rows,
        ((up_master, up_moment, up_average), (down_master, down_moment, down_average)),
        step_rate,
    )
    qkv_sum = reduce_halves(qkv_held[0::2], after(qkv_held[1::2], hidden_new), "wide", 2)
    expert_new = []
    for gradient, got, state, rate in (
        (owned[2], owned_got[0], (expert_up_master, expert_up_moment, expert_up_average), expert_rate),
        (
            owned[3],
            owned_got[1],
            (expert_down_master, expert_down_moment, expert_down_average),
            expert_down_boost * expert_rate,
        ),
    ):
        gradient = after(gradient, qkv_held) + got.astype(F32)
        expert_new.extend(apply_update(gradient[None], *state, rate))
    mlp_sum = last_steps(mlp_held, "narrow", done_sum)


    shared_out = after(shared_rows, mlp_sum, expert_new)
    qkv_columns = 3 * head_width
    small_one = sum(part[0, :, qkv_columns:].astype(F32) for part in qkv_sum)
    small = (shared_out[:, small_at:].astype(F32) + small_one).astype(BF16)
    out_parts = exchange_pieces(
        [
            jnp.concatenate(
                [
                    shared_out[:, out_at + m * head_width : out_at + (m + 1) * head_width],
                    small,
                ],
                1,
            )
            for m in range(narrow_count)
        ],
        "narrow",
    )
    out_new = out_update(
        out_parts,
        (
            (out_master, out_moment, out_average),
            (router_master, router_moment, router_average),
            (mix_master, mix_moment, mix_average),
            (norm_master, norm_moment, norm_average),
        ),
        side_columns,
        step_rate,
    )

    qkv_new = qkv_update(qkv_sum, (qkv_master, qkv_moment, qkv_average), step_rate)
    input_grad = first_norm_reverse(
        done_sum,
        dresid,
        tokens,
        norms,
    )
    digits = out_new[16][side_columns + 2 : side_columns + 2 + 4 * expert_count, 0]
    digits = jnp.sum(digits.reshape(expert_count, 4) * jnp.asarray([1.0, 8.0, 64.0, 512.0]), 1)
    expert_counts = (digits / narrow_count + 0.5).astype(jnp.int32)
    block_out = (resid + sum(part.astype(F32) for part in mlp_sum)).astype(BF16)
    results = [block_out, input_grad, expert_counts]
    for group in (out_new[12:16], qkv_new, out_new[0:4], hidden_new, out_new[4:12]):
        results.extend(group)
    results.extend(expert_new)
    return tuple(results)


def solution(mesh):
    in_specs = (
        P(("wide", "narrow"), None),
        P(("wide", "narrow"), None),
        P("wide"),
        P("wide", None),
        P(),
        P(None, None, "narrow"),
        P("narrow", None),
        P(None, "narrow"),
        P("narrow", None),
        P(),
        P(),
        P(None, "wide"),
        P(None, "wide"),
        P(None, "wide"),
        P(None, "wide", "narrow"),
        P(None, "wide", "narrow"),
        P(None, "wide", "narrow"),
        P("narrow", "wide"),
        P("narrow", "wide"),
        P("narrow", "wide"),
        P("wide", "narrow"),
        P("wide", "narrow"),
        P("wide", "narrow"),
        P("narrow", "wide"),
        P("narrow", "wide"),
        P("narrow", "wide"),
        P("wide", None),
        P("wide", None),
        P("wide", None),
        P("wide", None),
        P("wide", None),
        P("wide", None),
        P("wide", None, "narrow"),
        P("wide", None, "narrow"),
        P("wide", None, "narrow"),
        P("wide", "narrow", None),
        P("wide", "narrow", None),
        P("wide", "narrow", None),
    )
    out_specs = (
        P(("wide", "narrow"), None),
        P(("wide", "narrow"), None),
        P(),
        P(None, "wide"),
        P(None, "wide"),
        P(None, "wide"),
        P(None, "wide"),
        P(None, "wide", "narrow"),
        P(None, "wide", "narrow"),
        P(None, "wide", "narrow"),
        P(None, "wide", "narrow"),
        P("narrow", "wide"),
        P("narrow", "wide"),
        P("narrow", "wide"),
        P("narrow", "wide"),
        P("wide", "narrow"),
        P("wide", "narrow"),
        P("wide", "narrow"),
        P("wide", "narrow"),
        P("narrow", "wide"),
        P("narrow", "wide"),
        P("narrow", "wide"),
        P("narrow", "wide"),
        P("wide", None),
        P("wide", None),
        P("wide", None),
        P("wide", None),
        P("wide", None),
        P("wide", None),
        P("wide", None),
        P("wide", None),
        P("wide", None, "narrow"),
        P("wide", None, "narrow"),
        P("wide", None, "narrow"),
        P("wide", None, "narrow"),
        P("wide", "narrow", None),
        P("wide", "narrow", None),
        P("wide", "narrow", None),
        P("wide", "narrow", None),
    )
    return jax.shard_map(
        on_device, mesh=mesh, in_specs=in_specs, out_specs=out_specs, check_vma=False
    )
```

```python
import functools
import math

import jax
import jax.numpy as jnp
from jax import lax
from jax.experimental import pallas as pl
from jax.experimental.pallas import tpu as pltpu
from jax.sharding import PartitionSpec as P

HEAD_DIM = 64
F32 = jnp.float32
BF16 = jnp.bfloat16

precise = lax.Precision.HIGHEST
eps_norm = 1e-05
momentum_decay = 0.9
average_decay = 0.75
rate_base = 0.05
expert_down_boost = 12.0
neg_large = -1e30
lane_pad = 128


def dot_nn(a, b):
    return jnp.dot(a, b, preferred_element_type=F32)


def dot_nt(a, b):
    return lax.dot_general(a, b, (((1,), (1,)), ((), ())), preferred_element_type=F32)


def dot_tn(a, b):
    return lax.dot_general(a, b, (((0,), (0,)), ((), ())), preferred_element_type=F32)


def normalize(values):
    mean_val = jnp.mean(values, -1, keepdims=True)
    centered = values - mean_val
    inverse = lax.rsqrt(jnp.mean(centered * centered, -1, keepdims=True) + eps_norm)
    return (centered * inverse, inverse)


def layer_norm_reverse(upstream, normed, inverse, gain):
    scaled = upstream * gain
    return inverse * (
        scaled
        - jnp.mean(scaled, -1, keepdims=True)
        - normed * jnp.mean(scaled * normed, -1, keepdims=True)
    )


def gelu_pair(pre):
    root = math.sqrt(2.0 / math.pi)
    square = pre * pre
    half = 0.5 + 0.5 * jnp.tanh(pre * (root + (root * 0.044715) * square))
    hid = pre * half
    slope = half + hid * (1.0 - half) * (2.0 * root + (root * 0.26829) * square)
    return (hid, slope)


def attend_masks(length, keys, chunk):
    key_at = lax.broadcasted_iota(jnp.int32, (keys, 1), 0)
    bias = jnp.where(key_at < length, 0.0, neg_large).astype(F32)
    below = lax.broadcasted_iota(jnp.int32, (chunk, chunk), 0)
    across = lax.broadcasted_iota(jnp.int32, (chunk, chunk), 1)
    return (bias, below <= across)


def masked_scores(key, query, bias, causal, chunk):
    scores = dot_nt(key, query) + bias
    edge = jnp.where(causal, scores[-chunk:], neg_large)
    if scores.shape[0] == chunk:
        return edge
    return jnp.concatenate([scores[:-chunk], edge], 0)


VMEM = pl.BlockSpec(memory_space=pltpu.VMEM)
SMEM = pl.BlockSpec(memory_space=pltpu.SMEM)
MIB = 2**20
LIMITS = {"project": 12, "attend_forward": 16, "join": 20, "pack_expert": 12, "second_norm_reverse": 12, "attend_backward": 60, "qkv_grad": 60, "first_norm_reverse": 10, "owner_grad": 44, "hidden_update": 60, "out_update": 8, "qkv_update": 8}


def shape_of(shape, dtype=BF16):
    return jax.ShapeDtypeStruct(shape, dtype)


def cost(micros):
    return pl.CostEstimate(flops=int(micros * 1e5), bytes_accessed=1024, transcendentals=0)


def local_call(kernel, name, outs, in_specs, micros, scratch=()):
    return pl.pallas_call(
        kernel,
        out_shape=outs,
        in_specs=in_specs,
        out_specs=jax.tree.map(lambda _: VMEM, outs),
        scratch_shapes=list(scratch),
        compiler_params=pltpu.CompilerParams(vmem_limit_bytes=LIMITS[name] * MIB),
        cost_estimate=cost(micros),
        name=name,
    )


def project_kernel(tok_ref, norms_ref, weight_ref, act_ref, qkv_ref):
    hat, _ = normalize(tok_ref[...].astype(F32))
    act = (hat * norms_ref[0:1, :] + norms_ref[1:2, :]).astype(BF16)
    act_ref[...] = act
    width = weight_ref.shape[2]
    for c in range(3):
        qkv_ref[:, c * width : (c + 1) * width] = dot_nn(act, weight_ref[c]).astype(BF16)


def project(tok, norms, weight):
    rows, width = tok.shape
    columns = 3 * weight.shape[2]
    return local_call(
        project_kernel,
        "project",
        (shape_of((rows, width)), shape_of((rows, columns))),
        [VMEM] * 3,
        2,
    )(tok, norms, weight)


def place_rows(place_ref, pieces, full_ref):
    rows = pieces[0].shape[0]
    for m, piece in enumerate(pieces):
        at = pl.multiple_of(place_ref[m] * rows, rows)
        full_ref[pl.ds(at, rows), :] = piece[...]


def attend_forward_kernel(place_ref, length_ref, *refs, count, chunk):
    pieces, (heads_ref, sums_ref, qkv_ref) = refs[:count], refs[count:]
    place_rows(place_ref, pieces, qkv_ref)
    rows = qkv_ref.shape[0]
    width = qkv_ref.shape[1] // 3
    scale = jnp.asarray(HEAD_DIM**-0.5, BF16)
    for block in range(rows // chunk):
        at, keys = block * chunk, (block + 1) * chunk
        bias, causal = attend_masks(length_ref[0], keys, chunk)
        outs = []
        for head in range(width // HEAD_DIM):
            col = head * HEAD_DIM
            query = qkv_ref[at:keys, col : col + HEAD_DIM] * scale
            key = qkv_ref[0:keys, width + col : width + col + HEAD_DIM]
            value = qkv_ref[0:keys, 2 * width + col : 2 * width + col + HEAD_DIM]
            scores = masked_scores(key, query, bias, causal, chunk)
            top = jnp.max(scores, 0, keepdims=True)
            expo = jnp.exp(scores - top)
            total = jnp.sum(expo, 0, keepdims=True)
            soft = (expo * (1.0 / total)).astype(BF16)
            outs.append(dot_tn(value, soft))
            sums_ref[head : head + 1, at:keys] = top + jnp.log(total)
        heads_ref[at:keys, :] = jnp.concatenate(outs, 0).T.astype(BF16)


def attend_forward(place, length, pieces):
    count = len(pieces)
    rows = pieces[0].shape[0] * count
    width = pieces[0].shape[1] // 3
    heads = width // HEAD_DIM
    return local_call(
        functools.partial(attend_forward_kernel, count=count, chunk=min(256, rows)),
        "attend_forward",
        (shape_of((rows, width)), shape_of((heads, rows), F32), shape_of((rows, 3 * width))),
        [SMEM, SMEM] + [VMEM] * count,
        11,
    )(place, length, *pieces)


def join_kernel(place_ref, *refs, count):
    heads, toks = refs[:count], refs[count : 2 * count]
    out_ref, norms_ref, act_ref, resid_ref = refs[2 * count :]
    rows = toks[0].shape[0]
    for m in range(count):
        at = pl.multiple_of(place_ref[m] * rows, rows)
        total = toks[m][...].astype(F32)
        for j in range(count):
            total = total + dot_nn(heads[j][pl.ds(at, rows), :], out_ref[j])
        if m == 0:
            resid_ref[...] = total
        hat, _ = normalize(total)
        act = hat * norms_ref[2:3, :] + norms_ref[3:4, :]
        act_ref[m * rows : (m + 1) * rows, :] = act.astype(BF16)


def join(place, heads, toks, out_all, norms):
    count = len(heads)
    rows, width = toks[0].shape
    return local_call(
        functools.partial(join_kernel, count=count),
        "join",
        (shape_of((rows * count, width)), shape_of((rows, width), F32)),
        [SMEM] + [VMEM] * (2 * count + 2),
        6,
    )(place, *heads, *toks, out_all, norms)


def fixed(shape):
    return pl.BlockSpec(shape, lambda e: (0,) * len(shape), pipeline_mode=pl.Buffered(1))


def one_hot_block(slot_ref, at, rows):
    index = lax.broadcasted_iota(jnp.int32, (rows, slot_ref.shape[1]), 0) + at
    return jnp.where(index == slot_ref[...], 1.0, 0.0).astype(BF16)


def unsort(hot_ref, sorted_ref, outs):
    rows = outs[0].shape[0]
    for m, out in enumerate(outs):
        out[...] = dot_tn(hot_ref[:, m * rows : (m + 1) * rows], sorted_ref[...]).astype(BF16)


def pack_kernel(up_ref, down_ref, *refs):
    rest, out_ref = refs[:-1], refs[-1]
    units = down_ref.shape[0]
    out_ref[0:units, :] = up_ref[...].T.astype(BF16)
    out_ref[units : 2 * units, :] = down_ref[...].astype(BF16)
    out_ref[2 * units :, :] = jnp.concatenate([piece[...] for piece in rest], 0)


def pack_expert(up, down, rest):
    units, width = down.shape
    rows = 2 * units + sum(piece.shape[0] for piece in rest)
    return local_call(
        pack_kernel, "pack_expert", shape_of((rows, width)), [VMEM] * (2 + len(rest)), 3
    )(up, down, *rest)


def sorted_cot_kernel(slot_ref, *refs, count):
    cots, (down_ref, cot_ref, back_ref) = refs[:count], refs[count:]
    rows = cots[0].shape[0]
    capacity = cot_ref.shape[0]
    hot = one_hot_block(slot_ref, pl.program_id(0) * capacity, capacity)
    cot = sum(dot_nn(hot[:, m * rows : (m + 1) * rows], cots[m][...]) for m in range(count))
    cot = cot.astype(BF16)
    cot_ref[...] = cot
    back_ref[...] = dot_nt(cot, down_ref[...]).astype(BF16)


def sorted_cot(slot_row, cots, down):
    count = len(cots)
    rows, width = cots[0].shape
    total = rows * count
    hidden = down.shape[0]
    block_rows = min(256, rows)
    return pl.pallas_call(
        functools.partial(sorted_cot_kernel, count=count),
        grid=(total // block_rows,),
        in_specs=[fixed(slot_row.shape)] + [fixed((rows, width))] * count + [fixed(down.shape)],
        out_specs=[
            pl.BlockSpec((block_rows, width), lambda e: (e, 0)),
            pl.BlockSpec((block_rows, hidden), lambda e: (e, 0)),
        ],
        out_shape=[shape_of((total, width)), shape_of((total, hidden))],
        compiler_params=pltpu.CompilerParams(vmem_limit_bytes=16 * MIB),
        cost_estimate=cost(8),
        name="sorted_cot",
    )(slot_row, *cots, down)


def expert_back_kernel(cot_ref, pack_ref, back_ref):
    units = pack_ref.shape[1]
    for p in range(2):
        back_ref[:, p * units : (p + 1) * units] = dot_nt(cot_ref[...], pack_ref[p]).astype(BF16)


def expert_back(cot, pack, units):
    total, width = cot.shape
    experts = pack.shape[0] // 2
    capacity = total // experts
    return pl.pallas_call(
        expert_back_kernel,
        grid=(experts,),
        in_specs=[
            pl.BlockSpec((capacity, width), lambda e: (e, 0)),
            pl.BlockSpec((2, units, width), lambda e: (e, 1, 0)),
        ],
        out_specs=pl.BlockSpec((capacity, 2 * units), lambda e: (e, 0)),
        out_shape=shape_of((total, 2 * units)),
        compiler_params=pltpu.CompilerParams(vmem_limit_bytes=47 * MIB),
        cost_estimate=cost(4),
        name="expert_back",
    )(cot, pack)


def route_kernel(counts_ref, slot_ref, act_ref, side_ref, sorted_ref, table_ref, *, experts):
    expert = pl.program_id(0)
    capacity, lanes = table_ref.shape
    width = act_ref.shape[1]
    hot = one_hot_block(slot_ref, expert * capacity, capacity)
    act = dot_nn(hot, act_ref[...]).astype(BF16)
    lane = lax.broadcasted_iota(jnp.int32, (capacity, lanes), 1)

    def pick(values, index):
        return jnp.sum(jnp.where(lane == index, values, 0.0), -1, keepdims=True)

    def soft(values, inside):
        values = jnp.where(inside, values, neg_large)
        expo = jnp.exp(values - jnp.max(values, -1, keepdims=True))
        return expo / jnp.sum(expo, -1, keepdims=True)

    logits = dot_nn(act, side_ref[...])
    probs = soft(logits, lane < experts)
    coef = soft(logits, (lane >= experts) & (lane < experts + 2))
    gate = pick(probs, expert)
    coef0, coef1 = pick(coef, experts), pick(coef, experts + 1)
    live = jnp.where(
        lax.broadcasted_iota(jnp.int32, (capacity, 1), 0) < counts_ref[expert], 1.0, 0.0
    )
    scale = live * gate * coef1
    table = jnp.where(lane < experts, probs, 0.0)
    for at, column in enumerate((coef0, coef1, gate, live, scale)):
        table = jnp.where(lane == experts + at, column, table)
    table_ref[...] = table
    high = scale.astype(BF16).astype(F32)
    sorted_ref[:, :width] = act
    sorted_ref[:, width:] = jnp.where(
        lane == 0, high, jnp.where(lane == 1, scale - high, 0.0)
    ).astype(BF16)


def route(counts, slot_row, act, side, experts):
    total, width = act.shape
    capacity = total // experts
    lanes = side.shape[1]
    return pl.pallas_call(
        functools.partial(route_kernel, experts=experts),
        grid=(experts,),
        in_specs=[SMEM, fixed(slot_row.shape), fixed(act.shape), fixed(side.shape)],
        out_specs=[
            pl.BlockSpec((capacity, width + lanes), lambda e: (e, 0)),
            pl.BlockSpec((capacity, lanes), lambda e: (e, 0)),
        ],
        out_shape=[shape_of((total, width + lanes)), shape_of((total, lanes), F32)],
        compiler_params=pltpu.CompilerParams(vmem_limit_bytes=12 * MIB),
        cost_estimate=cost(4),
        name="route",
    )(counts, slot_row, act, side)


def mixture_kernel(
    slot_ref, act_ref, table_ref, back_ref, eback_ref, up_ref, pack_ref, side_ref, *refs,
    count, experts
):
    parts, refs = refs[:count], refs[count:]
    dpre_ref, hid_ref, ehid_ref, dside_ref, hot_ref, dact_ref = refs
    expert = pl.program_id(0)
    capacity, width = dpre_ref.shape[0], dact_ref.shape[1]
    at = pl.multiple_of(expert * capacity, capacity)
    hot_ref[pl.ds(at, capacity), :] = one_hot_block(slot_ref, at, capacity)
    act = act_ref[:, :width]
    table = table_ref[...]
    coef0, coef1, gate, live, scale = (
        table[:, experts + j : experts + j + 1] for j in range(5)
    )
    pre = dot_nn(act, up_ref[...])
    back = back_ref[...].astype(F32)
    hid, slope = gelu_pair(pre)
    dense_dot = jnp.sum(hid * back, -1, keepdims=True)
    dpre = (slope * (coef0 * back)).astype(BF16)
    hid_ref[...] = (coef0 * hid).astype(BF16)
    dpre_ref[...] = dpre
    dact = dot_nt(dpre, up_ref[...])
    expert_dot = jnp.zeros_like(dense_dot)
    units = pack_ref.shape[1]
    for p in range(2):
        here = slice(p * units, (p + 1) * units)
        pre = dot_nt(act, pack_ref[p])
        back = eback_ref[:, here].astype(F32)
        hid, slope = gelu_pair(pre)
        expert_dot = expert_dot + jnp.sum(hid * back, -1, keepdims=True)
        ehid_ref[:, here] = (scale * hid).astype(BF16)
        dact = dact + dot_nn((slope * (scale * back)).astype(BF16), pack_ref[p])
    expert_dot = live * expert_dot
    mean = coef0 * dense_dot + coef1 * gate * expert_dot
    dgate = coef1 * expert_dot
    lane = lax.broadcasted_iota(jnp.int32, table.shape, 1)
    dside = jnp.where(
        lane < experts, table * (jnp.where(lane == expert, dgate, 0.0) - gate * dgate), 0.0
    )
    dside = jnp.where(lane == experts, coef0 * (dense_dot - mean), dside)
    dside = jnp.where(lane == experts + 1, coef1 * (gate * expert_dot - mean), dside)
    high = dside.astype(BF16)
    rest = (dside - high.astype(F32)).astype(BF16)
    dside_ref[...] = high
    dact = dact + dot_nt(high, side_ref[...]) + dot_nt(rest, side_ref[...])
    dact_ref[pl.ds(at, capacity), :] = dact.astype(BF16)

    @pl.when(expert == pl.num_programs(0) - 1)
    def _():
        unsort(hot_ref, dact_ref, parts)


def mixture(slot_row, act, table, back, eback, up, pack, side, count):
    total, hidden = back.shape
    width = up.shape[0]
    rows = total // count
    experts, units = pack.shape[0] // 2, eback.shape[1] // 2
    capacity = total // experts
    lanes = side.shape[1]

    def block(columns):
        return pl.BlockSpec((capacity, columns), lambda e: (e, 0))

    return pl.pallas_call(
        functools.partial(mixture_kernel, count=count, experts=experts),
        grid=(experts,),
        in_specs=[
            fixed(slot_row.shape),
            block(width + lanes),
            block(lanes),
            block(hidden),
            block(2 * units),
            fixed(up.shape),
            pl.BlockSpec((2, units, width), lambda e: (e, 0, 0)),
            fixed(side.shape),
        ],
        out_specs=[fixed((rows, width))] * count
        + [block(hidden), block(hidden), block(2 * units), block(lanes)],
        out_shape=[shape_of((rows, width))] * count
        + [
            shape_of((total, hidden)),
            shape_of((total, hidden)),
            shape_of((total, 2 * units)),
            shape_of((total, lanes)),
        ],
        scratch_shapes=[pltpu.VMEM((total, total), BF16), pltpu.VMEM((total, width), BF16)],
        compiler_params=pltpu.CompilerParams(vmem_limit_bytes=52 * MIB),
        cost_estimate=cost(18),
        name="mixture",
    )(slot_row, act, table, back, eback, up, pack, side)


def output_kernel(slot_ref, hid_ref, ehid_ref, down_ref, pack_ref, *refs):
    parts, (hot_ref, sorted_ref) = refs[:-2], refs[-2:]
    expert = pl.program_id(0)
    capacity = hid_ref.shape[0]
    units = pack_ref.shape[1]
    at = pl.multiple_of(expert * capacity, capacity)
    hot_ref[pl.ds(at, capacity), :] = one_hot_block(slot_ref, at, capacity)
    dense = dot_nn(hid_ref[...], down_ref[...])
    routed = dot_nn(ehid_ref[:, :units], pack_ref[0]) + dot_nn(ehid_ref[:, units:], pack_ref[1])
    mixed = dense + routed
    sorted_ref[pl.ds(at, capacity), :] = mixed.astype(BF16)

    @pl.when(expert == pl.num_programs(0) - 1)
    def _():
        unsort(hot_ref, sorted_ref, parts)


def mixture_output(slot_row, hid, ehid, down, pack, count):
    total, hidden = hid.shape
    width = down.shape[1]
    experts, units = pack.shape[0] // 2, ehid.shape[1] // 2
    capacity = total // experts
    rows = total // count

    def block(columns):
        return pl.BlockSpec((capacity, columns), lambda e: (e, 0))

    return pl.pallas_call(
        output_kernel,
        grid=(experts,),
        in_specs=[
            fixed(slot_row.shape),
            block(hidden),
            block(2 * units),
            fixed(down.shape),
            pl.BlockSpec((2, units, width), lambda e: (e, 1, 0)),
        ],
        out_specs=[fixed((rows, width))] * count,
        out_shape=[shape_of((rows, width))] * count,
        scratch_shapes=[pltpu.VMEM((total, total), BF16), pltpu.VMEM((total, width), BF16)],
        compiler_params=pltpu.CompilerParams(vmem_limit_bytes=52 * MIB),
        cost_estimate=cost(10),
        name="mixture_output",
    )(slot_row, hid, ehid, down, pack)


def second_norm_kernel(*refs, got, count):
    parts, refs = refs[:got], refs[got:]
    resid_ref, cot_ref, norms_ref, out_ref = refs[:4]
    dresid_ref, low_ref, sums_ref = refs[4:7]
    dheads = refs[7:]
    upstream = sum(part[...].astype(F32) for part in parts)
    hat, inverse = normalize(resid_ref[...])
    sums_ref[...] = jnp.zeros_like(sums_ref)
    sums_ref[0:1, :] = jnp.sum(upstream * hat, 0, keepdims=True)
    sums_ref[1:2, :] = jnp.sum(upstream, 0, keepdims=True)
    dresid = cot_ref[...].astype(F32) + layer_norm_reverse(
        upstream, hat, inverse, norms_ref[2:3, :]
    )
    dresid_ref[...] = dresid
    low = dresid.astype(BF16)
    low_ref[...] = low
    for j in range(count):
        dheads[j][...] = dot_nt(low, out_ref[j]).astype(BF16)


def second_norm_reverse(parts, resid, cot, norms, out_all):
    rows, width = resid.shape
    count, head_width, _ = out_all.shape
    return local_call(
        functools.partial(second_norm_kernel, got=len(parts), count=count),
        "second_norm_reverse",
        [
            shape_of((rows, width), F32),
            shape_of((rows, width)),
            shape_of((8, width), F32),
        ]
        + [shape_of((rows, head_width))] * count,
        [VMEM] * (len(parts) + 4),
        3,
    )(*parts, resid, cot, norms, out_all)


def attend_backward_kernel(place_ref, length_ref, *refs, count, chunk):
    cots, refs = refs[:count], refs[count:]
    qkv_ref, lse_ref, weight_ref, out_ref = refs[:4]
    parts, (cot_ref, dk_ref, dv_ref, dqkv_ref) = refs[4 : 4 + count], refs[4 + count :]
    place_rows(place_ref, cots, cot_ref)
    rows = qkv_ref.shape[0]
    width = qkv_ref.shape[1] // 3
    scale = jnp.asarray(HEAD_DIM**-0.5, BF16)
    blocks = rows // chunk
    for block in range(blocks):
        at, keys = block * chunk, (block + 1) * chunk
        bias, causal = attend_masks(length_ref[0], keys, chunk)
        outs = []
        for head in range(width // HEAD_DIM):
            col = head * HEAD_DIM
            query = qkv_ref[at:keys, col : col + HEAD_DIM] * scale
            key = qkv_ref[0:keys, width + col : width + col + HEAD_DIM]
            value = qkv_ref[0:keys, 2 * width + col : 2 * width + col + HEAD_DIM]
            cot = cot_ref[at:keys, col : col + HEAD_DIM]
            scores = masked_scores(key, query, bias, causal, chunk)
            prob = jnp.exp(scores - lse_ref[head : head + 1, at:keys])
            dprob = dot_nt(value, cot)
            delta = jnp.sum(prob * dprob, 0, keepdims=True)
            dscore = (prob * (dprob - delta)).astype(BF16)
            dvalue = dot_nn(prob.astype(BF16), cot)
            dkey = dot_nn(dscore, query)
            outs.append(dot_tn(key * scale, dscore))
            here = slice(col, col + HEAD_DIM)
            if block > 0:
                dv_ref[0:at, here] += dvalue[:at]
                dk_ref[0:at, here] += dkey[:at]
            dv_ref[at:keys, here] = dvalue[at:]
            dk_ref[at:keys, here] = dkey[at:]
        dqkv_ref[at:keys, 0:width] = jnp.concatenate(outs, 0).T.astype(BF16)
    dqkv_ref[:, width : 2 * width] = dk_ref[...].astype(BF16)
    dqkv_ref[:, 2 * width : 3 * width] = dv_ref[...].astype(BF16)
    part_rows = parts[0].shape[0]
    for m in reversed(range(count)):
        at = pl.multiple_of(place_ref[m] * part_rows, part_rows)
        mine = dqkv_ref[pl.ds(at, part_rows), :]
        out_ref[m * part_rows : (m + 1) * part_rows, :] = mine
        total = sum(
            dot_nt(mine[:, c * width : (c + 1) * width], weight_ref[c]) for c in range(3)
        )
        parts[m][...] = total.astype(BF16)


def attend_backward(place, length, qkv, cots, lse, weight):
    count = len(cots)
    rows, wide3 = qkv.shape
    part_rows, width = rows // count, wide3 // 3
    heads = width // HEAD_DIM
    model = weight.shape[1]
    return local_call(
        functools.partial(attend_backward_kernel, count=count, chunk=min(256, rows)),
        "attend_backward",
        [shape_of((rows, wide3))] + [shape_of((part_rows, model))] * count,
        [SMEM, SMEM] + [VMEM] * (count + 3),
        12,
        [
            pltpu.VMEM((rows, width), BF16),
            pltpu.VMEM((rows, width), F32),
            pltpu.VMEM((rows, width), F32),
            pltpu.VMEM((rows, wide3), BF16),
        ],
    )(place, length, *cots, qkv, lse, weight)


def qkv_grad_kernel(owner_ref, *refs, count):
    acts, dones, toks = refs[:count], refs[count : 2 * count], refs[2 * count : 3 * count]
    dqkv_ref, even_ref, odd_ref, total_ref = refs[3 * count :]
    columns = dqkv_ref.shape[1]
    rows, width = acts[0].shape
    tile = min(256, width)
    for at in range(0, width, tile):
        total = sum(
            dot_tn(acts[m][:, at : at + tile], dqkv_ref[m * rows : (m + 1) * rows, :])
            for m in range(count)
        )
        total_ref[at : at + tile, :columns] = total.astype(BF16)
    first, second = 0.0, 0.0
    for m in range(count):
        hat, _ = normalize(toks[m][...].astype(F32))
        upstream = dones[m][...].astype(F32)
        first = first + jnp.sum(upstream * hat, 0, keepdims=True)
        second = second + jnp.sum(upstream, 0, keepdims=True)
    sums = jnp.concatenate([jnp.zeros((lane_pad - 2, width), F32), first, second], 0)
    total_ref[:, columns:] = sums.T.astype(BF16)
    owned = even_ref.shape[1]
    for m in range(2 * even_ref.shape[0]):
        at = pl.multiple_of(owner_ref[m] * owned, owned)
        (odd_ref if m % 2 else even_ref)[m // 2] = total_ref[pl.ds(at, owned), :]


def qkv_grad(owner, acts, dones, toks, dqkv):
    count = len(acts)
    width = acts[0].shape[1]
    columns = dqkv.shape[1] + lane_pad
    owners = owner.shape[0]
    half = shape_of((owners // 2, width // owners, columns))
    return local_call(
        functools.partial(qkv_grad_kernel, count=count),
        "qkv_grad",
        [half, half],
        [SMEM] + [VMEM] * (3 * count + 1),
        6,
        [pltpu.VMEM((width, columns), BF16)],
    )(owner, *acts, *dones, *toks, dqkv)


def first_norm_kernel(*refs, got):
    parts, (dresid_ref, tok_ref, norms_ref, out_ref) = refs[:got], refs[got:]
    upstream = sum(part[...].astype(F32) for part in parts)
    hat, inverse = normalize(tok_ref[...].astype(F32))
    out_ref[...] = dresid_ref[...] + layer_norm_reverse(
        upstream, hat, inverse, norms_ref[0:1, :]
    )


def first_norm_reverse(parts, dresid, tok, norms):
    rows, width = tok.shape
    return local_call(
        functools.partial(first_norm_kernel, got=len(parts)),
        "first_norm_reverse",
        shape_of((rows, width), F32),
        [VMEM] * (len(parts) + 3),
        2,
    )(*parts, dresid, tok, norms)


def dense_grad_kernel(act_ref, cot_ref, dpre_ref, hid_ref, out_ref):
    hidden = hid_ref.shape[1]
    out_ref[:, :hidden] = dot_tn(act_ref[...], dpre_ref[...]).astype(BF16)
    out_ref[:, hidden:] = dot_tn(cot_ref[...], hid_ref[...]).astype(BF16)


def columns_of(rows, tile):
    return pl.BlockSpec((rows, tile), lambda i: (0, i))


def dense_grad(act, cot, dpre, hid, columns):
    total, width = cot.shape
    tile = min(256, width)
    return pl.pallas_call(
        dense_grad_kernel,
        grid=(width // tile,),
        in_specs=[
            columns_of(total, tile),
            columns_of(total, tile),
            fixed(dpre.shape),
            fixed(hid.shape),
        ],
        out_specs=pl.BlockSpec((tile, 2 * hid.shape[1]), lambda i: (i, 0)),
        out_shape=pltpu.HBM((width, columns), BF16),
        compiler_params=pltpu.CompilerParams(vmem_limit_bytes=24 * MIB),
        cost_estimate=cost(7),
        name="dense_grad",
    )(act, cot, dpre, hid)


def out_grad_kernel(place_ref, *refs, count):
    heads, (low_ref, _, out_ref) = refs[:count], refs[count:]
    rows = low_ref.shape[0]
    head_width = heads[0].shape[1]
    at = pl.multiple_of(place_ref[0] * rows, rows)
    low = low_ref[...]
    for j in range(count):
        part = dot_tn(low, heads[j][pl.ds(at, rows), :])
        out_ref[:, j * head_width : (j + 1) * head_width] = part.astype(BF16)


def out_grad(place, heads, low, shared, at):
    count = len(heads)
    rows, width = low.shape
    columns = count * heads[0].shape[1]
    tile = min(256, width)
    return pl.pallas_call(
        functools.partial(out_grad_kernel, count=count),
        grid=(width // tile,),
        in_specs=[SMEM]
        + [fixed(h.shape) for h in heads]
        + [columns_of(rows, tile), pl.BlockSpec(memory_space=pl.ANY)],
        out_specs=pl.BlockSpec((tile, columns), lambda i: (i, at // columns)),
        out_shape=pltpu.HBM(shared.shape, BF16),
        input_output_aliases={count + 2: 0},
        compiler_params=pltpu.CompilerParams(vmem_limit_bytes=16 * MIB),
        cost_estimate=cost(3),
        name="out_grad",
    )(place, *heads, low, shared)


def side_grad_kernel(totals_ref, act_ref, sums_ref, dside_ref, _, out_ref, *, side):
    small = dot_tn(act_ref[...], dside_ref[...])
    tile = small.shape[0]
    lane = lax.broadcasted_iota(jnp.int32, small.shape, 1)
    sums = jnp.concatenate([sums_ref[...], jnp.zeros((lane_pad - 8, tile), F32)], 0).T
    small = jnp.where(lane == side, sums[:, 0:1], small)
    small = jnp.where(lane == side + 1, sums[:, 1:2], small)
    digit = lax.broadcasted_iota(jnp.int32, (8, lane_pad), 1) - (side + 2)
    row = jnp.zeros((8, lane_pad), F32)
    for e in range(side - 2):
        for d in range(4):
            value = lax.shift_right_logical(totals_ref[e], 3 * d) & 7
            row = jnp.where(digit == 4 * e + d, value.astype(F32), row)
    out_ref[...] = (small + row[0:1, :]).astype(BF16)


def side_grad(totals, act, sums, dside, shared, at, side):
    width = sums.shape[1]
    tile = min(256, width)
    return pl.pallas_call(
        functools.partial(side_grad_kernel, side=side),
        grid=(width // tile,),
        in_specs=[SMEM, columns_of(act.shape[0], tile), columns_of(8, tile), fixed(dside.shape)]
        + [pl.BlockSpec(memory_space=pl.ANY)],
        out_specs=pl.BlockSpec((tile, lane_pad), lambda i: (i, at // lane_pad)),
        out_shape=pltpu.HBM(shared.shape, BF16),
        input_output_aliases={4: 0},
        compiler_params=pltpu.CompilerParams(vmem_limit_bytes=16 * MIB),
        cost_estimate=cost(2),
        name="side_grad",
    )(totals, act, sums, dside, shared)


def owner_kernel(at_ref, *refs):
    count = (len(refs) - 5) // 2
    acts, cots = refs[:count], refs[count : 2 * count]
    pack_ref, dup_other, ddown_other, dup_mine, ddown_mine = refs[2 * count :]
    units, width = pack_ref.shape[1] // 2, pack_ref.shape[2]
    act = jnp.concatenate([block[:, :width] for block in acts], 0)
    scale = jnp.concatenate([block[:, width:] for block in acts], 0)
    scale = scale[:, 0:1].astype(F32) + scale[:, 1:2].astype(F32)
    cot = jnp.concatenate([block[...] for block in cots], 0)
    cot = (scale * cot.astype(F32)).astype(BF16)
    hid, slope = gelu_pair(dot_nt(act, pack_ref[0, 0:units, :]))
    dpre = (slope * dot_nt(cot, pack_ref[0, units : 2 * units, :])).astype(BF16)
    dup = dot_tn(act, dpre)
    ddown = dot_tn(hid.astype(BF16), cot)

    @pl.when(pl.program_id(0) == 0)
    def _():
        dup_other[...] = dup.astype(BF16)
        ddown_other[...] = ddown.astype(BF16)

    @pl.when(pl.program_id(0) == 1)
    def _():
        dup_mine[...] = dup
        ddown_mine[...] = ddown


def owner_grad(at, acts, cots, pack, units):
    width = pack.shape[2]
    up, down = (width, units), (units, width)

    def same(shape):
        return pl.BlockSpec(
            shape, lambda q, at: (0,) * len(shape), pipeline_mode=pl.Buffered(1)
        )

    return pl.pallas_call(
        owner_kernel,
        grid_spec=pltpu.PrefetchScalarGridSpec(
            num_scalar_prefetch=1,
            grid=(2,),
            in_specs=[same(block.shape) for block in (*acts, *cots)]
            + [pl.BlockSpec((1, 2 * units, width), lambda q, at: (at[q], 0, 0))],
            out_specs=[same(up), same(down), same(up), same(down)],
        ),
        out_shape=[shape_of(up), shape_of(down), shape_of(up, F32), shape_of(down, F32)],
        compiler_params=pltpu.CompilerParams(vmem_limit_bytes=40 * MIB),
        cost_estimate=cost(16),
        name="owner_grad",
    )(at, *acts, *cots, pack)


def update_into(outs, gradient, state, rate):
    master, moment, average = (ref[...] for ref in state)
    new_moment = momentum_decay * moment + gradient
    new_master = master - rate * (gradient + momentum_decay * new_moment)
    outs[0][...] = gradient
    outs[1][...] = new_master
    outs[2][...] = new_moment
    outs[3][...] = average_decay * average + (1.0 - average_decay) * new_master


def four(states):
    return [shape_of(state.shape, F32) for group in states for state in (group[0],) * 4]


def hidden_update_kernel(grad_ref, *refs, rate):
    hidden = refs[0].shape[1]
    grad = grad_ref[...].astype(F32)
    update_into(refs[6:10], grad[:, :hidden], refs[0:3], rate)
    update_into(refs[10:14], grad[:, hidden : 2 * hidden].T, refs[3:6], rate)


def hidden_update(grad, states, rate):
    return local_call(
        functools.partial(hidden_update_kernel, rate=rate),
        "hidden_update",
        four(states),
        [VMEM] * 7,
        4,
    )(grad, *states[0], *states[1])


def out_update_kernel(*refs, got, side, rate):
    parts, refs = refs[:got], refs[got:]
    total = sum(part[...].astype(F32) for part in parts)
    width = refs[0].shape[0]
    outs = refs[12:]
    update_into(outs[0:4], total[:, :width].T, refs[0:3], rate)
    small = total[:, width:].T
    update_into(outs[4:8], small[: side - 2], refs[3:6], rate)
    update_into(outs[8:12], small[side - 2 : side], refs[6:9], rate)
    norm = jnp.concatenate([small[lane_pad - 2 :], small[side : side + 2]], 0)
    update_into(outs[12:16], norm, refs[9:12], rate)
    outs[16][...] = small


def out_update(parts, states, side, rate):
    turned = [tuple(v.T for v in group) for group in states[1:3]]
    states = (states[0], *turned, states[3])
    made = local_call(
        functools.partial(out_update_kernel, got=len(parts), side=side, rate=rate),
        "out_update",
        four(states) + [shape_of((lane_pad, parts[0].shape[0]), F32)],
        [VMEM] * (len(parts) + 12),
        2,
    )(*parts, *states[0], *states[1], *states[2], *states[3])
    return list(made[:4]) + [v.T for v in made[4:12]] + list(made[12:])


def qkv_update_kernel(*refs, got, rate):
    parts, refs = refs[:got], refs[got:]
    qkv, outs = refs[0:3], refs[3:]
    total = sum(part[0].astype(F32) for part in parts)
    width = qkv[0].shape[2]
    gradient = jnp.stack([total[:, c * width : (c + 1) * width] for c in range(3)], 0)
    update_into(outs[0:4], gradient, qkv, rate)


def qkv_update(parts, state, rate):
    return local_call(
        functools.partial(qkv_update_kernel, got=len(parts), rate=rate),
        "qkv_update",
        four((state,)),
        [VMEM] * (len(parts) + 3),
        2,
    )(*parts, *state)


def swap(values, axis, bit):
    count = lax.axis_size(axis)
    return lax.ppermute(values, axis, [(i, i ^ bit) for i in range(count)])


def bits_of(axis):
    count = lax.axis_size(axis)
    return [1 << b for b in range(count.bit_length() - 1)]


def gather_pieces(own, axis, *earlier):
    pieces = {0: own}
    for bit in reversed(bits_of(axis)):
        for m in list(pieces):
            known = [*earlier] if m else []
            if bit == 1 and m:
                known.append(pieces[1])
            sent = after(pieces[m], *known) if known else pieces[m]
            pieces[m | bit] = swap(sent, axis, bit)
    return [pieces[m] for m in range(lax.axis_size(axis))]


def first_step(blocks, axis, *earlier):
    held = {m: [block] for m, block in enumerate(blocks)}
    for m in sorted((m for m in held if m & 1 and m > 1), reverse=True):
        got = swap(after(held.pop(m)[0], *earlier), axis, 1)
        held[m ^ 1] = [(held[m ^ 1][0].astype(F32) + got.astype(F32)).astype(BF16)]
    return held


def last_steps(held, axis, *earlier):
    held = {m: [after(parts[0], *earlier)] if m else list(parts) for m, parts in held.items()}
    if len(held) > 2:
        held[1] = [after(held[1][0], held[2][0])]
    for bit in bits_of(axis):
        for m in sorted((m for m in held if m & bit), reverse=True):
            parts = held.pop(m)
            sent = parts[0]
            if len(parts) > 1:
                sent = sum(part.astype(F32) for part in parts).astype(BF16)
            held[m ^ bit].append(swap(sent, axis, bit))
    return held[0]


def after(values, *earlier):
    return lax.optimization_barrier((values, earlier))[0]


def reduce_halves(even, odd, axis, bit):
    while True:
        got = swap(odd, axis, bit)
        if even.shape[0] == 1:
            return [even, got]
        held = (even.astype(F32) + got.astype(F32)).astype(BF16)
        even, odd, bit = held[0::2], held[1::2], bit * 2


def exchange_pieces(pieces, axis):
    return [pieces[0]] + [swap(pieces[m], axis, m) for m in range(1, len(pieces))]


def apply_update(gradient, master, moment, average, step_rate):
    new_moment = momentum_decay * moment + gradient
    new_master = master - step_rate * (gradient + momentum_decay * new_moment)
    new_average = average_decay * average + (1.0 - average_decay) * new_master
    return (gradient, new_master, new_moment, new_average)


def token_slots(route_ids, length, expert_count, capacity):
    rows = route_ids.shape[0]
    at = jnp.arange(rows, dtype=jnp.int32)
    live = at < length
    hot = (route_ids[:, None] == jnp.arange(expert_count, dtype=jnp.int32)[None, :]) & live[:, None]
    hot_f = hot.astype(F32)
    before = (at[None, :] < at[:, None]).astype(BF16)
    earlier = dot_nn(before, hot.astype(BF16))
    pos = jnp.sum(earlier * hot_f, -1)
    totals = jnp.sum(hot_f, 0)
    kept = live & (pos < capacity)
    counts = jnp.minimum(totals, capacity)
    spare = capacity - counts
    order = jnp.arange(expert_count)
    spare_before = jnp.sum(jnp.where(order[None, :] < order[:, None], spare[None, :], 0.0), 1)
    rank = at.astype(F32) - jnp.sum(jnp.minimum(earlier, capacity), -1)
    inside = (rank[:, None] >= spare_before[None, :]) & (rank[:, None] < (spare_before + spare)[None, :])
    base = order.astype(F32) * capacity + counts - spare_before
    loose = jnp.sum(jnp.where(inside, base[None, :] + rank[:, None], 0.0), -1)
    slot = jnp.where(kept, route_ids * capacity + pos.astype(jnp.int32), loose.astype(jnp.int32))
    return (slot.astype(jnp.int32), totals.astype(jnp.int32))


def on_device(
    tokens,
    cotangent,
    lengths,
    routes,
    norm_params,
    qkv_weight,
    out_weight,
    up_weight,
    down_weight,
    router_weight,
    mix_weight,
    norm_master,
    norm_moment,
    norm_average,
    qkv_master,
    qkv_moment,
    qkv_average,
    out_master,
    out_moment,
    out_average,
    up_master,
    up_moment,
    up_average,
    down_master,
    down_moment,
    down_average,
    router_master,
    router_moment,
    router_average,
    mix_master,
    mix_moment,
    mix_average,
    expert_up_master,
    expert_up_moment,
    expert_up_average,
    expert_down_master,
    expert_down_moment,
    expert_down_average,
):
    narrow_count = lax.axis_size("narrow")
    wide_count = lax.axis_size("wide")
    narrow_index = lax.axis_index("narrow")
    wide_index = lax.axis_index("wide")
    local_rows, width = tokens.shape
    group_rows = local_rows * narrow_count
    expert_count = router_weight.shape[1]
    capacity = group_rows // expert_count
    head_width = qkv_weight.shape[2]
    norms = norm_params.astype(F32)
    place = (narrow_index ^ jnp.arange(narrow_count, dtype=jnp.int32)).astype(jnp.int32)

    units = expert_up_master.shape[2]
    out_rows = out_weight.shape[0] // wide_count
    out_slice = lax.dynamic_slice_in_dim(out_weight, wide_index * out_rows, out_rows, 0)
    out_slices = exchange_pieces([out_slice] * narrow_count, "narrow")
    packed = pack_expert(expert_up_master[0], expert_down_master[0], out_slices)
    pack = lax.all_gather(packed, "wide", axis=0, tiled=False)
    out_all = pack[:, 2 * units :].reshape(wide_count, narrow_count, out_rows, width)
    out_all = out_all.transpose(1, 0, 2, 3).reshape(narrow_count, head_width, width)

    slot, totals = token_slots(routes[:, 0], lengths[0], expert_count, capacity)
    tok_pieces = gather_pieces(after(tokens, out_slices[1]), "narrow", packed)
    slot_row = jnp.concatenate(
        [
            lax.dynamic_slice_in_dim(slot, place[m] * local_rows, local_rows, 0)
            for m in range(narrow_count)
        ],
        0,
    )[None, :]
    side = jnp.concatenate(
        [
            router_weight,
            mix_weight,
            jnp.zeros((width, lane_pad - expert_count - 2), BF16),
        ],
        1,
    )

    projected = [project(piece, norms, qkv_weight) for piece in tok_pieces]
    act_pieces = [pair[0] for pair in projected]
    qkv_pieces = [pair[1] for pair in projected]
    heads, log_sums, qkv = attend_forward(after(place, slot_row), lengths, qkv_pieces)
    cot_pieces = gather_pieces(after(cotangent, tok_pieces[-1]), "narrow", heads)
    cot_sorted, dense_back = sorted_cot(slot_row, cot_pieces, down_weight)
    head_pieces = gather_pieces(after(heads, cot_pieces), "narrow", cot_sorted)

    def to_owners(rows):
        got = []
        for m in range(0, wide_count, 2):
            at = ((wide_index ^ m) // 2) * capacity
            block = lax.dynamic_slice_in_dim(rows, at, capacity, 0)
            got.append(block if m == 0 else swap(block, "wide", m))
        return got

    routed_back = expert_back(cot_sorted, pack, units)
    cot_blocks = to_owners(cot_sorted)
    act_two, resid = join(
        after(place, routed_back), head_pieces, tok_pieces, out_all, norms
    )
    act_sorted, table = route(
        jnp.minimum(totals, capacity), slot_row, act_two, side, expert_count
    )
    act_blocks = to_owners(act_sorted)
    made = mixture(
        slot_row,
        act_sorted,
        table,
        dense_back,
        routed_back,
        up_weight,
        pack,
        side,
        narrow_count,
    )
    dact_parts = made[:narrow_count]
    dense_dpre, dense_hid, expert_hid, dside = made[narrow_count:]
    dact_parts = [*dact_parts[:-1], after(dact_parts[-1], act_blocks[1:3])]
    mlp_parts = mixture_output(
        slot_row, dense_hid, expert_hid, down_weight, pack, narrow_count
    )
    dact_held = first_step(dact_parts, "narrow")
    dact_sum = last_steps(dact_held, "narrow", mlp_parts)
    out_at = 2 * up_weight.shape[1]
    small_at = out_at + narrow_count * head_width
    shared_part = dense_grad(
        after(act_sorted, mlp_parts), cot_sorted, dense_dpre, dense_hid, small_at + lane_pad
    )
    second = second_norm_reverse(
        [after(dact_sum[0], act_blocks[3:], cot_blocks[1:3], shared_part)] + dact_sum[1:], resid, cotangent, norms, out_all
    )
    dresid, resid_low, sums_two = second[:3]
    dheads = exchange_pieces(second[3:], "narrow")
    side_columns = expert_count + 2
    shared_part = out_grad(place, head_pieces, resid_low, shared_part, out_at)
    shared_part = side_grad(
        totals, act_sorted, sums_two, dside, shared_part, small_at, side_columns
    )
    shared_rows = lax.psum_scatter(
        after(shared_part, dheads), "wide", scatter_dimension=0, tiled=True)
    back = attend_backward(
        after(place, shared_part), lengths, qkv, dheads, log_sums, qkv_weight
    )
    dqkv, done_parts = back[0], back[1:]
    mlp_held = first_step(mlp_parts, "narrow", dheads)
    done_held = first_step(done_parts, "narrow", mlp_held[narrow_count // 2])

    owner = (wide_index ^ jnp.arange(wide_count, dtype=jnp.int32)).astype(jnp.int32)
    even, odd = qkv_grad(owner, act_pieces, done_parts, tok_pieces, dqkv)
    halves = jnp.stack([wide_index ^ 1, wide_index]).astype(jnp.int32)
    owned = owner_grad(after(halves, even), act_blocks, cot_blocks, pack, units)
    owned_got = [swap(part, "wide", 1) for part in owned[:2]]
    step_rate = rate_base / math.sqrt(group_rows * wide_count)
    expert_rate = step_rate * (expert_count / 4.0) ** 1.5
    done_sum = last_steps(done_held, "narrow", even)
    qkv_got = swap(after(odd, done_sum, owned), "wide", 1)
    qkv_held = (even.astype(F32) + qkv_got.astype(F32)).astype(BF16)
    hidden_new = hidden_update(
        shared_rows,
        ((up_master, up_moment, up_average), (down_master, down_moment, down_average)),
        step_rate,
    )
    qkv_sum = reduce_halves(qkv_held[0::2], qkv_held[1::2], "wide", 2)
    expert_new = []
    for gradient, got, state, rate in (
        (owned[2], owned_got[0], (expert_up_master, expert_up_moment, expert_up_average), expert_rate),
        (
            owned[3],
            owned_got[1],
            (expert_down_master, expert_down_moment, expert_down_average),
            expert_down_boost * expert_rate,
        ),
    ):
        gradient = after(gradient, qkv_held) + got.astype(F32)
        expert_new.extend(apply_update(gradient[None], *state, rate))
    mlp_sum = last_steps(mlp_held, "narrow", done_sum)


    shared_out = after(shared_rows, mlp_sum, expert_new, hidden_new)
    qkv_columns = 3 * head_width
    small_one = sum(part[0, :, qkv_columns:].astype(F32) for part in qkv_sum)
    small = (shared_out[:, small_at:].astype(F32) + small_one).astype(BF16)
    out_parts = exchange_pieces(
        [
            jnp.concatenate(
                [
                    shared_out[:, out_at + m * head_width : out_at + (m + 1) * head_width],
                    small,
                ],
                1,
            )
            for m in range(narrow_count)
        ],
        "narrow",
    )
    out_new = out_update(
        out_parts,
        (
            (out_master, out_moment, out_average),
            (router_master, router_moment, router_average),
            (mix_master, mix_moment, mix_average),
            (norm_master, norm_moment, norm_average),
        ),
        side_columns,
        step_rate,
    )

    qkv_new = qkv_update(qkv_sum, (qkv_master, qkv_moment, qkv_average), step_rate)
    input_grad = first_norm_reverse(
        done_sum,
        dresid,
        tokens,
        norms,
    )
    digits = out_new[16][side_columns + 2 : side_columns + 2 + 4 * expert_count, 0]
    digits = jnp.sum(digits.reshape(expert_count, 4) * jnp.asarray([1.0, 8.0, 64.0, 512.0]), 1)
    expert_counts = (digits / narrow_count + 0.5).astype(jnp.int32)
    block_out = (resid + sum(part.astype(F32) for part in mlp_sum)).astype(BF16)
    results = [block_out, input_grad, expert_counts]
    for group in (out_new[12:16], qkv_new, out_new[0:4], hidden_new, out_new[4:12]):
        results.extend(group)
    results.extend(expert_new)
    return tuple(results)


def solution(mesh):
    in_specs = (
        P(("wide", "narrow"), None),
        P(("wide", "narrow"), None),
        P("wide"),
        P("wide", None),
        P(),
        P(None, None, "narrow"),
        P("narrow", None),
        P(None, "narrow"),
        P("narrow", None),
        P(),
        P(),
        P(None, "wide"),
        P(None, "wide"),
        P(None, "wide"),
        P(None, "wide", "narrow"),
        P(None, "wide", "narrow"),
        P(None, "wide", "narrow"),
        P("narrow", "wide"),
        P("narrow", "wide"),
        P("narrow", "wide"),
        P("wide", "narrow"),
        P("wide", "narrow"),
        P("wide", "narrow"),
        P("narrow", "wide"),
        P("narrow", "wide"),
        P("narrow", "wide"),
        P("wide", None),
        P("wide", None),
        P("wide", None),
        P("wide", None),
        P("wide", None),
        P("wide", None),
        P("wide", None, "narrow"),
        P("wide", None, "narrow"),
        P("wide", None, "narrow"),
        P("wide", "narrow", None),
        P("wide", "narrow", None),
        P("wide", "narrow", None),
    )
    out_specs = (
        P(("wide", "narrow"), None),
        P(("wide", "narrow"), None),
        P(),
        P(None, "wide"),
        P(None, "wide"),
        P(None, "wide"),
        P(None, "wide"),
        P(None, "wide", "narrow"),
        P(None, "wide", "narrow"),
        P(None, "wide", "narrow"),
        P(None, "wide", "narrow"),
        P("narrow", "wide"),
        P("narrow", "wide"),
        P("narrow", "wide"),
        P("narrow", "wide"),
        P("wide", "narrow"),
        P("wide", "narrow"),
        P("wide", "narrow"),
        P("wide", "narrow"),
        P("narrow", "wide"),
        P("narrow", "wide"),
        P("narrow", "wide"),
        P("narrow", "wide"),
        P("wide", None),
        P("wide", None),
        P("wide", None),
        P("wide", None),
        P("wide", None),
        P("wide", None),
        P("wide", None),
        P("wide", None),
        P("wide", None, "narrow"),
        P("wide", None, "narrow"),
        P("wide", None, "narrow"),
        P("wide", None, "narrow"),
        P("wide", "narrow", None),
        P("wide", "narrow", None),
        P("wide", "narrow", None),
        P("wide", "narrow", None),
    )
    return jax.shard_map(
        on_device, mesh=mesh, in_specs=in_specs, out_specs=out_specs, check_vma=False
    )
```
